32 devices in a mesh: ang: 16 (over z, y, core), ax: 2 (over x).
Axes of the slice: x: 2, y: 2, z: 4, core: 2. Of those that a mesh axis runs over, the one named last changes fastest.
Arguments:
- concentration: float32 [3, 512, 32, 512], P(None, 'ang', 'ax'), may hold values from 0.1 to 2
- courant: float32 [512], replicated, may hold values from 0.1 to 0.35
- axial_diffusion: float32 [3], replicated, may hold values from 0.05 to 0.12
- angular_rate: float32 [3, 512], replicated, may hold values from 0.05 to 0.18
- rate_constants: float32 [4], replicated, may hold values from 0.05 to 0.2
- species_map: int32 [4, 3], replicated, may hold values from 0 to 2, each once within a row
- wall_flags: int32 [3, 512], P(None, 'ang'), may hold values 0 or 1
- radial_inverse: bfloat16 [3, 1024, 1024], replicated, may hold values from -1 to 1, as said below
Outputs:
- final_field: float32 [3, 512, 32, 512], P(None, 'ang', 'ax')
The draws below stay inside these ranges and needn't reach their ends.
Inputs may be any that keep to these rules, and one draw needn't show every extreme that they name: Every matrix is centrosymmetric: radial_inverse[s, i, j] equals radial_inverse[s, 1023 - i, 1023 - j].
All inputs are finite; a program needn't handle non-finite values. No bound on the sum of `wall_flags` on one device may be relied on, other than what follows from the above.
Results may differ from the reference program's by a relative error of at most 0.0029.
Values may be sent and summed in bfloat16 or wider, within the bound.
No kernel may reach another device: no remote copies, remote signals or barrier semaphores. Data moves between devices by JAX's collectives and lax.ppermute only.
A program may use at most 64 MiB of HBM per device.

```python
import math
import jax
import jax.numpy as jnp
from jax import lax

NSPEC = 3
NREACT = 4
NRAD = 1024
HALF = 512
STEPS = 2
ANG = 512
PLANES = 32


def draw_radial_inverse(key, part):
    spread = 0.6 / math.sqrt(NRAD)
    base = jax.random.normal(key, (NSPEC, NRAD, NRAD), jnp.float32)
    coupling = jnp.clip(base * spread, -0.1, 0.1)
    coupling = 0.5 * (coupling + coupling[:, ::-1, ::-1])
    matrix = coupling + 0.8 * jnp.eye(NRAD, dtype=jnp.float32)[None]
    return matrix.astype(jnp.bfloat16)


def plant(array, stream_key, low, high):
    spot = [jax.random.randint(jax.random.fold_in(stream_key, axis), (), 0, length) for axis, length in enumerate(array.shape)]
    widest = array.shape.index(max(array.shape))
    neighbour = spot[:widest] + [(spot[widest] + 1) % array.shape[widest]] + spot[widest + 1:]
    return array.at[tuple(spot)].set(low).at[tuple(neighbour)].set(high)


def steps_of(stream_key, shape, split, least, largest):
    gain = 1.0
    for position, blocks in split:
        draws = jax.random.uniform(jax.random.fold_in(jax.random.fold_in(stream_key, 6), position), (blocks,), jnp.float32, least / len(split), largest / len(split))
        gain = gain * jnp.repeat(jnp.exp(draws), shape[position] // blocks).reshape((-1,) + (1,) * (len(shape) - 1 - position))
    return gain


def setup_inputs(seed: int = 0) -> dict:
    key_of = jax.random.split(jax.random.key(seed), 9)
    concentration = jnp.clip(0.1 + 1.9 * jax.random.uniform(key_of[0], (NSPEC, ANG, PLANES, HALF), jnp.float32) ** steps_of(key_of[0], (NSPEC, ANG, PLANES, HALF), ((1, 16), (2, 2)), -0.2, 0.2), 0.1, 2.0)
    courant = jnp.clip(jax.random.uniform(key_of[1], (HALF,), jnp.float32, 0.1, 0.35), 0.1, 0.35)
    axial_diffusion = jnp.clip(jax.random.uniform(key_of[2], (NSPEC,), jnp.float32, 0.05, 0.12), 0.05, 0.12)
    angular_rate = jnp.clip(jnp.exp(jax.random.uniform(key_of[3], (NSPEC, HALF), jnp.float32, math.log(0.05), math.log(0.18))), 0.05, 0.18)
    rate_constants = jnp.clip(jnp.exp(jax.random.uniform(key_of[4], (NREACT,), jnp.float32, math.log(0.05), math.log(0.2))), 0.05, 0.2)
    species_map = jax.vmap(lambda own: jax.random.permutation(own, NSPEC))(jax.random.split(key_of[5], NREACT)).reshape((NREACT, NSPEC)).astype(jnp.int32)
    wall_flags = plant((jax.random.randint(key_of[6], (NSPEC, ANG), 0, 2) < 1).astype(jnp.int32), jax.random.fold_in(key_of[6], 1), 0, 1)
    radial_inverse = draw_radial_inverse(jax.random.fold_in(key_of[8], 71), 0)
    return {"concentration": concentration, "courant": courant, "axial_diffusion": axial_diffusion, "angular_rate": angular_rate, "rate_constants": rate_constants, "species_map": species_map, "wall_flags": wall_flags, "radial_inverse": radial_inverse}


def species_step(field, species, courant, axial_diffusion, angular_rate, rate_constants, species_map, wall_flags, radial_inverse):
    own_part = field[species]
    angle_before = jnp.roll(own_part, 1, 0)
    angle_after = jnp.roll(own_part, -1, 0)
    zero_plane = jnp.zeros_like(own_part[:, :1])
    axial_before = jnp.concatenate([zero_plane, own_part[:, :-1]], 1)
    axial_after = jnp.concatenate([own_part[:, 1:], zero_plane], 1)
    reaction = jnp.zeros_like(own_part)
    for which_reaction in range(NREACT):
        first_index = species_map[which_reaction, 0]
        second_index = species_map[which_reaction, 1]
        product_index = species_map[which_reaction, 2]
        rate_term = rate_constants[which_reaction] * field[first_index] * field[second_index]
        weight = (product_index == species).astype(own_part.dtype) - (first_index == species).astype(own_part.dtype) - (second_index == species).astype(own_part.dtype)
        reaction = reaction + weight * rate_term
    explicit = (own_part - courant * (own_part - axial_before)
                + axial_diffusion[species] * (axial_after - 2.0 * own_part + axial_before)
                + angular_rate[species] * (angle_after - 2.0 * own_part + angle_before)
                + reaction)
    opposite = jnp.roll(explicit, -(ANG // 2), 0)[:, :, ::-1]
    diameter = jnp.concatenate([explicit, opposite], 2).astype(jnp.bfloat16)
    rows_block = radial_inverse[species, :HALF, :]
    implicit = jnp.dot(diameter.reshape(-1, NRAD), jnp.transpose(rows_block), preferred_element_type=jnp.float32).reshape(explicit.shape)
    wall_mask = lax.broadcasted_iota(jnp.int32, implicit.shape, 2) == 0
    wall_value = jnp.where(wall_flags[species][:, None, None] == 1, 0.0, implicit[:, :, 1:2])
    return jnp.where(wall_mask, wall_value, implicit)


def reference(concentration, courant, axial_diffusion, angular_rate, rate_constants, species_map, wall_flags, radial_inverse):
    field = concentration
    for step_index in range(STEPS):
        current = field
        field = lax.map(lambda species: species_step(current, species, courant, axial_diffusion, angular_rate, rate_constants, species_map, wall_flags, radial_inverse), jnp.arange(NSPEC, dtype=jnp.int32))
    return field
```

```python
import functools

import jax
import jax.numpy as jnp
from jax import lax
from jax.experimental import pallas as pl
from jax.experimental.pallas import tpu as pltpu
from jax.sharding import PartitionSpec as P

STEPS = 2
F32 = jnp.float32
BF16 = jnp.bfloat16
VMEM_LIMIT = 48 * 1024 * 1024

ANY = pl.BlockSpec(memory_space=pl.ANY)
VM = pl.BlockSpec(memory_space=pltpu.VMEM)
SM = pl.BlockSpec(memory_space=pltpu.SMEM)


def call(body, out_shape, in_specs, out_specs, scratch, args, cost, aliases=None):
    return pl.pallas_call(
        body,
        out_shape=out_shape,
        in_specs=in_specs,
        out_specs=out_specs,
        scratch_shapes=scratch,
        input_output_aliases=aliases or {},
        cost_estimate=pl.CostEstimate(flops=cost[0], bytes_accessed=cost[1], transcendentals=0),
        compiler_params=pltpu.CompilerParams(vmem_limit_bytes=VMEM_LIMIT),
    )(*args)


def product_rates(rate_ref, map_ref):
    rates = []
    for species in range(3):
        total = jnp.float32(0.0)
        for k in range(map_ref.shape[0]):
            total = total + jnp.where(map_ref[k, 2] == species, rate_ref[k], 0.0)
        rates.append(total)
    return rates


def transport(now, before, after, around, courant, axial, angular, rates):
    made = (
        rates[0] * (now[1] * now[2]),
        rates[1] * (now[0] * now[2]),
        rates[2] * (now[0] * now[1]),
    )
    spent = made[0] + made[1] + made[2]
    out = []
    for s in range(3):
        own = (1.0 - 2.0 * axial[s]) - courant - 2.0 * angular[s]
        value = now[s] * own + before[s] * (courant + axial[s]) + after[s] * axial[s]
        value = value + around[s] * angular[s]
        out.append(value + (2.0 * made[s] - spent))
    return out


def coefficients(cour_ref, diff_ref, ang_ref, rate_ref, map_ref):
    courant = cour_ref[...]
    axial = [diff_ref[s] for s in range(3)]
    angular = [ang_ref[s : s + 1, :] for s in range(3)]
    return courant, axial, angular, product_rates(rate_ref, map_ref)


def plane_edges(nz, nr, first, last):
    row = lax.broadcasted_iota(jnp.int32, (nz, nr), 0)
    return row == first, row == last


def first_step_angle(read, low, high, coef, nz):
    now = [read(s, 0) for s in range(3)]
    around = [read(s, -1) + read(s, 1) for s in range(3)]
    before = [pltpu.roll(v, 1, 0) for v in now]
    after = [pltpu.roll(v, nz - 1, 0) for v in now]
    if low is not None:
        is_first, is_last = plane_edges(nz, now[0].shape[1], 0, nz - 1)
        before = [jnp.where(is_first, low(s), before[s]) for s in range(3)]
        after = [jnp.where(is_last, high(s), after[s]) for s in range(3)]
    out = transport(now, before, after, around, *coef)
    return [pltpu.roll(v, nz - nz // 4, 0) for v in out]


def head_kernel(sizes, conc, cour, diff, ang, rate, smap, low, high, first, last, mid, field, sems):
    na, nz, lo, hi = sizes
    half = nz // 2
    inner = pl.ds((lo - 1) * nz, (hi - lo + 2) * nz)
    left = pl.ds(0, (lo - 1) * nz)
    right = pl.ds((hi + 1) * nz, (na - hi - 1) * nz)
    copies = [
        pltpu.make_async_copy(conc.at[:, rows], field.at[:, rows], sems.at[k])
        for k, rows in enumerate((inner, left, right))
    ]
    for copy in copies:
        copy.start()
    coef = coefficients(cour, diff, ang, rate, smap)
    copies[0].wait()

    def pair(step, carry):
        tiles = []
        for k in range(2):
            t = lo + step * 2 + k

            def read(s, shift):
                return field[s, pl.ds(pl.multiple_of((t + shift) * nz, nz), nz), :]

            tiles.append(first_step_angle(read, None, None, coef, nz))
        for s in range(3):
            both = jnp.concatenate([tiles[0][s][:half], tiles[1][s][:half]], 0)
            mid[s, pl.ds(pl.multiple_of(step * nz, nz), nz), :] = both.astype(BF16)
        return carry

    lax.fori_loop(0, (hi - lo) // 2, pair, 0)
    copies[1].wait()
    copies[2].wait()
    for s in range(3):
        for t in range(na):
            low[s, t : t + 1, :] = field[s, t * nz : t * nz + 1, :]
            high[s, t : t + 1, :] = field[s, (t + 1) * nz - 1 : (t + 1) * nz, :]
        first[s] = field[s, pl.ds(0, nz), :]
        last[s] = field[s, pl.ds((na - 1) * nz, nz), :]


def inner_kernel(sizes, runs, conc, cour, diff, ang, rate, smap, *rest):
    na, nz = sizes
    half = nz // 2
    outs, field, sem = rest[:-2], rest[-2], rest[-1]
    copy = pltpu.make_async_copy(conc, field, sem)
    copy.start()
    coef = coefficients(cour, diff, ang, rate, smap)
    copy.wait()
    for out, begin, count, at in runs:

        def pair(step, carry):
            tiles = []
            for k in range(2):
                t = begin + step * 2 + k

                def read(s, shift):
                    return field[s, pl.ds(pl.multiple_of((t + shift) * nz, nz), nz), :]

                tiles.append(first_step_angle(read, None, None, coef, nz))
            for s in range(3):
                both = jnp.concatenate([tiles[0][s][:half], tiles[1][s][:half]], 0)
                rows = pl.ds(pl.multiple_of(at * half + step * nz, nz), nz)
                outs[out][s, rows, :] = both.astype(BF16)
            return carry

        lax.fori_loop(0, count // 2, pair, 0)


def frame_kernel(sizes, conc, before, after, low, high, cour, diff, ang, rate, smap, out1, out2, field, sems):
    na, nz, ends = sizes
    half = nz // 2
    copies = [
        pltpu.make_async_copy(conc, field.at[:, pl.ds(nz, na * nz)], sems.at[0]),
        pltpu.make_async_copy(before, field.at[:, pl.ds(0, nz)], sems.at[1]),
        pltpu.make_async_copy(after, field.at[:, pl.ds((na + 1) * nz, nz)], sems.at[2]),
    ]
    for copy in copies:
        copy.start()
    coef = coefficients(cour, diff, ang, rate, smap)
    for copy in copies:
        copy.wait()

    def angle(t):
        def read(s, shift):
            return field[s, pl.ds(pl.multiple_of((t + 1 + shift) * nz, nz), nz), :]

        return first_step_angle(
            read, lambda s: low[s, pl.ds(t, 1), :], lambda s: high[s, pl.ds(t, 1), :], coef, nz
        )

    def pair(t, out, row, ends_row):
        tiles = [angle(t), angle(t + 1)]
        for s in range(3):
            both = jnp.concatenate([tiles[0][s][half:], tiles[1][s][half:]], 0)
            out[s, pl.ds(row, nz), :] = both.astype(BF16)
            if ends_row is not None:
                both = jnp.concatenate([tiles[0][s][:half], tiles[1][s][:half]], 0)
                out2[s, pl.ds(ends_row, nz), :] = both.astype(BF16)

    quarter = na // 4
    tail = na // 2 * half
    pair(0, out1, 0, tail)
    pair(na - 2, out2, (na // 2 - 2) * half, tail + nz)

    def first_part(step, carry):
        pair(step * 2, out1, pl.multiple_of(step * nz, nz), None)
        return carry

    def second_part(step, carry):
        pair(na // 2 + step * 2, out2, pl.multiple_of(step * nz, nz), None)
        return carry

    lax.fori_loop(1, quarter, first_part, 0)
    lax.fori_loop(0, quarter - 1, second_part, 0)


def weights_kernel(matrix, out, left, lower, sems):
    half = out.shape[1]
    copies = []
    for s in range(out.shape[0]):
        copies.append(
            pltpu.make_async_copy(
                matrix.at[s, pl.ds(0, half), pl.ds(0, half)], left.at[s], sems.at[0, s]
            )
        )
        copies.append(
            pltpu.make_async_copy(
                matrix.at[s, pl.ds(half, half), pl.ds(0, half)], lower.at[s], sems.at[1, s]
            )
        )
    for copy in copies:
        copy.start()
    row = lax.broadcasted_iota(jnp.int32, (half, half), 0)
    col = lax.broadcasted_iota(jnp.int32, (half, half), 1)
    row = jnp.maximum(row, 1)
    pick = jnp.where(col == row, 1.0, 0.0).astype(BF16)
    flip = jnp.where(col == half - 1 - row, 1.0, 0.0).astype(BF16)
    for copy in copies:
        copy.wait()
    for s in range(out.shape[0]):
        out[s, :, :half] = jnp.dot(pick, left[s], preferred_element_type=F32).astype(BF16)
        out[s, :, half:] = jnp.dot(flip, lower[s], preferred_element_type=F32).astype(BF16)


def both_sides(mine, theirs, weights):
    rows = jnp.concatenate(
        [jnp.concatenate([mine, theirs], 1), jnp.concatenate([theirs, mine], 1)], 0
    )
    return lax.dot_general(rows, weights, (((1,), (1,)), ((), ())), preferred_element_type=F32)


def absorb(value, flag):
    lane = lax.broadcasted_iota(jnp.int32, value.shape, 1)
    return jnp.where((lane == 0) & (flag == 1), 0.0, value)


def store_absorbed(out, ab, s, at, value, flags, angles, half):
    lanes = 128
    out[ab, s, pl.ds(at, value.shape[0]), :] = value
    for k, t in enumerate(angles):
        part = value[k * half : (k + 1) * half, :lanes]
        out[ab, s, pl.ds(at + k * half, half), :lanes] = absorb(part, flags[s, t])


def radial_kernel(groups, half, weights, flags_own, flags_opp, *refs):
    n = len(groups)
    mines, theirs, outs = refs[:n], refs[n : 2 * n], refs[2 * n :]
    for s in range(3):
        for k, angles in enumerate(groups):
            rows = len(angles) * half
            value = both_sides(mines[k][s], theirs[k][s], weights[s])
            store_absorbed(outs[k], 0, s, 0, value[:rows], flags_own, angles, half)
            store_absorbed(outs[k], 1, s, 0, value[rows:], flags_opp, angles, half)


def edges_kernel(na, nz, outer1, outer2, low, high, first, last):
    half = nz // 2
    part = na // 2
    tail = part * half
    for ab in range(2):
        for s in range(3):
            for k, outer in enumerate((outer1, outer2)):
                for t in range(part):
                    to = pl.ds(k * part + t, 1)
                    at = t * half + half // 2
                    high[ab, s, to, :] = outer[ab, s, at - 1 : at, :]
                    low[ab, s, to, :] = outer[ab, s, at : at + 1, :]
            first[ab, s, pl.ds(0, half), :] = outer2[ab, s, pl.ds(tail, half), :]
            first[ab, s, pl.ds(half, half), :] = outer1[ab, s, pl.ds(0, half), :]
            last[ab, s, pl.ds(0, half), :] = outer2[ab, s, pl.ds(tail + 3 * half, half), :]
            last[ab, s, pl.ds(half, half), :] = outer2[ab, s, pl.ds(tail - half, half), :]


def second_step(read_mid, read_outer, low, high, coef, nz):
    now = [jnp.concatenate([read_mid(s, 0), read_outer(s, 0)], 0) for s in range(3)]
    around = [
        jnp.concatenate(
            [read_mid(s, -1) + read_mid(s, 1), read_outer(s, -1) + read_outer(s, 1)], 0
        )
        for s in range(3)
    ]
    quarter = nz // 4
    is_first, is_last = plane_edges(nz, now[0].shape[1], nz - quarter, nz - quarter - 1)
    before = [jnp.where(is_first, low(s), pltpu.roll(now[s], 1, 0)) for s in range(3)]
    after = [jnp.where(is_last, high(s), pltpu.roll(now[s], nz - 1, 0)) for s in range(3)]
    return transport(now, before, after, around, *coef)


def step_angles(begin, count, mid, outer, low, high, coef, rows, nz):
    half = nz // 2

    def one(step, carry):
        t = begin + step
        for ab in range(2):

            def read(ref, s, shift):
                return ref[ab, s, pl.ds(pl.multiple_of((t + 1 + shift) * half, half), half), :]

            out = second_step(
                lambda s, shift: read(mid, s, shift),
                lambda s, shift: read(outer, s, shift),
                lambda s: low[ab, s, pl.ds(t, 1), :],
                lambda s: high[ab, s, pl.ds(t, 1), :],
                coef,
                nz,
            )
            width = out[0].shape[1]
            for s in range(3):
                at = pl.ds(pl.multiple_of(t * nz, nz), nz)
                rows[s, at, ab * width : (ab + 1) * width] = out[s].astype(BF16)
        return carry

    lax.fori_loop(0, count, one, 0)


def finish_angles(begin, count, s, rows, weights, flags, result, nz):
    lanes = 128
    value = lax.dot_general(
        rows[s, pl.ds(begin * nz, count * nz), :],
        weights[s],
        (((1,), (1,)), ((), ())),
        preferred_element_type=F32,
    )
    for k in range(count):
        part = pltpu.roll(value[k * nz : (k + 1) * nz], nz // 4, 0)
        result[s, begin + k] = part
        result[s, begin + k, :, :lanes] = absorb(part[:, :lanes], flags[s, begin + k])


def early_kernel(
    sizes, weights, flags, swap, outer1, outer2, mid_a, mid_c, before, after, low, high,
    cour, diff, ang, rate, smap, out, mid, outer, rows, result, sems, out_sems,
):
    na, nz, lo, hi, ends = sizes
    half = nz // 2
    part = na // 2
    tail = part * half
    copies = []

    def bring(src, dst):
        copies.append(pltpu.make_async_copy(src, dst, sems.at[len(copies)]))

    def slots(ref, t, count):
        return ref.at[:, :, pl.ds((t + 1) * half, count * half)]

    def cut(ref, at, count):
        return ref.at[:, :, pl.ds(at, count * half)]

    bring(cut(outer1, 0, part), slots(outer, 0, part))
    bring(cut(outer2, 0, part), slots(outer, part, part))
    bring(cut(outer2, tail, 2), slots(mid, 0, 2))
    bring(cut(outer2, tail + 2 * half, 2), slots(mid, na - 2, 2))
    bring(mid_a, slots(mid, lo, hi - lo))
    bring(cut(mid_c, 0, lo - 2), slots(mid, 2, lo - 2))
    bring(cut(mid_c, (lo - 2) * half, lo - 2), slots(mid, na - lo, lo - 2))
    for ab in range(2):
        src = jnp.where(swap[0] == 1, 1 - ab, ab)
        bring(before.at[src, :, pl.ds(0, half)], mid.at[ab, :, pl.ds(0, half)])
        bring(before.at[src, :, pl.ds(half, half)], outer.at[ab, :, pl.ds(0, half)])
        src = jnp.where(swap[1] == 1, 1 - ab, ab)
        end = pl.ds((na + 1) * half, half)
        bring(after.at[src, :, pl.ds(0, half)], mid.at[ab, :, end])
        bring(after.at[src, :, pl.ds(half, half)], outer.at[ab, :, end])
    for copy in copies:
        copy.start()
    coef = coefficients(cour, diff, ang, rate, smap)
    for copy in copies:
        copy.wait()
    runs = ((0, hi - 1), (na - lo + 1, lo - 1))
    for begin, count in runs:
        step_angles(begin, count, mid, outer, low, high, coef, rows, nz)
    leaves = []
    for s in range(3):
        for k, (begin, count) in enumerate(runs):
            finish_angles(begin, count, s, rows, weights, flags, result, nz)
            span = pl.ds(begin, count)
            leave = pltpu.make_async_copy(
                result.at[s, span], out.at[s, span], out_sems.at[k, s]
            )
            leave.start()
            leaves.append(leave)
    for leave in leaves:
        leave.wait()


def late_kernel(
    sizes, given, weights, flags_own, flags_opp, mine, theirs, outer1, outer2, mid_a, mid_c,
    low, high, cour, diff, ang, rate, smap, out, mid, outer, rows, result, sems, out_sems,
):
    na, nz, lo, hi = sizes
    half = nz // 2
    part = na // 2
    copies = []

    def bring(src, dst):
        copies.append(pltpu.make_async_copy(src, dst, sems.at[len(copies)]))

    def slots(ref, t, count):
        return ref.at[:, :, pl.ds((t + 1) * half, count * half)]

    def cut(ref, at, count):
        return ref.at[:, :, pl.ds(at, count * half)]

    bring(cut(outer1, (lo - 2) * half, 2), slots(outer, lo - 2, 2))
    bring(cut(outer2, 0, hi + 2 - part), slots(outer, part, hi + 2 - part))
    bring(cut(mid_a, mid_a.shape[2] - 2 * half, 2), slots(mid, lo - 2, 2))
    bring(cut(mid_c, mid_c.shape[2] // 2, 2), slots(mid, hi, 2))
    for copy in copies:
        copy.start()
    coef = coefficients(cour, diff, ang, rate, smap)
    count = hi - lo
    size = count * half
    for s in range(3):
        value = both_sides(mine[s], theirs[s], weights[s])
        for ab, flags in ((0, flags_own), (1, flags_opp)):
            store_absorbed(
                mid, ab, s, (lo + 1) * half, value[ab * size : (ab + 1) * size],
                flags, range(lo, hi), half,
            )
    for copy in copies:
        copy.wait()
    step_angles(lo - 1, count + 2, mid, outer, low, high, coef, rows, nz)
    leaves = []
    for s in range(3):
        finish_angles(lo - 1, count + 2, s, rows, weights, flags_own, result, nz)
        span = pl.ds(lo - 1, count + 2)
        leave = pltpu.make_async_copy(result.at[s, span], out.at[s, span], out_sems.at[s])
        leave.start()
        leaves.append(leave)
    for leave in leaves:
        leave.wait()


def ring(count, step):
    half = count // 2
    return [(i, i // half * half + (i % half + step) % half) for i in range(count)]


def per_device(
    concentration, courant, axial_diffusion, angular_rate, rate_constants, species_map,
    wall_flags, radial_inverse,
):
    ns, na, nz, nr = concentration.shape
    half = nz // 2
    count = lax.axis_size("ang")
    planes = lax.axis_size("ax")
    quarter = na // 4
    lo, hi = quarter, 2 * quarter
    ends = 2
    opposite = [(i, (i + count // 2) % count) for i in range(count)]
    up = [(i, i + 1) for i in range(planes - 1)]
    down = [(i + 1, i) for i in range(planes - 1)]
    after_ring = [(i, (i - 1) % count) for i in range(count)]
    before_ring = [(i, (i + 1) % count) for i in range(count)]

    def shape(*dims, dtype=F32):
        return jax.ShapeDtypeStruct(dims, dtype)

    conc = concentration.reshape(ns, na * nz, nr)
    cour = courant[None]
    params = (cour, axial_diffusion, angular_rate, rate_constants, species_map)
    param_specs = [VM, SM, VM, SM, SM]
    field = ns * na * nz * nr

    low, high, first, last, mid_a = call(
        functools.partial(head_kernel, (na, nz, lo, hi)),
        [
            shape(ns, na, nr), shape(ns, na, nr), shape(ns, nz, nr), shape(ns, nz, nr),
            shape(ns, quarter * half, nr, dtype=BF16),
        ],
        [ANY] + param_specs,
        [VM] * 5,
        [pltpu.VMEM((ns, na * nz, nr), F32), pltpu.SemaphoreType.DMA((3,))],
        (conc,) + params,
        (field * 10, field * 4),
    )
    plane_before = lax.ppermute(high, "ax", up)
    plane_after = lax.ppermute(low, "ax", down)
    angle_before = lax.ppermute(last, "ang", before_ring)
    angle_after = lax.ppermute(first, "ang", after_ring)
    opp_a = lax.ppermute(mid_a, "ang", opposite)

    inner_count = quarter - ends
    mid_c, mid_d = call(
        functools.partial(
            inner_kernel,
            (na, nz),
            (
                (0, ends, inner_count, 0),
                (0, na - quarter, inner_count, inner_count),
                (1, hi, quarter, 0),
            ),
        ),
        [
            shape(ns, 2 * inner_count * half, nr, dtype=BF16),
            shape(ns, quarter * half, nr, dtype=BF16),
        ],
        [ANY] + param_specs,
        [VM] * 2,
        [pltpu.VMEM((ns, na * nz, nr), F32), pltpu.SemaphoreType.DMA],
        (conc,) + params,
        (field * 10, field * 4),
    )
    out1, out2 = call(
        functools.partial(frame_kernel, (na, nz, ends)),
        [
            shape(ns, na // 2 * half, nr, dtype=BF16),
            shape(ns, (na // 2 + 2 * ends) * half, nr, dtype=BF16),
        ],
        [ANY] * 3 + [VM] * 2 + param_specs,
        [VM] * 2,
        [pltpu.VMEM((ns, (na + 2) * nz, nr), F32), pltpu.SemaphoreType.DMA((3,))],
        (conc, angle_before, angle_after, plane_before, plane_after) + params,
        (field * 20, field * 4),
    )
    opp_1 = lax.ppermute(out1, "ang", opposite)
    opp_2 = lax.ppermute(out2, "ang", opposite)
    mid_c, opp_a = lax.optimization_barrier((mid_c, opp_a))
    opp_c = lax.ppermute(mid_c, "ang", opposite)
    mid_d, opp_1 = lax.optimization_barrier((mid_d, opp_1))
    opp_d = lax.ppermute(mid_d, "ang", opposite)

    weights = call(
        weights_kernel,
        shape(ns, nr, 2 * nr, dtype=BF16),
        [ANY],
        VM,
        [
            pltpu.VMEM((ns, nr, nr), BF16), pltpu.VMEM((ns, nr, nr), BF16),
            pltpu.SemaphoreType.DMA((2, ns)),
        ],
        (radial_inverse,),
        (ns * 4 * nr**3, ns * 8 * nr * nr),
    )
    flags_opp = lax.ppermute(wall_flags, "ang", opposite)

    middle = tuple(range(lo, hi))
    group_1 = tuple(range(na // 2))
    group_2 = tuple(range(na // 2, na)) + (0, 1, na - 2, na - 1)
    group_c = tuple(range(ends, quarter)) + tuple(range(na - quarter, na - ends))

    def radial(groups, mines, theirs):
        rows = sum(len(g) for g in groups) * half
        return call(
            functools.partial(radial_kernel, groups, half),
            [shape(2, ns, len(g) * half, nr) for g in groups],
            [VM, SM, SM] + [VM] * (2 * len(groups)),
            [VM] * len(groups),
            [],
            (weights, wall_flags, flags_opp) + tuple(mines) + tuple(theirs),
            (ns * 2 * rows * 4 * nr * nr, ns * rows * nr * 12),
        )

    new_a, new_1, new_2 = radial((middle, group_1, group_2), (mid_a, out1, out2), (opp_a, opp_1, opp_2))
    (new_c,) = radial((group_c,), (mid_c,), (opp_c,))
    low2, high2, first2, last2 = call(
        functools.partial(edges_kernel, na, nz),
        [shape(2, ns, na, nr), shape(2, ns, na, nr), shape(2, ns, nz, nr), shape(2, ns, nz, nr)],
        [VM] * 2,
        [VM] * 4,
        [],
        (new_1, new_2),
        (0, field * 8),
    )
    plane_before = lax.ppermute(high2, "ax", up)
    plane_after = lax.ppermute(low2, "ax", down)
    angle_before = lax.ppermute(last2, "ang", ring(count, 1))
    angle_after = lax.ppermute(first2, "ang", ring(count, -1))
    place = lax.axis_index("ang") % (count // 2)
    swap = jnp.stack([place == 0, place == count // 2 - 1]).astype(jnp.int32)

    stage = [
        pltpu.VMEM((2, ns, (na + 2) * half, nr), F32),
        pltpu.VMEM((2, ns, (na + 2) * half, nr), F32),
        pltpu.VMEM((ns, na * nz, 2 * nr), BF16),
        pltpu.VMEM((ns, na, nz, nr), F32),
    ]
    partial = call(
        functools.partial(early_kernel, (na, nz, lo, hi, ends)),
        shape(ns, na, nz, nr),
        [VM, SM, SM] + [ANY] * 6 + [VM] * 2 + param_specs,
        ANY,
        stage + [pltpu.SemaphoreType.DMA((15,)), pltpu.SemaphoreType.DMA((2, ns))],
        (weights, wall_flags, swap, new_1, new_2, new_a, new_c, angle_before, angle_after,
         plane_before, plane_after) + params,
        (field * 1024 * 2, field * 16),
    )
    return call(
        functools.partial(late_kernel, (na, nz, hi, hi + quarter)),
        shape(ns, na, nz, nr),
        [ANY, VM, SM, SM] + [VM] * 2 + [ANY] * 4 + [VM] * 2 + param_specs,
        ANY,
        stage + [pltpu.SemaphoreType.DMA((4,)), pltpu.SemaphoreType.DMA((ns,))],
        (partial, weights, wall_flags, flags_opp, mid_d, opp_d, new_1, new_2, new_a, new_c,
         plane_before, plane_after) + params,
        (field * 512 * 2, field * 4),
        {0: 0},
    )


def solution(mesh):
    in_specs = (P(None, "ang", "ax", None), P(), P(), P(), P(), P(), P(None, "ang"), P())
    out_specs = P(None, "ang", "ax", None)
    return jax.shard_map(
        per_device, mesh=mesh, in_specs=in_specs, out_specs=out_specs, check_vma=False
    )
```

```python
import functools

import jax
import jax.numpy as jnp
from jax import lax
from jax.experimental import pallas as pl
from jax.experimental.pallas import tpu as pltpu
from jax.sharding import PartitionSpec as P

F32 = jnp.float32
BF16 = jnp.bfloat16
MIB = 1024 * 1024
LANES = 128

ANY = pl.BlockSpec(memory_space=pl.ANY)
HBM = pl.BlockSpec(memory_space=pltpu.HBM)
VM = pl.BlockSpec(memory_space=pltpu.VMEM)
SM = pl.BlockSpec(memory_space=pltpu.SMEM)

OWN, BEFORE, ANGULAR, AXIAL, RATE = 0, 3, 6, 9, 12


def call(body, out_shape, in_specs, out_specs, scratch, args, mib, aliases=None):
    return pl.pallas_call(
        body,
        out_shape=out_shape,
        in_specs=in_specs,
        out_specs=out_specs,
        scratch_shapes=scratch,
        input_output_aliases=aliases or {},
        cost_estimate=pl.CostEstimate(flops=1, bytes_accessed=1, transcendentals=0),
        compiler_params=pltpu.CompilerParams(vmem_limit_bytes=mib * MIB),
    )(*args)


def shape(*dims, dtype=F32):
    return jax.ShapeDtypeStruct(dims, dtype)


def transport(now, before, after, around, coef):
    made = (
        coef[RATE] * (now[1] * now[2]),
        coef[RATE + 1] * (now[0] * now[2]),
        coef[RATE + 2] * (now[0] * now[1]),
    )
    spent = made[0] + made[1] + made[2]
    out = []
    for s in range(3):
        value = now[s] * coef[OWN + s] + before[s] * coef[BEFORE + s]
        value = value + after[s] * coef[AXIAL + s] + around[s] * coef[ANGULAR + s]
        out.append(value + ((made[s] + made[s]) - spent))
    return out


def turned(first, second, rows):
    first, second = pltpu.roll(first, rows // 2, 0), pltpu.roll(second, rows // 2, 0)
    upper = lax.broadcasted_iota(jnp.int32, first.shape, 0) < rows // 2
    return jnp.where(upper, first, second), jnp.where(upper, second, first)


def first_step(read, low, high, coef, half):
    tiles = [[read(s, 0, k) for s in range(3)] for k in range(2)]
    around = [[read(s, -1, k) + read(s, 1, k) for s in range(3)] for k in range(2)]
    row = lax.broadcasted_iota(jnp.int32, tiles[0][0].shape, 0)
    top, bottom = row == 0, row == half - 1
    fall = [[pltpu.roll(v, 1, 0) for v in tile] for tile in tiles]
    rise = [[pltpu.roll(v, half - 1, 0) for v in tile] for tile in tiles]
    out = []
    for k in range(2):
        other = 1 - k
        before = [
            jnp.where(top, low(s) if low is not None and k == 0 else fall[other][s], fall[k][s])
            for s in range(3)
        ]
        after = [
            jnp.where(bottom, high(s) if high is not None and k == 1 else rise[other][s], rise[k][s])
            for s in range(3)
        ]
        out.append(transport(tiles[k], before, after, around[k], coef))
    pairs = [turned(out[0][s], out[1][s], half) for s in range(3)]
    return [p[0] for p in pairs], [p[1] for p in pairs]


def second_step(read, low, high, coef, half):
    tiles = [[read(k, s, 0) for s in range(3)] for k in range(2)]
    around = [[read(k, s, -1) + read(k, s, 1) for s in range(3)] for k in range(2)]
    row = lax.broadcasted_iota(jnp.int32, tiles[0][0].shape, 0)
    top, bottom = row == 0, row == half - 1
    first, last = row == half // 2, row == half // 2 - 1
    fall = [[pltpu.roll(v, 1, 0) for v in tile] for tile in tiles]
    rise = [[pltpu.roll(v, half - 1, 0) for v in tile] for tile in tiles]
    out = []
    for k in range(2):
        before = [jnp.where(top, fall[1 - k][s], fall[k][s]) for s in range(3)]
        after = [jnp.where(bottom, rise[1 - k][s], rise[k][s]) for s in range(3)]
        if k == 1:
            before = [jnp.where(first, low(s), before[s]) for s in range(3)]
            after = [jnp.where(last, high(s), after[s]) for s in range(3)]
        out.append(transport(tiles[k], before, after, around[k], coef))
    return out


def pack(tiles):
    return jnp.concatenate(tiles, 0).astype(BF16)


def at_rows(start, count, step):
    return pl.ds(pl.multiple_of(start, step), count)


def field_reader(field, t, nz):
    half = nz // 2
    return lambda s, shift, k: field[s, at_rows((t + shift) * nz + k * half, half, half), :]


def mid_run(field, out, begin, count, at, coef, nz):
    half = nz // 2

    def pair(step, carry):
        t = begin + step * 2
        tiles = [first_step(field_reader(field, t + k, nz), None, None, coef, half)[0] for k in range(2)]
        for s in range(3):
            out[s, at_rows(at * half + step * nz, nz, nz), :] = pack([tiles[0][s], tiles[1][s]])
        return carry

    lax.fori_loop(0, count // 2, pair, 0)


def head_kernel(sizes, conc, cour, diff, ang, rate, smap, *rest):
    na, nz, lo, hi, planes = sizes
    edges = rest[: 1 if planes == 2 else 2]
    first, last, mid, coef, field, cour_v, ang_v, diff_s, rate_s, map_s, sems = rest[len(edges) :]
    half = nz // 2
    inner = pl.ds((lo - 1) * nz, (hi - lo + 2) * nz)
    left = pl.ds(0, (lo - 1) * nz)
    right = pl.ds((hi + 1) * nz, (na - hi - 1) * nz)
    small = [
        pltpu.make_async_copy(src, dst, sems.at[k + 3])
        for k, (src, dst) in enumerate(
            ((cour, cour_v), (ang, ang_v), (diff, diff_s), (rate, rate_s), (smap, map_s))
        )
    ]
    copies = [
        pltpu.make_async_copy(conc.at[:, rows], field.at[:, rows], sems.at[k])
        for k, rows in enumerate((inner, left, right))
    ]
    for copy in small + copies:
        copy.start()
    for copy in small:
        copy.wait()
    tile = coef.shape[1:]
    for s in range(3):
        courant, angular = cour_v[...], ang_v[s : s + 1, :]
        axial = diff_s[s]
        total = jnp.float32(0.0)
        for k in range(map_s.shape[0]):
            total = total + jnp.where(map_s[k, 2] == s, rate_s[k], 0.0)
        coef[OWN + s] = jnp.broadcast_to((1.0 - 2.0 * axial) - courant - 2.0 * angular, tile)
        coef[BEFORE + s] = jnp.broadcast_to(courant + axial, tile)
        coef[ANGULAR + s] = jnp.broadcast_to(angular, tile)
        coef[AXIAL + s] = jnp.full(tile, axial, F32)
        coef[RATE + s] = jnp.full(tile, total, F32)
    copies[0].wait()
    mid_run(field, mid, lo, hi - lo, 0, coef, nz)
    copies[1].wait()
    copies[2].wait()
    for s in range(3):
        if planes == 2:
            row = jnp.where(lax.axis_index("ax") == 0, nz - 1, 0)
            for t in range(na):
                edges[0][s, t : t + 1, :] = field[s, pl.ds(t * nz + row, 1), :]
        else:
            for t in range(na):
                edges[0][s, t : t + 1, :] = field[s, t * nz : t * nz + 1, :]
                edges[1][s, t : t + 1, :] = field[s, (t + 1) * nz - 1 : (t + 1) * nz, :]
        first[s] = field[s, pl.ds(0, nz), :]
        last[s] = field[s, pl.ds((na - 1) * nz, nz), :]


def inner_kernel(sizes, runs, conc, coef, *rest):
    na, nz = sizes
    outs, field, sem = rest[:-2], rest[-2], rest[-1]
    copy = pltpu.make_async_copy(conc, field, sem)
    copy.start()
    copy.wait()
    for out, parts in runs:
        at = 0
        for begin, count in parts:
            mid_run(field, outs[out], begin, count, at, coef, nz)
            at += count


def edge_weights(planes):
    if planes != 2:
        return 1.0, 1.0
    place = lax.axis_index("ax")
    return jnp.where(place == 1, 1.0, 0.0), jnp.where(place == 0, 1.0, 0.0)


def frame_kernel(sizes, conc, before, after, low, high, coef, out1, out2, field, sems):
    na, nz, ends, planes = sizes
    half = nz // 2
    copies = [
        pltpu.make_async_copy(conc, field.at[:, pl.ds(nz, na * nz)], sems.at[0]),
        pltpu.make_async_copy(before, field.at[:, pl.ds(0, nz)], sems.at[1]),
        pltpu.make_async_copy(after, field.at[:, pl.ds((na + 1) * nz, nz)], sems.at[2]),
    ]
    for copy in copies:
        copy.start()
    low_weight, high_weight = edge_weights(planes)
    for copy in copies:
        copy.wait()

    def angle(t):
        return first_step(
            field_reader(field, t + 1, nz),
            lambda s: low[s, pl.ds(t, 1), :] * low_weight,
            lambda s: high[s, pl.ds(t, 1), :] * high_weight,
            coef,
            half,
        )

    def pair(t, out, row, ends_row):
        tiles = [angle(t), angle(t + 1)]
        for s in range(3):
            out[s, pl.ds(row, nz), :] = pack([tiles[0][1][s], tiles[1][1][s]])
            if ends_row is not None:
                out2[s, pl.ds(ends_row, nz), :] = pack([tiles[0][0][s], tiles[1][0][s]])

    quarter = na // 4
    tail = na // 2 * half
    pair(0, out1, 0, tail)
    pair(na - 2, out2, (na // 2 - 2) * half, tail + nz)

    def first_part(step, carry):
        pair(step * 2, out1, pl.multiple_of(step * nz, nz), None)
        return carry

    def second_part(step, carry):
        pair(na // 2 + step * 2, out2, pl.multiple_of(step * nz, nz), None)
        return carry

    lax.fori_loop(1, quarter, first_part, 0)
    lax.fori_loop(0, quarter - 1, second_part, 0)


def weights_kernel(matrix, flags_own, flags_opp, out, keep, left, lower, sems):
    half = out.shape[1]
    copies = []
    for s in range(out.shape[0]):
        for k, ref in enumerate((left, lower)):
            src = matrix.at[s, pl.ds(k * half, half), pl.ds(0, half)]
            copies.append(pltpu.make_async_copy(src, ref.at[s], sems.at[k, s]))
    for copy in copies:
        copy.start()
    lane = lax.broadcasted_iota(jnp.int32, (1, LANES), 1)
    for ab, flags in enumerate((flags_own, flags_opp)):
        for s in range(out.shape[0]):
            for t in range(keep.shape[2]):
                keep[ab, s, t : t + 1, :] = jnp.where((lane == 0) & (flags[s, t] == 1), 0.0, 1.0)
    row = lax.broadcasted_iota(jnp.int32, (half, half), 0)
    col = lax.broadcasted_iota(jnp.int32, (half, half), 1)
    row = jnp.maximum(row, 1)
    pick = jnp.where(col == row, 1.0, 0.0).astype(BF16)
    flip = jnp.where(col == half - 1 - row, 1.0, 0.0).astype(BF16)
    for copy in copies:
        copy.wait()
    for s in range(out.shape[0]):
        out[s, :, :half] = jnp.dot(pick, left[s], preferred_element_type=F32).astype(BF16)
        out[s, :, half:] = jnp.dot(flip, lower[s], preferred_element_type=F32).astype(BF16)


def rows_product(rows, weights):
    return lax.dot_general(rows, weights, (((1,), (1,)), ((), ())), preferred_element_type=F32)


def both_sides(mine, theirs, weights):
    rows = jnp.concatenate(
        [jnp.concatenate([mine, theirs], 1), jnp.concatenate([theirs, mine], 1)], 0
    )
    return rows_product(rows, weights)


def store_run(state, s, begin, place, count, at, value, keep, half):
    total = value.shape[0] // 2
    for ab in range(2):
        part = value[ab * total + at * half : ab * total + (at + count) * half]
        state[ab, s, pl.ds(place * half, count * half), LANES:] = part[:, LANES:]
        for k in range(count):
            state[ab, s, pl.ds((place + k) * half, half), :LANES] = (
                part[k * half : (k + 1) * half, :LANES] * keep[ab, s, begin + k : begin + k + 1, :]
            )


def radial_kernel(runs, copies, half, weights, keep, mine, theirs, *refs):
    n_in = 1 + max((part for part, *_ in copies), default=-1)
    parts, states = refs[:n_in], refs[n_in:]
    for s in range(3):
        value = both_sides(mine[s], theirs[s], weights[s])
        at = 0
        for which, begin, place, count in runs:
            store_run(states[which], s, begin, place, count, at, value, keep, half)
            at += count
    for part, source, which, place, count in copies:
        to, rows = pl.ds(place * half, count * half), pl.ds(source * half, count * half)
        for ab in range(2):
            for s in range(3):
                states[which][ab, s, to, :] = parts[part][ab, s, rows, :]


def edges_of_state(na, nz, planes, mid, outer, edges, first, last, stage):
    half = nz // 2
    if planes == 2:
        row = jnp.where(lax.axis_index("ax") == 0, half // 2 - 1, half // 2)
    end = pl.ds((na - 1) * half, half)
    ends_end = pl.ds(mid.shape[2] - half, half)
    for ab in range(2):
        for s in range(3):
            for t in range(na):
                to = pl.ds(t, 1)
                at = t * half + half // 2
                if planes == 2:
                    stage[0, to, :] = outer[ab, s, pl.ds(t * half + row, 1), :]
                else:
                    stage[0, to, :] = outer[ab, s, at : at + 1, :]
                    stage[1, to, :] = outer[ab, s, at - 1 : at, :]
            for k, edge in enumerate(edges):
                edge[ab, s] = stage[k].astype(BF16)
            begin = pl.ds(0, half)
            first[ab, s] = pack([mid[ab, s, begin, :], outer[ab, s, begin, :]])
            last[ab, s] = pack([mid[ab, s, ends_end, :], outer[ab, s, end, :]])


def radial_edges_kernel(sizes, runs, copies, half, weights, keep, mine, theirs, *refs):
    na, nz, planes = sizes
    n_edges = 1 if planes == 2 else 2
    *edges, first, last, stage = refs[-3 - n_edges :]
    refs = refs[: -3 - n_edges]
    radial_kernel(runs, copies, half, weights, keep, mine, theirs, *refs)
    edges_of_state(na, nz, planes, refs[-2], refs[-1], edges, first, last, stage)


def explicit_angle(t, reader, low, high, edge_factors, coef, rows, nz):
    half = nz // 2
    for ab in range(2):
        out = second_step(
            functools.partial(reader, ab),
            lambda s: low[ab, s, pl.ds(t, 1), :] * edge_factors[0],
            lambda s: high[ab, s, pl.ds(t, 1), :] * edge_factors[1],
            coef,
            half,
        )
        width = out[0][0].shape[1]
        for s in range(3):
            rows[s, at_rows(t * nz, nz, nz), ab * width : (ab + 1) * width] = pack(
                [out[0][s], out[1][s]]
            )


def explicit_run(begin, count, states, low, high, edge_factors, coef, rows, nz):
    half = nz // 2

    def one(step, carry):
        t = begin + step

        def reader(ab, k, s, shift):
            state, base = states[k]
            return state[ab, s, at_rows((t - base + shift) * half, half, half), :]

        explicit_angle(t, reader, low, high, edge_factors, coef, rows, nz)
        return carry

    lax.fori_loop(0, count, one, 0)


def finish_run(begin, count, s, rows, weights, keep, result, nz):
    half = nz // 2
    value = rows_product(rows[s, pl.ds(begin * nz, count * nz), :], weights[s])
    for k in range(count):
        t = begin + k
        parts = turned(value[k * nz + half : (k + 1) * nz], value[k * nz : k * nz + half], half)
        for p in range(2):
            span = pl.ds(p * half, half)
            result[s, t, span, LANES:] = parts[p][:, LANES:]
            result[s, t, span, :LANES] = parts[p][:, :LANES] * keep[0, s, t : t + 1, :]


def widen(pairs):
    for source, target in pairs:
        target[...] = source[...].astype(F32)


def early_kernel(
    sizes, weights, keep, mid, outer, before_low, after_low, low_low, high_low, coef,
    out, before, after, low, high, rows, result, out_sems
):
    na, nz, runs, half_ring, planes = sizes
    half = nz // 2
    place = lax.rem(lax.axis_index("ang"), half_ring)
    wrap_before = jnp.where(place == 0, 1, 0)
    wrap_after = jnp.where(place == half_ring - 1, 1, 0)
    factors = edge_weights(planes)
    states = (mid, outer)
    widen(((before_low, before), (after_low, after), (low_low, low), (high_low, high)))
    for begin, count in runs:
        end = begin + count
        if begin == 0:

            def reader(ab, k, s, shift):
                if shift == -1:
                    return before[jnp.where(wrap_before == 1, 1 - ab, ab), s, pl.ds(k * half, half), :]
                return states[k][ab, s, pl.ds(shift * half, half), :]

            explicit_angle(0, reader, low, high, factors, coef, rows, nz)
        if end == na:

            def reader(ab, k, s, shift):
                if shift == 1:
                    return after[jnp.where(wrap_after == 1, 1 - ab, ab), s, pl.ds(k * half, half), :]
                return states[k][ab, s, pl.ds((na - 1 + shift) * half, half), :]

            explicit_angle(na - 1, reader, low, high, factors, coef, rows, nz)
        start, stop = max(begin, 1), min(end, na - 1)
        explicit_run(start, stop - start, ((mid, 0), (outer, 0)), low, high, factors, coef, rows, nz)
    leaves = []
    for s in range(3):
        for k, (begin, count) in enumerate(runs):
            finish_run(begin, count, s, rows, weights, keep, result, nz)
            span = pl.ds(begin, count)
            leave = pltpu.make_async_copy(result.at[s, span], out.at[s, span], out_sems.at[k, s])
            leave.start()
            leaves.append(leave)
    for leave in leaves:
        leave.wait()


def late_kernel(
    sizes, given, state, weights, keep, mine, theirs, outer, low_low, high_low, coef,
    out, mid, low, high, rows, result, out_sems,
):
    na, nz, lo, hi, planes = sizes
    half = nz // 2
    factors = edge_weights(planes)
    count = hi - lo
    widen(((low_low, low), (high_low, high)))
    for s in range(3):
        value = both_sides(mine[s], theirs[s], weights[s])
        store_run(mid, s, lo, 2, count, 0, value, keep, half)
        for ab in range(2):
            for k in range(2):
                to = pl.ds((2 + count) * k * half, 2 * half)
                mid[ab, s, to, :] = state[ab, s, pl.ds((lo - 2 + (2 + count) * k) * half, 2 * half), :]
    explicit_run(lo - 1, count + 2, ((mid, lo - 2), (outer, 0)), low, high, factors, coef, rows, nz)
    leaves = []
    for s in range(3):
        finish_run(lo - 1, count + 2, s, rows, weights, keep, result, nz)
        span = pl.ds(lo - 1, count + 2)
        leave = pltpu.make_async_copy(result.at[s, span], out.at[s, span], out_sems.at[s])
        leave.start()
        leaves.append(leave)
    for leave in leaves:
        leave.wait()


def ring(count, step):
    half = count // 2
    return [(i, i // half * half + (i % half + step) % half) for i in range(count)]


def plane_halos(edges, planes):
    if planes == 2:
        got = lax.ppermute(edges[0], "ax", [(0, 1), (1, 0)])
        return got, got
    up = [(i, i + 1) for i in range(planes - 1)]
    down = [(i + 1, i) for i in range(planes - 1)]
    return lax.ppermute(edges[1], "ax", up), lax.ppermute(edges[0], "ax", down)


def after(value, done):
    return lax.optimization_barrier((value, done))


def per_device(
    concentration, courant, axial_diffusion, angular_rate, rate_constants, species_map,
    wall_flags, radial_inverse,
):
    ns, na, nz, nr = concentration.shape
    half = nz // 2
    count = lax.axis_size("ang")
    planes = lax.axis_size("ax")
    n_edges = 1 if planes == 2 else 2
    quarter = na // 4
    ends = 2
    first_lo, first_hi = quarter, 2 * quarter
    last_lo, last_hi = first_hi, 3 * quarter + ends
    inner = ((ends, first_lo - ends), (last_hi, na - ends - last_hi))
    inner_count = sum(n for _, n in inner)
    opposite = [(i, (i + count // 2) % count) for i in range(count)]

    def dma(*dims):
        return pltpu.SemaphoreType.DMA(dims)

    def message(angles):
        return shape(ns, angles * half, nr, dtype=BF16)

    conc = concentration.reshape(ns, na * nz, nr)
    field = pltpu.VMEM((ns, na * nz, nr), F32)
    *edges, first, last, mid_a, coef = call(
        functools.partial(head_kernel, (na, nz, first_lo, first_hi, planes)),
        [shape(ns, na, nr)] * n_edges
        + [shape(ns, nz, nr)] * 2
        + [message(first_hi - first_lo), shape(RATE + 3, half, nr)],
        [HBM] * 6,
        [VM] * (n_edges + 4),
        [
            field, pltpu.VMEM((1, nr), F32), pltpu.VMEM(angular_rate.shape, F32),
            pltpu.SMEM(axial_diffusion.shape, F32), pltpu.SMEM(rate_constants.shape, F32),
            pltpu.SMEM(species_map.shape, jnp.int32), dma(8),
        ],
        (conc, courant[None], axial_diffusion, angular_rate, rate_constants, species_map),
        58,
    )
    opp_a = lax.ppermute(mid_a, "ang", opposite)
    low, high = plane_halos(edges, planes)
    angle_before = lax.ppermute(last, "ang", [(i, (i + 1) % count) for i in range(count)])
    angle_after = lax.ppermute(first, "ang", [(i, (i - 1) % count) for i in range(count)])
    flags_opp = lax.ppermute(wall_flags, "ang", opposite)

    mid_c, mid_d = call(
        functools.partial(
            inner_kernel,
            (na, nz),
            ((0, inner), (1, ((last_lo, last_hi - last_lo),))),
        ),
        [message(inner_count), message(last_hi - last_lo)],
        [ANY, VM],
        [VM] * 2,
        [field, pltpu.SemaphoreType.DMA],
        (conc, coef),
        8,
    )
    out1, out2 = call(
        functools.partial(frame_kernel, (na, nz, ends, planes)),
        [message(na // 2), message(na // 2 + 2 * ends)],
        [ANY] * 3 + [VM] * 3,
        [VM] * 2,
        [pltpu.VMEM((ns, (na + 2) * nz, nr), F32), dma(3)],
        (conc, angle_before, angle_after, low, high, coef),
        8,
    )
    (out1, out2), opp_a = after((out1, out2), opp_a)
    opp_1 = lax.ppermute(out1, "ang", opposite)
    opp_2 = lax.ppermute(out2, "ang", opposite)
    weights, keep = call(
        weights_kernel,
        [shape(ns, nr, 2 * nr, dtype=BF16), shape(2, ns, na, LANES)],
        [ANY, SM, SM],
        [VM] * 2,
        [pltpu.VMEM((ns, nr, nr), BF16), pltpu.VMEM((ns, nr, nr), BF16), dma(2, ns)],
        (radial_inverse, wall_flags, flags_opp),
        12,
    )

    def state(angles):
        return shape(2, ns, angles * half, nr)

    count_a, side = first_hi - first_lo, na // 2
    (mid_first,) = call(
        functools.partial(radial_kernel, ((0, first_lo, 0, count_a),), (), half),
        [state(count_a)],
        [VM] * 4,
        [VM],
        [],
        (weights, keep, mid_a, opp_a),
        8,
    )
    opp_1, mid_first = after(opp_1, mid_first)
    (outer_first,) = call(
        functools.partial(radial_kernel, ((0, 0, 0, side),), (), half),
        [state(side)],
        [VM] * 4,
        [VM],
        [],
        (weights, keep, out1, opp_1),
        8,
    )
    mid_c, outer_first = after(mid_c, outer_first)
    opp_c = lax.ppermute(mid_c, "ang", opposite)
    mid_d, opp_2 = after(mid_d, opp_2)
    opp_d = lax.ppermute(mid_d, "ang", opposite)
    runs = ((1, side, side, side), (0, 0, 0, ends), (0, na - ends, ends, ends))
    mid_ends, outer_state, *rest = call(
        functools.partial(
            radial_edges_kernel, (na, nz, planes), runs, ((0, 0, 1, 0, side),), half
        ),
        [state(2 * ends), state(na)]
        + [shape(2, ns, na, nr, dtype=BF16)] * n_edges
        + [shape(2, ns, nz, nr, dtype=BF16)] * 2,
        [VM] * 5,
        [VM] * (4 + n_edges),
        [pltpu.VMEM((n_edges, na, nr), F32)],
        (weights, keep, out2, opp_2, outer_first),
        8,
    )
    *edges, first, last = rest
    low, high = plane_halos(edges, planes)
    angle_before = lax.ppermute(last, "ang", ring(count, 1))
    angle_after = lax.ppermute(first, "ang", ring(count, -1))
    (mid_state,) = call(
        functools.partial(
            radial_kernel,
            tuple((0, begin, begin, n) for begin, n in inner),
            ((0, 0, 0, first_lo, count_a), (1, 0, 0, 0, ends), (1, ends, 0, na - ends, ends)),
            half,
        ),
        [state(na)],
        [VM] * 6,
        [VM],
        [],
        (weights, keep, mid_c, opp_c, mid_first, mid_ends),
        8,
    )

    stage = [pltpu.VMEM((ns, na * nz, 2 * nr), BF16), pltpu.VMEM((ns, na, nz, nr), F32)]
    edge_scratch = [pltpu.VMEM((2, ns, na, nr), F32)] * 2
    early = ((0, last_lo - 1), (last_hi + 1, na - last_hi - 1))
    partial = call(
        functools.partial(early_kernel, (na, nz, early, count // 2, planes)),
        shape(ns, na, nz, nr),
        [VM] * 9,
        ANY,
        [pltpu.VMEM((2, ns, nz, nr), F32)] * 2 + edge_scratch + stage + [dma(2, ns)],
        (weights, keep, mid_state, outer_state, angle_before, angle_after, low, high, coef),
        12,
    )
    wide = last_hi - last_lo + 4
    return call(
        functools.partial(late_kernel, (na, nz, last_lo, last_hi, planes)),
        shape(ns, na, nz, nr),
        [ANY] + [VM] * 9,
        ANY,
        [pltpu.VMEM((2, ns, wide * half, nr), F32)] + edge_scratch + stage + [dma(ns)],
        (partial, mid_state, weights, keep, mid_d, opp_d, outer_state, low, high, coef),
        12,
        {0: 0},
    )


def solution(mesh):
    in_specs = (P(None, "ang", "ax", None), P(), P(), P(), P(), P(), P(None, "ang"), P())
    out_specs = P(None, "ang", "ax", None)
    return jax.shard_map(
        per_device, mesh=mesh, in_specs=in_specs, out_specs=out_specs, check_vma=False
    )
```

```python
import functools

import jax
import jax.numpy as jnp
from jax import lax
from jax.experimental import pallas as pl
from jax.experimental.pallas import tpu as pltpu
from jax.sharding import PartitionSpec as P

F32 = jnp.float32
BF16 = jnp.bfloat16
MIB = 1024 * 1024
LANES = 128

ANY = pl.BlockSpec(memory_space=pl.ANY)
HBM = pl.BlockSpec(memory_space=pltpu.HBM)
VM = pl.BlockSpec(memory_space=pltpu.VMEM)
SM = pl.BlockSpec(memory_space=pltpu.SMEM)

OWN, BEFORE, ANGULAR, AXIAL, RATE = 0, 3, 6, 9, 12


def call(body, out_shape, in_specs, out_specs, scratch, args, mib, aliases=None):
    return pl.pallas_call(
        body,
        out_shape=out_shape,
        in_specs=in_specs,
        out_specs=out_specs,
        scratch_shapes=scratch,
        input_output_aliases=aliases or {},
        cost_estimate=pl.CostEstimate(flops=1, bytes_accessed=1, transcendentals=0),
        compiler_params=pltpu.CompilerParams(vmem_limit_bytes=mib * MIB),
    )(*args)


def shape(*dims, dtype=F32):
    return jax.ShapeDtypeStruct(dims, dtype)


def transport(now, before, after, around, coef):
    made = (
        coef[RATE] * (now[1] * now[2]),
        coef[RATE + 1] * (now[0] * now[2]),
        coef[RATE + 2] * (now[0] * now[1]),
    )
    spent = made[0] + made[1] + made[2]
    out = []
    for s in range(3):
        value = now[s] * coef[OWN + s] + before[s] * coef[BEFORE + s]
        value = value + after[s] * coef[AXIAL + s] + around[s] * coef[ANGULAR + s]
        out.append(value + ((made[s] + made[s]) - spent))
    return out


def turned(first, second, rows):
    first, second = pltpu.roll(first, rows // 2, 0), pltpu.roll(second, rows // 2, 0)
    upper = lax.broadcasted_iota(jnp.int32, first.shape, 0) < rows // 2
    return jnp.where(upper, first, second), jnp.where(upper, second, first)


def first_step(read, low, high, coef, half):
    tiles = [[read(s, 0, k) for s in range(3)] for k in range(2)]
    around = [[read(s, -1, k) + read(s, 1, k) for s in range(3)] for k in range(2)]
    row = lax.broadcasted_iota(jnp.int32, tiles[0][0].shape, 0)
    top, bottom = row == 0, row == half - 1
    fall = [[pltpu.roll(v, 1, 0) for v in tile] for tile in tiles]
    rise = [[pltpu.roll(v, half - 1, 0) for v in tile] for tile in tiles]
    out = []
    for k in range(2):
        other = 1 - k
        before = [
            jnp.where(top, low(s) if low is not None and k == 0 else fall[other][s], fall[k][s])
            for s in range(3)
        ]
        after = [
            jnp.where(bottom, high(s) if high is not None and k == 1 else rise[other][s], rise[k][s])
            for s in range(3)
        ]
        out.append(transport(tiles[k], before, after, around[k], coef))
    pairs = [turned(out[0][s], out[1][s], half) for s in range(3)]
    return [p[0] for p in pairs], [p[1] for p in pairs]


def second_step(read, low, high, coef, half):
    tiles = [[read(k, s, 0) for s in range(3)] for k in range(2)]
    around = [[read(k, s, -1) + read(k, s, 1) for s in range(3)] for k in range(2)]
    row = lax.broadcasted_iota(jnp.int32, tiles[0][0].shape, 0)
    top, bottom = row == 0, row == half - 1
    first, last = row == half // 2, row == half // 2 - 1
    fall = [[pltpu.roll(v, 1, 0) for v in tile] for tile in tiles]
    rise = [[pltpu.roll(v, half - 1, 0) for v in tile] for tile in tiles]
    out = []
    for k in range(2):
        before = [jnp.where(top, fall[1 - k][s], fall[k][s]) for s in range(3)]
        after = [jnp.where(bottom, rise[1 - k][s], rise[k][s]) for s in range(3)]
        if k == 1:
            before = [jnp.where(first, low(s), before[s]) for s in range(3)]
            after = [jnp.where(last, high(s), after[s]) for s in range(3)]
        out.append(transport(tiles[k], before, after, around[k], coef))
    return out


def pack(tiles):
    return jnp.concatenate(tiles, 0).astype(BF16)


def at_rows(start, count, step):
    return pl.ds(pl.multiple_of(start, step), count)


def field_reader(field, t, nz):
    half = nz // 2
    return lambda s, shift, k: field[s, at_rows((t + shift) * nz + k * half, half, half), :]


def mid_run(field, out_of, begin, count, at, coef, nz):
    half = nz // 2

    def pair(step, carry):
        t = begin + step * 2
        tiles = [first_step(field_reader(field, t + k, nz), None, None, coef, half)[0] for k in range(2)]
        for s in range(3):
            out_of(s)[at_rows(at * half + step * nz, nz, nz), :] = pack([tiles[0][s], tiles[1][s]])
        return carry

    lax.fori_loop(0, count // 2, pair, 0)


def head_kernel(sizes, conc, cour, diff, ang, rate, smap, flags, *rest):
    na, nz, lo, hi, planes = sizes
    edges = rest[: 1 if planes == 2 else 2]
    first, last, mid, coef, field, flag_v, cour_v, ang_v, diff_s, rate_s, map_s, flags_s, sems = rest[
        len(edges) :
    ]
    half = nz // 2
    inner = pl.ds((lo - 1) * nz, (hi - lo + 2) * nz)
    left = pl.ds(0, (lo - 1) * nz)
    right = pl.ds((hi + 1) * nz, (na - hi - 1) * nz)
    small = [
        pltpu.make_async_copy(src, dst, sems.at[k + 3])
        for k, (src, dst) in enumerate(
            ((cour, cour_v), (ang, ang_v), (diff, diff_s), (rate, rate_s), (smap, map_s), (flags, flags_s))
        )
    ]
    copies = [
        pltpu.make_async_copy(conc.at[:, rows], field.at[:, rows], sems.at[k])
        for k, rows in enumerate((inner, left, right))
    ]
    for copy in small + copies:
        copy.start()
    for copy in small:
        copy.wait()
    tile = coef.shape[1:]
    for s in range(3):
        courant, angular = cour_v[...], ang_v[s : s + 1, :]
        axial = diff_s[s]
        total = jnp.float32(0.0)
        for k in range(map_s.shape[0]):
            total = total + jnp.where(map_s[k, 2] == s, rate_s[k], 0.0)
        coef[OWN + s] = jnp.broadcast_to((1.0 - 2.0 * axial) - courant - 2.0 * angular, tile)
        coef[BEFORE + s] = jnp.broadcast_to(courant + axial, tile)
        coef[ANGULAR + s] = jnp.broadcast_to(angular, tile)
        coef[AXIAL + s] = jnp.full(tile, axial, F32)
        coef[RATE + s] = jnp.full(tile, total, F32)
    lane = lax.broadcasted_iota(jnp.int32, (1, LANES), 1)
    for t in range(na):
        row = jnp.zeros((1, LANES), jnp.int32)
        for s in range(3):
            row = jnp.where(lane == s, flags_s[s, t], row)
        flag_v[t : t + 1, :] = row.astype(F32)
    rows = (hi - lo) * half
    span = pl.ds(3 * rows, na)
    mid[span, :] = jnp.zeros((na, mid.shape[1]), BF16)
    mid[span, :LANES] = flag_v[...].astype(BF16)
    copies[0].wait()
    mid_run(field, lambda s: mid.at[pl.ds(s * rows, rows)], lo, hi - lo, 0, coef, nz)
    copies[1].wait()
    copies[2].wait()
    for s in range(3):
        if planes == 2:
            row = jnp.where(lax.axis_index("ax") == 0, nz - 1, 0)
            for t in range(na):
                edges[0][s, t : t + 1, :] = field[s, pl.ds(t * nz + row, 1), :]
        else:
            for t in range(na):
                edges[0][s, t : t + 1, :] = field[s, t * nz : t * nz + 1, :]
                edges[1][s, t : t + 1, :] = field[s, (t + 1) * nz - 1 : (t + 1) * nz, :]
        first[s] = field[s, pl.ds(0, nz), :]
        last[s] = field[s, pl.ds((na - 1) * nz, nz), :]


def inner_kernel(sizes, runs, conc, coef, *rest):
    na, nz = sizes
    outs, field, sem = rest[:-2], rest[-2], rest[-1]
    copy = pltpu.make_async_copy(conc, field, sem)
    copy.start()
    copy.wait()
    for out, parts in runs:
        at = 0
        for begin, count in parts:
            mid_run(field, outs[out].at.__getitem__, begin, count, at, coef, nz)
            at += count


def edge_weights(planes):
    if planes != 2:
        return 1.0, 1.0
    place = lax.axis_index("ax")
    return jnp.where(place == 1, 1.0, 0.0), jnp.where(place == 0, 1.0, 0.0)


def frame_kernel(
    sizes, conc, before, after, low, high, coef_in, out1, out2, field, coef, sems
):
    na, nz, ends, planes = sizes
    half = nz // 2
    copies = [
        pltpu.make_async_copy(conc, field.at[:, pl.ds(nz, na * nz)], sems.at[0]),
        pltpu.make_async_copy(before, field.at[:, pl.ds(0, nz)], sems.at[1]),
        pltpu.make_async_copy(after, field.at[:, pl.ds((na + 1) * nz, nz)], sems.at[2]),
        pltpu.make_async_copy(coef_in, coef, sems.at[3]),
    ]
    for copy in copies:
        copy.start()
    low_weight, high_weight = edge_weights(planes)
    for copy in copies:
        copy.wait()

    def angle(t):
        return first_step(
            field_reader(field, t + 1, nz),
            lambda s: low[s, pl.ds(t, 1), :] * low_weight,
            lambda s: high[s, pl.ds(t, 1), :] * high_weight,
            coef,
            half,
        )

    def pair(t, out, row, ends_row):
        tiles = [angle(t), angle(t + 1)]
        for s in range(3):
            out[s, pl.ds(row, nz), :] = pack([tiles[0][1][s], tiles[1][1][s]])
            if ends_row is not None:
                out2[s, pl.ds(ends_row, nz), :] = pack([tiles[0][0][s], tiles[1][0][s]])

    quarter = na // 4
    tail = na // 2 * half
    pair(0, out1, 0, tail)
    pair(na - 2, out2, (na // 2 - 2) * half, tail + nz)

    def first_part(step, carry):
        pair(step * 2, out1, pl.multiple_of(step * nz, nz), None)
        return carry

    def second_part(step, carry):
        pair(na // 2 + step * 2, out2, pl.multiple_of(step * nz, nz), None)
        return carry

    lax.fori_loop(1, quarter, first_part, 0)
    lax.fori_loop(0, quarter - 1, second_part, 0)


def weights_kernel(matrix, mine, theirs, out, keep, left, lower, sems):
    half = out.shape[1]
    copies = []
    for s in range(out.shape[0]):
        for k, ref in enumerate((left, lower)):
            src = matrix.at[s, pl.ds(k * half, half), pl.ds(0, half)]
            copies.append(pltpu.make_async_copy(src, ref.at[s], sems.at[k, s]))
    for copy in copies:
        copy.start()
    na = keep.shape[2]
    lane = lax.broadcasted_iota(jnp.int32, (na, LANES), 1)
    for ab, ref in enumerate((mine, theirs)):
        flags = ref[pl.ds(ref.shape[0] - na, na), :LANES].astype(F32)
        for s in range(out.shape[0]):
            moved = pltpu.roll(flags, LANES - s, 1) if s else flags
            keep[ab, s] = jnp.where(lane == 0, 1.0 - moved, 1.0)
    row = lax.broadcasted_iota(jnp.int32, (half, half), 0)
    col = lax.broadcasted_iota(jnp.int32, (half, half), 1)
    row = jnp.maximum(row, 1)
    pick = jnp.where(col == row, 1.0, 0.0).astype(BF16)
    flip = jnp.where(col == half - 1 - row, 1.0, 0.0).astype(BF16)
    for copy in copies:
        copy.wait()
    for s in range(out.shape[0]):
        out[s, :, :half] = jnp.dot(pick, left[s], preferred_element_type=F32).astype(BF16)
        out[s, :, half:] = jnp.dot(flip, lower[s], preferred_element_type=F32).astype(BF16)


def rows_product(rows, weights):
    return lax.dot_general(rows, weights, (((1,), (1,)), ((), ())), preferred_element_type=F32)


def both_sides(mine, theirs, weights):
    rows = jnp.concatenate(
        [jnp.concatenate([mine, theirs], 1), jnp.concatenate([theirs, mine], 1)], 0
    )
    return rows_product(rows, weights)


def store_run(state, s, begin, place, count, at, value, keep, half):
    total = value.shape[0] // 2
    for ab in range(2):
        part = value[ab * total + at * half : ab * total + (at + count) * half]
        state[ab, s, pl.ds(place * half, count * half), LANES:] = part[:, LANES:]
        for k in range(count):
            state[ab, s, pl.ds((place + k) * half, half), :LANES] = (
                part[k * half : (k + 1) * half, :LANES] * keep[ab, s, begin + k : begin + k + 1, :]
            )


def species_rows(ref, s, runs, half):
    if len(ref.shape) == 3:
        return ref[s]
    rows = sum(run[3] for run in runs) * half
    return ref[pl.ds(s * rows, rows), :]


def radial_kernel(runs, copies, half, weights, keep, mine, theirs, *refs):
    n_in = 1 + max((part for part, *_ in copies), default=-1)
    parts, states = refs[:n_in], refs[n_in:]
    for s in range(3):
        value = both_sides(species_rows(mine, s, runs, half), species_rows(theirs, s, runs, half), weights[s])
        at = 0
        for which, begin, place, count in runs:
            store_run(states[which], s, begin, place, count, at, value, keep, half)
            at += count
    for part, source, which, place, count in copies:
        to, rows = pl.ds(place * half, count * half), pl.ds(source * half, count * half)
        for ab in range(2):
            for s in range(3):
                states[which][ab, s, to, :] = parts[part][ab, s, rows, :]


def edges_of_state(na, nz, planes, mid, mid_end, outer, edges, first, last, stage):
    half = nz // 2
    if planes == 2:
        row = jnp.where(lax.axis_index("ax") == 0, half // 2 - 1, half // 2)
    end = pl.ds((na - 1) * half, half)
    ends_end = pl.ds(mid_end.shape[2] - half, half)
    for ab in range(2):
        for s in range(3):
            for t in range(na):
                to = pl.ds(t, 1)
                at = t * half + half // 2
                if planes == 2:
                    stage[0, to, :] = outer[ab, s, pl.ds(t * half + row, 1), :]
                else:
                    stage[0, to, :] = outer[ab, s, at : at + 1, :]
                    stage[1, to, :] = outer[ab, s, at - 1 : at, :]
            for k, edge in enumerate(edges):
                edge[ab, s] = stage[k].astype(BF16)
            begin = pl.ds(0, half)
            first[ab, s] = pack([mid[ab, s, begin, :], outer[ab, s, begin, :]])
            last[ab, s] = pack([mid_end[ab, s, ends_end, :], outer[ab, s, end, :]])


def radial_edges_kernel(sizes, runs, copies, half, weights, keep, mine, theirs, *refs):
    na, nz, planes = sizes
    n_edges = 1 if planes == 2 else 2
    *edges, first, last, stage = refs[-3 - n_edges :]
    refs = refs[: -3 - n_edges]
    radial_kernel(runs, copies, half, weights, keep, mine, theirs, *refs)
    edges_of_state(na, nz, planes, refs[-3], refs[-2], refs[-1], edges, first, last, stage)


def explicit_angle(t, reader, low, high, edge_factors, coef, rows, nz):
    half = nz // 2
    for ab in range(2):
        out = second_step(
            functools.partial(reader, ab),
            lambda s: low[ab, s, pl.ds(t, 1), :] * edge_factors[0],
            lambda s: high[ab, s, pl.ds(t, 1), :] * edge_factors[1],
            coef,
            half,
        )
        width = out[0][0].shape[1]
        for s in range(3):
            rows[s, at_rows(t * nz, nz, nz), ab * width : (ab + 1) * width] = pack(
                [out[0][s], out[1][s]]
            )


def explicit_run(begin, count, states, low, high, edge_factors, coef, rows, nz):
    half = nz // 2

    def one(step, carry):
        t = begin + step

        def reader(ab, k, s, shift):
            state, base = states[k]
            return state[ab, s, at_rows((t - base + shift) * half, half, half), :]

        explicit_angle(t, reader, low, high, edge_factors, coef, rows, nz)
        return carry

    lax.fori_loop(0, count, one, 0)


def finish_run(begin, count, s, rows, weights, keep, result, nz):
    half = nz // 2
    value = rows_product(rows[s, pl.ds(begin * nz, count * nz), :], weights[s])
    for k in range(count):
        t = begin + k
        parts = turned(value[k * nz + half : (k + 1) * nz], value[k * nz : k * nz + half], half)
        for p in range(2):
            span = pl.ds(p * half, half)
            result[s, t, span, LANES:] = parts[p][:, LANES:]
            result[s, t, span, :LANES] = parts[p][:, :LANES] * keep[0, s, t : t + 1, :]


def widen(pairs):
    for source, target in pairs:
        target[...] = source[...].astype(F32)


def early_kernel(sizes, *refs):
    na, nz, runs, base, half_ring, planes = sizes
    if len(refs) == 18:
        refs = refs[1:]
    (weights, keep, mid, outer, before_low, after_low, low_low, high_low, coef, out,
     before, after, low, high, rows, result, out_sems) = refs
    half = nz // 2
    place = lax.rem(lax.axis_index("ang"), half_ring)
    wrap_before = jnp.where(place == 0, 1, 0)
    wrap_after = jnp.where(place == half_ring - 1, 1, 0)
    factors = edge_weights(planes)
    states = ((mid, base), (outer, 0))
    widen(((low_low, low), (high_low, high)))
    for begin, count in runs:
        end = begin + count
        if begin == 0:
            widen(((before_low, before),))

            def reader(ab, k, s, shift):
                if shift == -1:
                    source = jnp.where(wrap_before == 1, 1 - ab, ab)
                    return before[source, s, pl.ds(k * half, half), :]
                return states[k][0][ab, s, pl.ds((shift - states[k][1]) * half, half), :]

            explicit_angle(0, reader, low, high, factors, coef, rows, nz)
        if end == na:
            widen(((after_low, after),))

            def reader(ab, k, s, shift):
                if shift == 1:
                    source = jnp.where(wrap_after == 1, 1 - ab, ab)
                    return after[source, s, pl.ds(k * half, half), :]
                return states[k][0][ab, s, pl.ds((na - 1 + shift - states[k][1]) * half, half), :]

            explicit_angle(na - 1, reader, low, high, factors, coef, rows, nz)
        start, stop = max(begin, 1), min(end, na - 1)
        if stop > start:
            explicit_run(start, stop - start, states, low, high, factors, coef, rows, nz)
    leaves = []
    for s in range(3):
        for k, (begin, count) in enumerate(runs):
            finish_run(begin, count, s, rows, weights, keep, result, nz)
            span = pl.ds(begin, count)
            leave = pltpu.make_async_copy(result.at[s, span], out.at[s, span], out_sems.at[k, s])
            leave.start()
            leaves.append(leave)
    for leave in leaves:
        leave.wait()


def late_kernel(
    sizes, given, state, weights, keep, mine, theirs, outer, low_low, high_low, coef,
    out, mid, low, high, rows, result, out_sems,
):
    na, nz, lo, hi, base, planes = sizes
    half = nz // 2
    factors = edge_weights(planes)
    count = hi - lo
    widen(((low_low, low), (high_low, high)))
    for s in range(3):
        value = both_sides(mine[s], theirs[s], weights[s])
        store_run(mid, s, lo, 2, count, 0, value, keep, half)
        for ab in range(2):
            for k in range(2):
                to = pl.ds((2 + count) * k * half, 2 * half)
                mid[ab, s, to, :] = state[
                    ab, s, pl.ds((lo - 2 - base + (2 + count) * k) * half, 2 * half), :
                ]
    explicit_run(lo - 1, count + 2, ((mid, lo - 2), (outer, 0)), low, high, factors, coef, rows, nz)
    leaves = []
    for s in range(3):
        finish_run(lo - 1, count + 2, s, rows, weights, keep, result, nz)
        span = pl.ds(lo - 1, count + 2)
        leave = pltpu.make_async_copy(result.at[s, span], out.at[s, span], out_sems.at[s])
        leave.start()
        leaves.append(leave)
    for leave in leaves:
        leave.wait()


def ring(count, step):
    half = count // 2
    return [(i, i // half * half + (i % half + step) % half) for i in range(count)]


def plane_halos(edges, planes):
    if planes == 2:
        got = lax.ppermute(edges[0], "ax", [(0, 1), (1, 0)])
        return got, got
    up = [(i, i + 1) for i in range(planes - 1)]
    down = [(i + 1, i) for i in range(planes - 1)]
    return lax.ppermute(edges[1], "ax", up), lax.ppermute(edges[0], "ax", down)


def after(value, done):
    return lax.optimization_barrier((value, done))


def per_device(
    concentration, courant, axial_diffusion, angular_rate, rate_constants, species_map,
    wall_flags, radial_inverse,
):
    ns, na, nz, nr = concentration.shape
    half = nz // 2
    count = lax.axis_size("ang")
    planes = lax.axis_size("ax")
    n_edges = 1 if planes == 2 else 2
    quarter = na // 4
    ends = 2
    side = na // 2
    first_lo, first_hi = ends, side
    last_lo, last_hi = na - 3 * ends, na - ends
    opposite = [(i, (i + count // 2) % count) for i in range(count)]

    def dma(*dims):
        return pltpu.SemaphoreType.DMA(dims)

    def message(angles):
        return shape(ns, angles * half, nr, dtype=BF16)

    conc = concentration.reshape(ns, na * nz, nr)
    field = pltpu.VMEM((ns, na * nz, nr), F32)
    *edges, first, last, mid_a, coef = call(
        functools.partial(head_kernel, (na, nz, first_lo, first_hi, planes)),
        [shape(ns, na, nr)] * n_edges
        + [shape(ns, nz, nr)] * 2
        + [
            shape(ns * (first_hi - first_lo) * half + na, nr, dtype=BF16),
            shape(RATE + 3, half, nr),
        ],
        [HBM] * 7,
        [VM] * (n_edges + 4),
        [
            field, pltpu.VMEM((na, LANES), F32), pltpu.VMEM((1, nr), F32), pltpu.VMEM(angular_rate.shape, F32),
            pltpu.SMEM(axial_diffusion.shape, F32), pltpu.SMEM(rate_constants.shape, F32),
            pltpu.SMEM(species_map.shape, jnp.int32), pltpu.SMEM(wall_flags.shape, jnp.int32), dma(9),
        ],
        (conc, courant[None], axial_diffusion, angular_rate, rate_constants, species_map, wall_flags),
        58,
    )
    opp_a = lax.ppermute(mid_a, "ang", opposite)
    low, high = plane_halos(edges, planes)
    angle_before = lax.ppermute(last, "ang", [(i, (i + 1) % count) for i in range(count)])
    angle_after = lax.ppermute(first, "ang", [(i, (i - 1) % count) for i in range(count)])
    mid_x, mid_l = call(
        functools.partial(
            inner_kernel,
            (na, nz),
            ((0, ((first_hi, last_lo - first_hi),)), (1, ((last_lo, last_hi - last_lo),))),
        ),
        [message(last_lo - first_hi), message(last_hi - last_lo)],
        [ANY, VM],
        [VM] * 2,
        [field, pltpu.SemaphoreType.DMA],
        (conc, coef),
        8,
    )
    out1, out2 = call(
        functools.partial(frame_kernel, (na, nz, ends, planes)),
        [message(na // 2), message(na // 2 + 2 * ends)],
        [ANY] * 3 + [VM] * 2 + [ANY],
        [VM] * 2,
        [pltpu.VMEM((ns, (na + 2) * nz, nr), F32), pltpu.VMEM((RATE + 3, half, nr), F32), dma(4)],
        (conc, angle_before, angle_after, low, high, coef),
        8,
    )
    (out1, out2), opp_a = after((out1, out2), opp_a)
    opp_1 = lax.ppermute(out1, "ang", opposite)
    opp_2 = lax.ppermute(out2, "ang", opposite)
    weights, keep = call(
        weights_kernel,
        [shape(ns, nr, 2 * nr, dtype=BF16), shape(2, ns, na, LANES)],
        [ANY, VM, VM],
        [VM] * 2,
        [pltpu.VMEM((ns, nr, nr), BF16), pltpu.VMEM((ns, nr, nr), BF16), dma(2, ns)],
        (radial_inverse, mid_a, opp_a),
        12,
    )

    def state(angles):
        return shape(2, ns, angles * half, nr)

    count_a = first_hi - first_lo
    (mid_first,) = call(
        functools.partial(radial_kernel, ((0, first_lo, 0, count_a),), (), half),
        [state(count_a)],
        [VM] * 4,
        [VM],
        [],
        (weights, keep, mid_a, opp_a),
        8,
    )
    opp_1, mid_first = after(opp_1, mid_first)
    mid_x, opp_1 = after(mid_x, opp_1)
    opp_x = lax.ppermute(mid_x, "ang", opposite)
    (outer_first,) = call(
        functools.partial(radial_kernel, ((0, 0, 0, side),), (), half),
        [state(side)],
        [VM] * 4,
        [VM],
        [],
        (weights, keep, out1, opp_1),
        8,
    )
    mid_l, opp_2 = after(mid_l, opp_2)
    opp_l = lax.ppermute(mid_l, "ang", opposite)
    runs = ((2, side, side, side), (0, 0, 0, ends), (1, na - ends, 0, ends))
    mid_left, ends_right, outer_state, *rest = call(
        functools.partial(
            radial_edges_kernel,
            (na, nz, planes),
            runs,
            ((0, 0, 0, first_lo, count_a), (1, 0, 2, 0, side)),
            half,
        ),
        [state(side), state(ends), state(na)]
        + [shape(2, ns, na, nr, dtype=BF16)] * n_edges
        + [shape(2, ns, nz, nr, dtype=BF16)] * 2,
        [VM] * 6,
        [VM] * (5 + n_edges),
        [pltpu.VMEM((n_edges, na, nr), F32)],
        (weights, keep, out2, opp_2, mid_first, outer_first),
        8,
    )
    *edges, first, last = rest
    low, high = plane_halos(edges, planes)
    angle_before = lax.ppermute(last, "ang", ring(count, 1))
    angle_after = lax.ppermute(first, "ang", ring(count, -1))
    stage = [pltpu.VMEM((ns, na * nz, 2 * nr), BF16), pltpu.VMEM((ns, na, nz, nr), F32)]
    edge_scratch = [pltpu.VMEM((2, ns, na, nr), F32)] * 2
    def early(runs, base, mid, given):
        return call(
            functools.partial(early_kernel, (na, nz, runs, base, count // 2, planes)),
            shape(ns, na, nz, nr),
            [ANY] * len(given) + [VM] * 9,
            ANY,
            [pltpu.VMEM((2, ns, nz, nr), F32)] * 2 + edge_scratch + stage + [dma(len(runs), ns)],
            (*given, weights, keep, mid, outer_state, angle_before, angle_after, low, high, coef),
            12,
            {0: 0} if given else None,
        )

    partial = early(((0, first_hi - 1),), 0, mid_left, ())
    opp_x, partial = after(opp_x, partial)
    base = first_hi - 2
    (mid_right,) = call(
        functools.partial(
            radial_kernel,
            ((0, first_hi, 2, last_lo - first_hi),),
            ((0, base, 0, 0, 2), (1, 0, 0, na - ends - base, ends)),
            half,
        ),
        [state(na - base)],
        [VM] * 6,
        [VM],
        [],
        (weights, keep, mid_x, opp_x, mid_left, ends_right),
        8,
    )

    partial = early(
        ((first_hi - 1, last_lo - first_hi), (na - 1, 1)), base, mid_right, (partial,)
    )
    wide = last_hi - last_lo + 4
    return call(
        functools.partial(late_kernel, (na, nz, last_lo, last_hi, base, planes)),
        shape(ns, na, nz, nr),
        [ANY] + [VM] * 9,
        ANY,
        [pltpu.VMEM((2, ns, wide * half, nr), F32)] + edge_scratch + stage + [dma(ns)],
        (partial, mid_right, weights, keep, mid_l, opp_l, outer_state, low, high, coef),
        12,
        {0: 0},
    )


def solution(mesh):
    in_specs = (P(None, "ang", "ax", None), P(), P(), P(), P(), P(), P(None, "ang"), P())
    out_specs = P(None, "ang", "ax", None)
    return jax.shard_map(
        per_device, mesh=mesh, in_specs=in_specs, out_specs=out_specs, check_vma=False
    )
```

```python
import functools

import jax
import jax.numpy as jnp
from jax import lax
from jax.experimental import pallas as pl
from jax.experimental.pallas import tpu as pltpu
from jax.sharding import PartitionSpec as P

F32 = jnp.float32
BF16 = jnp.bfloat16
MIB = 1024 * 1024
LANES = 128

ANY = pl.BlockSpec(memory_space=pl.ANY)
HBM = pl.BlockSpec(memory_space=pltpu.HBM)
VM = pl.BlockSpec(memory_space=pltpu.VMEM)
SM = pl.BlockSpec(memory_space=pltpu.SMEM)

OWN, BEFORE, ANGULAR, AXIAL, RATE = 0, 3, 6, 9, 12


def call(body, out_shape, in_specs, out_specs, scratch, args, mib, aliases=None):
    return pl.pallas_call(
        body,
        out_shape=out_shape,
        in_specs=in_specs,
        out_specs=out_specs,
        scratch_shapes=scratch,
        input_output_aliases=aliases or {},
        cost_estimate=pl.CostEstimate(flops=1, bytes_accessed=1, transcendentals=0),
        compiler_params=pltpu.CompilerParams(vmem_limit_bytes=mib * MIB),
    )(*args)


def shape(*dims, dtype=F32):
    return jax.ShapeDtypeStruct(dims, dtype)


def transport(now, before, after, around, coef):
    made = (
        coef[RATE] * (now[1] * now[2]),
        coef[RATE + 1] * (now[0] * now[2]),
        coef[RATE + 2] * (now[0] * now[1]),
    )
    spent = made[0] + made[1] + made[2]
    out = []
    for s in range(3):
        value = now[s] * coef[OWN + s] + before[s] * coef[BEFORE + s]
        value = value + after[s] * coef[AXIAL + s] + around[s] * coef[ANGULAR + s]
        out.append(value + ((made[s] + made[s]) - spent))
    return out


def turned(first, second, rows):
    first, second = pltpu.roll(first, rows // 2, 0), pltpu.roll(second, rows // 2, 0)
    upper = lax.broadcasted_iota(jnp.int32, first.shape, 0) < rows // 2
    return jnp.where(upper, first, second), jnp.where(upper, second, first)


def first_step(read, low, high, coef, half):
    tiles = [[read(s, 0, k) for s in range(3)] for k in range(2)]
    around = [[read(s, -1, k) + read(s, 1, k) for s in range(3)] for k in range(2)]
    row = lax.broadcasted_iota(jnp.int32, tiles[0][0].shape, 0)
    top, bottom = row == 0, row == half - 1
    fall = [[pltpu.roll(v, 1, 0) for v in tile] for tile in tiles]
    rise = [[pltpu.roll(v, half - 1, 0) for v in tile] for tile in tiles]
    out = []
    for k in range(2):
        other = 1 - k
        before = [
            jnp.where(top, low(s) if low is not None and k == 0 else fall[other][s], fall[k][s])
            for s in range(3)
        ]
        after = [
            jnp.where(bottom, high(s) if high is not None and k == 1 else rise[other][s], rise[k][s])
            for s in range(3)
        ]
        out.append(transport(tiles[k], before, after, around[k], coef))
    pairs = [turned(out[0][s], out[1][s], half) for s in range(3)]
    return [p[0] for p in pairs], [p[1] for p in pairs]


def second_step(read, low, high, coef, half):
    tiles = [[read(k, s, 0) for s in range(3)] for k in range(2)]
    around = [[read(k, s, -1) + read(k, s, 1) for s in range(3)] for k in range(2)]
    row = lax.broadcasted_iota(jnp.int32, tiles[0][0].shape, 0)
    top, bottom = row == 0, row == half - 1
    first, last = row == half // 2, row == half // 2 - 1
    fall = [[pltpu.roll(v, 1, 0) for v in tile] for tile in tiles]
    rise = [[pltpu.roll(v, half - 1, 0) for v in tile] for tile in tiles]
    out = []
    for k in range(2):
        before = [jnp.where(top, fall[1 - k][s], fall[k][s]) for s in range(3)]
        after = [jnp.where(bottom, rise[1 - k][s], rise[k][s]) for s in range(3)]
        if k == 1:
            before = [jnp.where(first, low(s), before[s]) for s in range(3)]
            after = [jnp.where(last, high(s), after[s]) for s in range(3)]
        out.append(transport(tiles[k], before, after, around[k], coef))
    return out


def pack(tiles):
    return jnp.concatenate(tiles, 0).astype(BF16)


def at_rows(start, count, step):
    return pl.ds(pl.multiple_of(start, step), count)


def field_reader(field, t, nz):
    half = nz // 2
    return lambda s, shift, k: field[s, at_rows((t + shift) * nz + k * half, half, half), :]


def mid_run(field, out_of, begin, count, at, coef, nz):
    half = nz // 2

    def pair(step, carry):
        t = begin + step * 2
        tiles = [first_step(field_reader(field, t + k, nz), None, None, coef, half)[0] for k in range(2)]
        for s in range(3):
            out_of(s)[at_rows(at * half + step * nz, nz, nz), :] = pack([tiles[0][s], tiles[1][s]])
        return carry

    lax.fori_loop(0, count // 2, pair, 0)


def head_kernel(sizes, conc, cour, diff, ang, rate, smap, flags, *rest):
    na, nz, lo, hi, planes = sizes
    edges = rest[: 1 if planes == 2 else 2]
    first, last, mid, coef, field, flag_v, cour_v, ang_v, diff_s, rate_s, map_s, flags_s, sems = rest[
        len(edges) :
    ]
    half = nz // 2
    inner = pl.ds((lo - 1) * nz, (hi - lo + 2) * nz)
    left = pl.ds(0, (lo - 1) * nz)
    right = pl.ds((hi + 1) * nz, (na - hi - 1) * nz)
    small = [
        pltpu.make_async_copy(src, dst, sems.at[k + 3])
        for k, (src, dst) in enumerate(
            ((cour, cour_v), (ang, ang_v), (diff, diff_s), (rate, rate_s), (smap, map_s), (flags, flags_s))
        )
    ]
    copies = [
        pltpu.make_async_copy(conc.at[:, rows], field.at[:, rows], sems.at[k])
        for k, rows in enumerate((inner, left, right))
    ]
    for copy in small + copies:
        copy.start()
    for copy in small:
        copy.wait()
    tile = coef.shape[1:]
    for s in range(3):
        courant, angular = cour_v[...], ang_v[s : s + 1, :]
        axial = diff_s[s]
        total = jnp.float32(0.0)
        for k in range(map_s.shape[0]):
            total = total + jnp.where(map_s[k, 2] == s, rate_s[k], 0.0)
        coef[OWN + s] = jnp.broadcast_to((1.0 - 2.0 * axial) - courant - 2.0 * angular, tile)
        coef[BEFORE + s] = jnp.broadcast_to(courant + axial, tile)
        coef[ANGULAR + s] = jnp.broadcast_to(angular, tile)
        coef[AXIAL + s] = jnp.full(tile, axial, F32)
        coef[RATE + s] = jnp.full(tile, total, F32)
    lane = lax.broadcasted_iota(jnp.int32, (1, LANES), 1)
    for t in range(na):
        row = jnp.zeros((1, LANES), jnp.int32)
        for s in range(3):
            row = jnp.where(lane == s, flags_s[s, t], row)
        flag_v[t : t + 1, :] = row.astype(F32)
    rows = (hi - lo) * half
    span = pl.ds(3 * rows, na)
    mid[span, :] = jnp.zeros((na, mid.shape[1]), BF16)
    mid[span, :LANES] = flag_v[...].astype(BF16)
    copies[0].wait()
    mid_run(field, lambda s: mid.at[pl.ds(s * rows, rows)], lo, hi - lo, 0, coef, nz)
    copies[1].wait()
    copies[2].wait()
    for s in range(3):
        if planes == 2:
            row = jnp.where(lax.axis_index("ax") == 0, nz - 1, 0)
            for t in range(na):
                edges[0][s, t : t + 1, :] = field[s, pl.ds(t * nz + row, 1), :]
        else:
            for t in range(na):
                edges[0][s, t : t + 1, :] = field[s, t * nz : t * nz + 1, :]
                edges[1][s, t : t + 1, :] = field[s, (t + 1) * nz - 1 : (t + 1) * nz, :]
        first[s] = field[s, pl.ds(0, nz), :]
        last[s] = field[s, pl.ds((na - 1) * nz, nz), :]


def inner_kernel(sizes, runs, conc, coef, *rest):
    na, nz = sizes
    outs, field, sem = rest[:-2], rest[-2], rest[-1]
    copy = pltpu.make_async_copy(conc, field, sem)
    copy.start()
    copy.wait()
    for out, parts in runs:
        at = 0
        for begin, count in parts:
            mid_run(field, outs[out].at.__getitem__, begin, count, at, coef, nz)
            at += count


def edge_weights(planes):
    if planes != 2:
        return 1.0, 1.0
    place = lax.axis_index("ax")
    return jnp.where(place == 1, 1.0, 0.0), jnp.where(place == 0, 1.0, 0.0)


def frame_kernel(sizes, conc, low, high, coef_in, out1, out2, field, coef, sems):
    na, nz, ends, planes = sizes
    half = nz // 2
    copies = [
        pltpu.make_async_copy(conc, field, sems.at[0]),
        pltpu.make_async_copy(coef_in, coef, sems.at[1]),
    ]
    for copy in copies:
        copy.start()
    low_weight, high_weight = edge_weights(planes)
    for copy in copies:
        copy.wait()

    def part(begin, out):
        def pair(step, carry):
            tiles = []
            for k in range(2):
                t = begin + step * 2 + k
                tiles.append(
                    first_step(
                        field_reader(field, t, nz),
                        lambda s: low[s, pl.ds(t, 1), :] * low_weight,
                        lambda s: high[s, pl.ds(t, 1), :] * high_weight,
                        coef,
                        half,
                    )[1]
                )
            for s in range(3):
                out[s, at_rows(step * nz, nz, nz), :] = pack([tiles[0][s], tiles[1][s]])
            return carry

        lax.fori_loop(0, out.shape[1] // nz, pair, 0)

    part(ends, out1)
    part(ends + out1.shape[1] // half, out2)


def ends_kernel(sizes, conc, before, after, low, high, coef, out, field, sems):
    na, nz, planes = sizes
    half = nz // 2
    copies = [
        pltpu.make_async_copy(src, field.at[:, pl.ds(at * nz, count * nz)], sems.at[k])
        for k, (src, at, count) in enumerate(
            (
                (before, 0, 1),
                (conc.at[:, pl.ds(0, 3 * nz)], 1, 3),
                (conc.at[:, pl.ds((na - 3) * nz, 3 * nz)], 4, 3),
                (after, 7, 1),
            )
        )
    ]
    for copy in copies:
        copy.start()
    low_weight, high_weight = edge_weights(planes)
    for copy in copies:
        copy.wait()
    for k, (slot, first) in enumerate(((1, 0), (5, na - 2))):
        tiles = []
        for j in range(2):
            t = first + j
            tiles.append(
                first_step(
                    field_reader(field, slot + j, nz),
                    lambda s: low[s, t : t + 1, :] * low_weight,
                    lambda s: high[s, t : t + 1, :] * high_weight,
                    coef,
                    half,
                )
            )
        for s in range(3):
            out[s, pl.ds(k * nz, nz), :] = pack([tiles[0][1][s], tiles[1][1][s]])
            out[s, pl.ds((k + 2) * nz, nz), :] = pack([tiles[0][0][s], tiles[1][0][s]])


def weights_kernel(matrix, mine, theirs, out, keep, left, lower, sems):
    half = out.shape[1]
    copies = []
    for s in range(out.shape[0]):
        for k, ref in enumerate((left, lower)):
            src = matrix.at[s, pl.ds(k * half, half), pl.ds(0, half)]
            copies.append(pltpu.make_async_copy(src, ref.at[s], sems.at[k, s]))
    for copy in copies:
        copy.start()
    na = keep.shape[2]
    lane = lax.broadcasted_iota(jnp.int32, (na, LANES), 1)
    for ab, ref in enumerate((mine, theirs)):
        flags = ref[pl.ds(ref.shape[0] - na, na), :LANES].astype(F32)
        for s in range(out.shape[0]):
            moved = pltpu.roll(flags, LANES - s, 1) if s else flags
            keep[ab, s] = jnp.where(lane == 0, 1.0 - moved, 1.0)
    row = lax.broadcasted_iota(jnp.int32, (half, half), 0)
    col = lax.broadcasted_iota(jnp.int32, (half, half), 1)
    row = jnp.maximum(row, 1)
    pick = jnp.where(col == row, 1.0, 0.0).astype(BF16)
    flip = jnp.where(col == half - 1 - row, 1.0, 0.0).astype(BF16)
    for copy in copies:
        copy.wait()
    for s in range(out.shape[0]):
        out[s, :, :half] = jnp.dot(pick, left[s], preferred_element_type=F32).astype(BF16)
        out[s, :, half:] = jnp.dot(flip, lower[s], preferred_element_type=F32).astype(BF16)


def rows_product(rows, weights):
    return lax.dot_general(rows, weights, (((1,), (1,)), ((), ())), preferred_element_type=F32)


def both_sides(mine, theirs, weights):
    rows = jnp.concatenate(
        [jnp.concatenate([mine, theirs], 1), jnp.concatenate([theirs, mine], 1)], 0
    )
    return rows_product(rows, weights)


def store_run(state, s, begin, place, count, at, value, keep, half):
    total = value.shape[0] // 2
    for ab in range(2):
        part = value[ab * total + at * half : ab * total + (at + count) * half]
        state[ab, s, pl.ds(place * half, count * half), LANES:] = part[:, LANES:]
        for k in range(count):
            state[ab, s, pl.ds((place + k) * half, half), :LANES] = (
                part[k * half : (k + 1) * half, :LANES] * keep[ab, s, begin + k : begin + k + 1, :]
            )


def species_rows(ref, s, runs, half):
    if len(ref.shape) == 3:
        return ref[s]
    rows = sum(run[3] for run in runs) * half
    return ref[pl.ds(s * rows, rows), :]


def radial_kernel(plan, copies, half, weights, keep, *refs):
    n = len(plan)
    mines, theirs, refs = refs[:n], refs[n : 2 * n], refs[2 * n :]
    n_in = 1 + max((part for part, *_ in copies), default=-1)
    parts, states = refs[:n_in], refs[n_in:]
    for s in range(3):
        for k, runs in enumerate(plan):
            value = both_sides(
                species_rows(mines[k], s, runs, half),
                species_rows(theirs[k], s, runs, half),
                weights[s],
            )
            at = 0
            for which, begin, place, count in runs:
                store_run(states[which], s, begin, place, count, at, value, keep, half)
                at += count
    for part, source, which, place, count in copies:
        to, rows = pl.ds(place * half, count * half), pl.ds(source * half, count * half)
        for ab in range(2):
            for s in range(3):
                states[which][ab, s, to, :] = parts[part][ab, s, rows, :]


def edges_of_state(na, nz, planes, mid, mid_end, outer, edges, first, last, stage):
    half = nz // 2
    if planes == 2:
        row = jnp.where(lax.axis_index("ax") == 0, half // 2 - 1, half // 2)
    end = pl.ds((na - 1) * half, half)
    ends_end = pl.ds(mid_end.shape[2] - half, half)
    for ab in range(2):
        for s in range(3):
            for t in range(na):
                to = pl.ds(t, 1)
                at = t * half + half // 2
                if planes == 2:
                    stage[0, to, :] = outer[ab, s, pl.ds(t * half + row, 1), :]
                else:
                    stage[0, to, :] = outer[ab, s, at : at + 1, :]
                    stage[1, to, :] = outer[ab, s, at - 1 : at, :]
            for k, edge in enumerate(edges):
                edge[ab, s] = stage[k].astype(BF16)
            begin = pl.ds(0, half)
            first[ab, s] = pack([mid[ab, s, begin, :], outer[ab, s, begin, :]])
            last[ab, s] = pack([mid_end[ab, s, ends_end, :], outer[ab, s, end, :]])


def radial_edges_kernel(sizes, plan, copies, half, weights, keep, *refs):
    na, nz, planes = sizes
    n_edges = 1 if planes == 2 else 2
    *edges, first, last, stage = refs[-3 - n_edges :]
    refs = refs[: -3 - n_edges]
    radial_kernel(plan, copies, half, weights, keep, *refs)
    edges_of_state(na, nz, planes, refs[-3], refs[-2], refs[-1], edges, first, last, stage)


def explicit_angle(t, reader, low, high, edge_factors, coef, rows, nz):
    half = nz // 2
    for ab in range(2):
        out = second_step(
            functools.partial(reader, ab),
            lambda s: low[ab, s, pl.ds(t, 1), :] * edge_factors[0],
            lambda s: high[ab, s, pl.ds(t, 1), :] * edge_factors[1],
            coef,
            half,
        )
        width = out[0][0].shape[1]
        for s in range(3):
            rows[s, at_rows(t * nz, nz, nz), ab * width : (ab + 1) * width] = pack(
                [out[0][s], out[1][s]]
            )


def explicit_run(begin, count, states, low, high, edge_factors, coef, rows, nz):
    half = nz // 2

    def one(step, carry):
        t = begin + step

        def reader(ab, k, s, shift):
            state, base = states[k]
            return state[ab, s, at_rows((t - base + shift) * half, half, half), :]

        explicit_angle(t, reader, low, high, edge_factors, coef, rows, nz)
        return carry

    lax.fori_loop(0, count, one, 0)


def finish_run(begin, count, s, rows, weights, keep, result, nz):
    half = nz // 2
    value = rows_product(rows[s, pl.ds(begin * nz, count * nz), :], weights[s])
    for k in range(count):
        t = begin + k
        parts = turned(value[k * nz + half : (k + 1) * nz], value[k * nz : k * nz + half], half)
        for p in range(2):
            span = pl.ds(p * half, half)
            result[s, t, span, LANES:] = parts[p][:, LANES:]
            result[s, t, span, :LANES] = parts[p][:, :LANES] * keep[0, s, t : t + 1, :]


def widen(pairs):
    for source, target in pairs:
        target[...] = source[...].astype(F32)


def early_kernel(sizes, *refs):
    na, nz, runs, base, half_ring, planes = sizes
    if len(refs) == 18:
        refs = refs[1:]
    (weights, keep, mid, outer, before_low, after_low, low_low, high_low, coef, out,
     before, after, low, high, rows, result, out_sems) = refs
    half = nz // 2
    place = lax.rem(lax.axis_index("ang"), half_ring)
    wrap_before = jnp.where(place == 0, 1, 0)
    wrap_after = jnp.where(place == half_ring - 1, 1, 0)
    factors = edge_weights(planes)
    states = ((mid, base), (outer, 0))
    widen(((low_low, low), (high_low, high)))
    for begin, count in runs:
        end = begin + count
        if begin == 0:
            widen(((before_low, before),))

            def reader(ab, k, s, shift):
                if shift == -1:
                    source = jnp.where(wrap_before == 1, 1 - ab, ab)
                    return before[source, s, pl.ds(k * half, half), :]
                return states[k][0][ab, s, pl.ds((shift - states[k][1]) * half, half), :]

            explicit_angle(0, reader, low, high, factors, coef, rows, nz)
        if end == na:
            widen(((after_low, after),))

            def reader(ab, k, s, shift):
                if shift == 1:
                    source = jnp.where(wrap_after == 1, 1 - ab, ab)
                    return after[source, s, pl.ds(k * half, half), :]
                return states[k][0][ab, s, pl.ds((na - 1 + shift - states[k][1]) * half, half), :]

            explicit_angle(na - 1, reader, low, high, factors, coef, rows, nz)
        start, stop = max(begin, 1), min(end, na - 1)
        if stop > start:
            explicit_run(start, stop - start, states, low, high, factors, coef, rows, nz)
    leaves = []
    for s in range(3):
        for k, (begin, count) in enumerate(runs):
            finish_run(begin, count, s, rows, weights, keep, result, nz)
            span = pl.ds(begin, count)
            leave = pltpu.make_async_copy(result.at[s, span], out.at[s, span], out_sems.at[k, s])
            leave.start()
            leaves.append(leave)
    for leave in leaves:
        leave.wait()


def late_kernel(
    sizes, given, state, weights, keep, mine, theirs, outer, low_low, high_low, coef,
    out, mid, low, high, rows, result, out_sems,
):
    na, nz, lo, hi, base, planes = sizes
    half = nz // 2
    factors = edge_weights(planes)
    count = hi - lo
    widen(((low_low, low), (high_low, high)))
    for s in range(3):
        value = both_sides(mine[s], theirs[s], weights[s])
        store_run(mid, s, lo, 2, count, 0, value, keep, half)
        for ab in range(2):
            for k in range(2):
                to = pl.ds((2 + count) * k * half, 2 * half)
                mid[ab, s, to, :] = state[
                    ab, s, pl.ds((lo - 2 - base + (2 + count) * k) * half, 2 * half), :
                ]
    explicit_run(lo - 1, count + 2, ((mid, lo - 2), (outer, 0)), low, high, factors, coef, rows, nz)
    leaves = []
    for s in range(3):
        finish_run(lo - 1, count + 2, s, rows, weights, keep, result, nz)
        span = pl.ds(lo - 1, count + 2)
        leave = pltpu.make_async_copy(result.at[s, span], out.at[s, span], out_sems.at[s])
        leave.start()
        leaves.append(leave)
    for leave in leaves:
        leave.wait()


def ring(count, step):
    half = count // 2
    return [(i, i // half * half + (i % half + step) % half) for i in range(count)]


def plane_halos(edges, planes):
    if planes == 2:
        got = lax.ppermute(edges[0], "ax", [(0, 1), (1, 0)])
        return got, got
    up = [(i, i + 1) for i in range(planes - 1)]
    down = [(i + 1, i) for i in range(planes - 1)]
    return lax.ppermute(edges[1], "ax", up), lax.ppermute(edges[0], "ax", down)


def after(value, done):
    return lax.optimization_barrier((value, done))


def per_device(
    concentration, courant, axial_diffusion, angular_rate, rate_constants, species_map,
    wall_flags, radial_inverse,
):
    ns, na, nz, nr = concentration.shape
    half = nz // 2
    count = lax.axis_size("ang")
    planes = lax.axis_size("ax")
    n_edges = 1 if planes == 2 else 2
    quarter = na // 4
    ends = 2
    side = na // 2
    cut = 7 * na // 16
    first_lo, first_cut, first_hi = ends, ends + na // 4, side
    last_lo, last_hi = na - 3 * ends, na - ends
    opposite = [(i, (i + count // 2) % count) for i in range(count)]

    def dma(*dims):
        return pltpu.SemaphoreType.DMA(dims)

    def message(angles):
        return shape(ns, angles * half, nr, dtype=BF16)

    conc = concentration.reshape(ns, na * nz, nr)
    field = pltpu.VMEM((ns, na * nz, nr), F32)
    *edges, first, last, mid_a, coef = call(
        functools.partial(head_kernel, (na, nz, first_lo, first_cut, planes)),
        [shape(ns, na, nr)] * n_edges
        + [shape(ns, nz, nr)] * 2
        + [
            shape(ns * (first_cut - first_lo) * half + na, nr, dtype=BF16),
            shape(RATE + 3, half, nr),
        ],
        [HBM] * 7,
        [VM] * (n_edges + 4),
        [
            field, pltpu.VMEM((na, LANES), F32), pltpu.VMEM((1, nr), F32), pltpu.VMEM(angular_rate.shape, F32),
            pltpu.SMEM(axial_diffusion.shape, F32), pltpu.SMEM(rate_constants.shape, F32),
            pltpu.SMEM(species_map.shape, jnp.int32), pltpu.SMEM(wall_flags.shape, jnp.int32), dma(9),
        ],
        (conc, courant[None], axial_diffusion, angular_rate, rate_constants, species_map, wall_flags),
        58,
    )
    opp_a = lax.ppermute(mid_a, "ang", opposite)
    low, high = plane_halos(edges, planes)
    angle_before = lax.ppermute(last, "ang", [(i, (i + 1) % count) for i in range(count)])
    angle_after = lax.ppermute(first, "ang", [(i, (i - 1) % count) for i in range(count)])
    mid_b, mid_x, mid_l = call(
        functools.partial(
            inner_kernel,
            (na, nz),
            (
                (0, ((first_cut, first_hi - first_cut),)),
                (1, ((first_hi, last_lo - first_hi),)),
                (2, ((last_lo, last_hi - last_lo),)),
            ),
        ),
        [message(first_hi - first_cut), message(last_lo - first_hi), message(last_hi - last_lo)],
        [ANY, VM],
        [VM] * 3,
        [field, pltpu.SemaphoreType.DMA],
        (conc, coef),
        8,
    )
    opp_b = lax.ppermute(mid_b, "ang", opposite)
    out1, out2 = call(
        functools.partial(frame_kernel, (na, nz, ends, planes)),
        [message(cut - ends), message(na - ends - cut)],
        [ANY] + [VM] * 2 + [ANY],
        [VM] * 2,
        [field, pltpu.VMEM((RATE + 3, half, nr), F32), dma(2)],
        (conc, low, high, coef),
        8,
    )
    out2, opp_a = after(out2, opp_a)
    opp_2 = lax.ppermute(out2, "ang", opposite)
    out1, (opp_b, angle_before, angle_after) = after(out1, (opp_b, angle_before, angle_after))
    opp_1 = lax.ppermute(out1, "ang", opposite)
    out_e = call(
        functools.partial(ends_kernel, (na, nz, planes)),
        message(4 * ends),
        [ANY] * 3 + [VM] * 3,
        VM,
        [pltpu.VMEM((ns, 8 * nz, nr), F32), dma(4)],
        (conc, angle_before, angle_after, low, high, coef),
        8,
    )
    opp_e = lax.ppermute(out_e, "ang", opposite)

    weights, keep = call(
        weights_kernel,
        [shape(ns, nr, 2 * nr, dtype=BF16), shape(2, ns, na, LANES)],
        [ANY, VM, VM],
        [VM] * 2,
        [pltpu.VMEM((ns, nr, nr), BF16), pltpu.VMEM((ns, nr, nr), BF16), dma(2, ns)],
        (radial_inverse, mid_a, opp_a),
        12,
    )

    def state(angles):
        return shape(2, ns, angles * half, nr)

    count_a, count_b = first_cut - first_lo, first_hi - first_cut
    (mid_first,) = call(
        functools.partial(
            radial_kernel,
            (((0, first_lo, 0, count_a),), ((0, first_cut, count_a, count_b),)),
            (),
            half,
        ),
        [state(count_a + count_b)],
        [VM] * 6,
        [VM],
        [],
        (weights, keep, mid_a, mid_b, opp_a, opp_b),
        8,
    )
    opp_1, mid_first = after(opp_1, mid_first)
    mid_x, opp_1 = after(mid_x, opp_1)
    opp_x = lax.ppermute(mid_x, "ang", opposite)
    span = na - 2 * ends
    (outer_first,) = call(
        functools.partial(radial_kernel, (((0, ends, 0, cut - ends),), ((0, cut, cut - ends, na - ends - cut),)), (), half),
        [state(span)],
        [VM] * 6,
        [VM],
        [],
        (weights, keep, out1, out2, opp_1, opp_2),
        8,
    )
    mid_l, opp_e = after(mid_l, opp_e)
    opp_l = lax.ppermute(mid_l, "ang", opposite)
    plan = (
        (
            (2, 0, 0, ends), (2, na - ends, na - ends, ends),
            (0, 0, 0, ends), (1, na - ends, 0, ends),
        ),
    )
    mid_left, ends_right, outer_state, *rest = call(
        functools.partial(
            radial_edges_kernel,
            (na, nz, planes),
            plan,
            ((0, 0, 0, first_lo, count_a + count_b), (1, 0, 2, ends, span)),
            half,
        ),
        [state(side), state(ends), state(na)]
        + [shape(2, ns, na, nr, dtype=BF16)] * n_edges
        + [shape(2, ns, nz, nr, dtype=BF16)] * 2,
        [VM] * 6,
        [VM] * (5 + n_edges),
        [pltpu.VMEM((n_edges, na, nr), F32)],
        (weights, keep, out_e, opp_e, mid_first, outer_first),
        8,
    )
    *edges, first, last = rest
    low, high = plane_halos(edges, planes)
    angle_before = lax.ppermute(last, "ang", ring(count, 1))
    angle_after = lax.ppermute(first, "ang", ring(count, -1))
    stage = [pltpu.VMEM((ns, na * nz, 2 * nr), BF16), pltpu.VMEM((ns, na, nz, nr), F32)]
    edge_scratch = [pltpu.VMEM((2, ns, na, nr), F32)] * 2
    def early(runs, base, mid, given):
        return call(
            functools.partial(early_kernel, (na, nz, runs, base, count // 2, planes)),
            shape(ns, na, nz, nr),
            [ANY] * len(given) + [VM] * 9,
            ANY,
            [pltpu.VMEM((2, ns, nz, nr), F32)] * 2 + edge_scratch + stage + [dma(len(runs), ns)],
            (*given, weights, keep, mid, outer_state, angle_before, angle_after, low, high, coef),
            12,
            {0: 0} if given else None,
        )

    partial = early(((0, first_hi - 1),), 0, mid_left, ())
    opp_x, partial = after(opp_x, partial)
    base = first_hi - 2
    (mid_right,) = call(
        functools.partial(
            radial_kernel,
            (((0, first_hi, 2, last_lo - first_hi),),),
            ((0, base, 0, 0, 2), (1, 0, 0, na - ends - base, ends)),
            half,
        ),
        [state(na - base)],
        [VM] * 6,
        [VM],
        [],
        (weights, keep, mid_x, opp_x, mid_left, ends_right),
        8,
    )

    partial = early(
        ((first_hi - 1, last_lo - first_hi), (na - 1, 1)), base, mid_right, (partial,)
    )
    wide = last_hi - last_lo + 4
    return call(
        functools.partial(late_kernel, (na, nz, last_lo, last_hi, base, planes)),
        shape(ns, na, nz, nr),
        [ANY] + [VM] * 9,
        ANY,
        [pltpu.VMEM((2, ns, wide * half, nr), F32)] + edge_scratch + stage + [dma(ns)],
        (partial, mid_right, weights, keep, mid_l, opp_l, outer_state, low, high, coef),
        12,
        {0: 0},
    )


def solution(mesh):
    in_specs = (P(None, "ang", "ax", None), P(), P(), P(), P(), P(), P(None, "ang"), P())
    out_specs = P(None, "ang", "ax", None)
    return jax.shard_map(
        per_device, mesh=mesh, in_specs=in_specs, out_specs=out_specs, check_vma=False
    )
```

```python
import functools

import jax
import jax.numpy as jnp
from jax import lax
from jax.experimental import pallas as pl
from jax.experimental.pallas import tpu as pltpu
from jax.sharding import PartitionSpec as P

F32 = jnp.float32
BF16 = jnp.bfloat16
MIB = 1024 * 1024
LANES = 128

ANY = pl.BlockSpec(memory_space=pl.ANY)
HBM = pl.BlockSpec(memory_space=pltpu.HBM)
VM = pl.BlockSpec(memory_space=pltpu.VMEM)
SM = pl.BlockSpec(memory_space=pltpu.SMEM)

OWN, BEFORE, ANGULAR, AXIAL, RATE = 0, 3, 6, 9, 12


def call(body, out_shape, in_specs, out_specs, scratch, args, mib, aliases=None):
    return pl.pallas_call(
        body,
        out_shape=out_shape,
        in_specs=in_specs,
        out_specs=out_specs,
        scratch_shapes=scratch,
        input_output_aliases=aliases or {},
        cost_estimate=pl.CostEstimate(flops=1, bytes_accessed=1, transcendentals=0),
        compiler_params=pltpu.CompilerParams(vmem_limit_bytes=mib * MIB),
    )(*args)


def shape(*dims, dtype=F32):
    return jax.ShapeDtypeStruct(dims, dtype)


def transport(now, before, after, around, coef):
    made = (
        coef[RATE] * (now[1] * now[2]),
        coef[RATE + 1] * (now[0] * now[2]),
        coef[RATE + 2] * (now[0] * now[1]),
    )
    spent = made[0] + made[1] + made[2]
    out = []
    for s in range(3):
        value = now[s] * coef[OWN + s] + before[s] * coef[BEFORE + s]
        value = value + after[s] * coef[AXIAL + s] + around[s] * coef[ANGULAR + s]
        out.append(value + ((made[s] + made[s]) - spent))
    return out


def turned(first, second, rows):
    first, second = pltpu.roll(first, rows // 2, 0), pltpu.roll(second, rows // 2, 0)
    upper = lax.broadcasted_iota(jnp.int32, first.shape, 0) < rows // 2
    return jnp.where(upper, first, second), jnp.where(upper, second, first)


def first_step(read, low, high, coef, half):
    tiles = [[read(s, 0, k) for s in range(3)] for k in range(2)]
    around = [[read(s, -1, k) + read(s, 1, k) for s in range(3)] for k in range(2)]
    row = lax.broadcasted_iota(jnp.int32, tiles[0][0].shape, 0)
    top, bottom = row == 0, row == half - 1
    fall = [[pltpu.roll(v, 1, 0) for v in tile] for tile in tiles]
    rise = [[pltpu.roll(v, half - 1, 0) for v in tile] for tile in tiles]
    out = []
    for k in range(2):
        other = 1 - k
        before = [
            jnp.where(top, low(s) if low is not None and k == 0 else fall[other][s], fall[k][s])
            for s in range(3)
        ]
        after = [
            jnp.where(bottom, high(s) if high is not None and k == 1 else rise[other][s], rise[k][s])
            for s in range(3)
        ]
        out.append(transport(tiles[k], before, after, around[k], coef))
    pairs = [turned(out[0][s], out[1][s], half) for s in range(3)]
    return [p[0] for p in pairs], [p[1] for p in pairs]


def second_step(read, low, high, coef, half):
    tiles = [[read(k, s, 0) for s in range(3)] for k in range(2)]
    around = [[read(k, s, -1) + read(k, s, 1) for s in range(3)] for k in range(2)]
    row = lax.broadcasted_iota(jnp.int32, tiles[0][0].shape, 0)
    top, bottom = row == 0, row == half - 1
    first, last = row == half // 2, row == half // 2 - 1
    fall = [[pltpu.roll(v, 1, 0) for v in tile] for tile in tiles]
    rise = [[pltpu.roll(v, half - 1, 0) for v in tile] for tile in tiles]
    out = []
    for k in range(2):
        before = [jnp.where(top, fall[1 - k][s], fall[k][s]) for s in range(3)]
        after = [jnp.where(bottom, rise[1 - k][s], rise[k][s]) for s in range(3)]
        if k == 1:
            before = [jnp.where(first, low(s), before[s]) for s in range(3)]
            after = [jnp.where(last, high(s), after[s]) for s in range(3)]
        out.append(transport(tiles[k], before, after, around[k], coef))
    return out


def pack(tiles):
    return jnp.concatenate(tiles, 0).astype(BF16)


def at_rows(start, count, step):
    return pl.ds(pl.multiple_of(start, step), count)


def field_reader(field, t, nz):
    half = nz // 2
    return lambda s, shift, k: field[s, at_rows((t + shift) * nz + k * half, half, half), :]


def mid_run(field, out_of, begin, count, at, coef, nz):
    half = nz // 2

    def pair(step, carry):
        t = begin + step * 2
        tiles = [first_step(field_reader(field, t + k, nz), None, None, coef, half)[0] for k in range(2)]
        for s in range(3):
            out_of(s)[at_rows(at * half + step * nz, nz, nz), :] = pack([tiles[0][s], tiles[1][s]])
        return carry

    lax.fori_loop(0, count // 2, pair, 0)


def head_kernel(sizes, conc, cour, diff, ang, rate, smap, *rest):
    na, nz, planes = sizes
    edges = rest[: 1 if planes == 2 else 2]
    first, last, coef, field, cour_v, ang_v, diff_s, rate_s, map_s, sems = rest[len(edges) :]
    small = [
        pltpu.make_async_copy(src, dst, sems.at[k + 1])
        for k, (src, dst) in enumerate(
            ((cour, cour_v), (ang, ang_v), (diff, diff_s), (rate, rate_s), (smap, map_s))
        )
    ]
    copies = [pltpu.make_async_copy(conc, field, sems.at[0])]
    for copy in small + copies:
        copy.start()
    for copy in small:
        copy.wait()
    tile = coef.shape[1:]
    for s in range(3):
        courant, angular = cour_v[...], ang_v[s : s + 1, :]
        axial = diff_s[s]
        total = jnp.float32(0.0)
        for k in range(map_s.shape[0]):
            total = total + jnp.where(map_s[k, 2] == s, rate_s[k], 0.0)
        coef[OWN + s] = jnp.broadcast_to((1.0 - 2.0 * axial) - courant - 2.0 * angular, tile)
        coef[BEFORE + s] = jnp.broadcast_to(courant + axial, tile)
        coef[ANGULAR + s] = jnp.broadcast_to(angular, tile)
        coef[AXIAL + s] = jnp.full(tile, axial, F32)
        coef[RATE + s] = jnp.full(tile, total, F32)
    copies[0].wait()
    if planes == 2:
        row = jnp.where(lax.axis_index("ax") == 0, nz - 1, 0)
    for s in range(3):
        first[s] = field[s, pl.ds(0, nz), :]
        last[s] = field[s, pl.ds((na - 1) * nz, nz), :]
        for t in range(na):
            if planes == 2:
                edges[0][s, t : t + 1, :] = field[s, pl.ds(t * nz + row, 1), :]
            else:
                edges[0][s, t : t + 1, :] = field[s, t * nz : t * nz + 1, :]
                edges[1][s, t : t + 1, :] = field[s, (t + 1) * nz - 1 : (t + 1) * nz, :]


def inner_kernel(sizes, runs, conc, coef, flags, *rest):
    na, nz = sizes
    outs, field, flag_v, sem = rest[:-3], rest[-3], rest[-2], rest[-1]
    copy = pltpu.make_async_copy(conc, field, sem)
    copy.start()
    lane = lax.broadcasted_iota(jnp.int32, (1, LANES), 1)
    for t in range(na):
        row = jnp.zeros((1, LANES), jnp.int32)
        for s in range(3):
            row = jnp.where(lane == s, flags[s, t], row)
        flag_v[t : t + 1, :] = row.astype(F32)
    rows = runs[0][1] * nz // 2
    span = pl.ds(3 * rows, na)
    outs[0][span, :] = jnp.zeros((na, outs[0].shape[1]), BF16)
    outs[0][span, :LANES] = flag_v[...].astype(BF16)
    copy.wait()
    for k, (begin, count) in enumerate(runs):
        out = outs[k]
        if k == 0:
            mid_run(field, lambda s: out.at[pl.ds(s * rows, rows)], begin, count, 0, coef, nz)
        else:
            mid_run(field, out.at.__getitem__, begin, count, 0, coef, nz)


def edge_weights(planes):
    if planes != 2:
        return 1.0, 1.0
    place = lax.axis_index("ax")
    return jnp.where(place == 1, 1.0, 0.0), jnp.where(place == 0, 1.0, 0.0)


def frame_kernel(
    sizes, conc, before, after, low, high, coef_in, out1, out2, field, coef, sems
):
    na, nz, ends, planes = sizes
    half = nz // 2
    copies = [
        pltpu.make_async_copy(conc, field.at[:, pl.ds(nz, na * nz)], sems.at[0]),
        pltpu.make_async_copy(before, field.at[:, pl.ds(0, nz)], sems.at[1]),
        pltpu.make_async_copy(after, field.at[:, pl.ds((na + 1) * nz, nz)], sems.at[2]),
        pltpu.make_async_copy(coef_in, coef, sems.at[3]),
    ]
    for copy in copies:
        copy.start()
    low_weight, high_weight = edge_weights(planes)
    for copy in copies:
        copy.wait()

    def angle(t):
        return first_step(
            field_reader(field, t + 1, nz),
            lambda s: low[s, pl.ds(t, 1), :] * low_weight,
            lambda s: high[s, pl.ds(t, 1), :] * high_weight,
            coef,
            half,
        )

    def pair(t, out, row, ends_row):
        tiles = [angle(t), angle(t + 1)]
        for s in range(3):
            out[s, pl.ds(row, nz), :] = pack([tiles[0][1][s], tiles[1][1][s]])
            if ends_row is not None:
                out2[s, pl.ds(ends_row, nz), :] = pack([tiles[0][0][s], tiles[1][0][s]])

    quarter = na // 4
    tail = na // 2 * half
    pair(0, out1, 0, tail)
    pair(na - 2, out2, (na // 2 - 2) * half, tail + nz)

    def first_part(step, carry):
        pair(step * 2, out1, pl.multiple_of(step * nz, nz), None)
        return carry

    def second_part(step, carry):
        pair(na // 2 + step * 2, out2, pl.multiple_of(step * nz, nz), None)
        return carry

    lax.fori_loop(1, quarter, first_part, 0)
    lax.fori_loop(0, quarter - 1, second_part, 0)


def weights_kernel(matrix, mine, theirs, out, keep, left, lower, sems):
    half = out.shape[1]
    copies = []
    for s in range(out.shape[0]):
        for k, ref in enumerate((left, lower)):
            src = matrix.at[s, pl.ds(k * half, half), pl.ds(0, half)]
            copies.append(pltpu.make_async_copy(src, ref.at[s], sems.at[k, s]))
    for copy in copies:
        copy.start()
    na = keep.shape[2]
    lane = lax.broadcasted_iota(jnp.int32, (na, LANES), 1)
    for ab, ref in enumerate((mine, theirs)):
        flags = ref[pl.ds(ref.shape[0] - na, na), :LANES].astype(F32)
        for s in range(out.shape[0]):
            moved = pltpu.roll(flags, LANES - s, 1) if s else flags
            keep[ab, s] = jnp.where(lane == 0, 1.0 - moved, 1.0)
    row = lax.broadcasted_iota(jnp.int32, (half, half), 0)
    col = lax.broadcasted_iota(jnp.int32, (half, half), 1)
    row = jnp.maximum(row, 1)
    pick = jnp.where(col == row, 1.0, 0.0).astype(BF16)
    flip = jnp.where(col == half - 1 - row, 1.0, 0.0).astype(BF16)
    for copy in copies:
        copy.wait()
    for s in range(out.shape[0]):
        out[s, :, :half] = jnp.dot(pick, left[s], preferred_element_type=F32).astype(BF16)
        out[s, :, half:] = jnp.dot(flip, lower[s], preferred_element_type=F32).astype(BF16)


def rows_product(rows, weights):
    return lax.dot_general(rows, weights, (((1,), (1,)), ((), ())), preferred_element_type=F32)


def both_sides(mine, theirs, weights):
    rows = jnp.concatenate(
        [jnp.concatenate([mine, theirs], 1), jnp.concatenate([theirs, mine], 1)], 0
    )
    return rows_product(rows, weights)


def store_run(state, s, begin, place, count, at, value, keep, half):
    total = value.shape[0] // 2
    for ab in range(2):
        part = value[ab * total + at * half : ab * total + (at + count) * half]
        state[ab, s, pl.ds(place * half, count * half), LANES:] = part[:, LANES:]
        for k in range(count):
            state[ab, s, pl.ds((place + k) * half, half), :LANES] = (
                part[k * half : (k + 1) * half, :LANES] * keep[ab, s, begin + k : begin + k + 1, :]
            )


def species_rows(ref, s, runs, half):
    if len(ref.shape) == 3:
        return ref[s]
    rows = sum(run[3] for run in runs) * half
    return ref[pl.ds(s * rows, rows), :]


def radial_kernel(plan, copies, half, weights, keep, *refs):
    n = len(plan)
    mines, theirs, refs = refs[:n], refs[n : 2 * n], refs[2 * n :]
    n_in = 1 + max((part for part, *_ in copies), default=-1)
    parts, states = refs[:n_in], refs[n_in:]
    for s in range(3):
        for k, runs in enumerate(plan):
            value = both_sides(
                species_rows(mines[k], s, runs, half),
                species_rows(theirs[k], s, runs, half),
                weights[s],
            )
            at = 0
            for which, begin, place, count in runs:
                store_run(states[which], s, begin, place, count, at, value, keep, half)
                at += count
    for part, source, which, place, count in copies:
        to, rows = pl.ds(place * half, count * half), pl.ds(source * half, count * half)
        for ab in range(2):
            for s in range(3):
                states[which][ab, s, to, :] = parts[part][ab, s, rows, :]


def edges_of_state(na, nz, planes, mid, mid_end, outer, edges, first, last, stage):
    half = nz // 2
    if planes == 2:
        row = jnp.where(lax.axis_index("ax") == 0, half // 2 - 1, half // 2)
    end = pl.ds((na - 1) * half, half)
    ends_end = pl.ds(mid_end.shape[2] - half, half)
    for ab in range(2):
        for s in range(3):
            for t in range(na):
                to = pl.ds(t, 1)
                at = t * half + half // 2
                if planes == 2:
                    stage[0, to, :] = outer[ab, s, pl.ds(t * half + row, 1), :]
                else:
                    stage[0, to, :] = outer[ab, s, at : at + 1, :]
                    stage[1, to, :] = outer[ab, s, at - 1 : at, :]
            for k, edge in enumerate(edges):
                edge[ab, s] = stage[k].astype(BF16)
            begin = pl.ds(0, half)
            first[ab, s] = pack([mid[ab, s, begin, :], outer[ab, s, begin, :]])
            last[ab, s] = pack([mid_end[ab, s, ends_end, :], outer[ab, s, end, :]])


def radial_edges_kernel(sizes, plan, copies, half, weights, keep, *refs):
    na, nz, planes = sizes
    n_edges = 1 if planes == 2 else 2
    *edges, first, last, stage = refs[-3 - n_edges :]
    refs = refs[: -3 - n_edges]
    radial_kernel(plan, copies, half, weights, keep, *refs)
    edges_of_state(na, nz, planes, refs[-3], refs[-2], refs[-1], edges, first, last, stage)


def explicit_angle(t, reader, low, high, edge_factors, coef, rows, nz):
    half = nz // 2
    for ab in range(2):
        out = second_step(
            functools.partial(reader, ab),
            lambda s: low[ab, s, pl.ds(t, 1), :] * edge_factors[0],
            lambda s: high[ab, s, pl.ds(t, 1), :] * edge_factors[1],
            coef,
            half,
        )
        width = out[0][0].shape[1]
        for s in range(3):
            rows[s, at_rows(t * nz, nz, nz), ab * width : (ab + 1) * width] = pack(
                [out[0][s], out[1][s]]
            )


def explicit_run(begin, count, states, low, high, edge_factors, coef, rows, nz):
    half = nz // 2

    def one(step, carry):
        t = begin + step

        def reader(ab, k, s, shift):
            state, base = states[k]
            return state[ab, s, at_rows((t - base + shift) * half, half, half), :]

        explicit_angle(t, reader, low, high, edge_factors, coef, rows, nz)
        return carry

    lax.fori_loop(0, count, one, 0)


def finish_run(begin, count, s, rows, weights, keep, result, nz):
    half = nz // 2
    value = rows_product(rows[s, pl.ds(begin * nz, count * nz), :], weights[s])
    for k in range(count):
        t = begin + k
        parts = turned(value[k * nz + half : (k + 1) * nz], value[k * nz : k * nz + half], half)
        for p in range(2):
            span = pl.ds(p * half, half)
            result[s, t, span, LANES:] = parts[p][:, LANES:]
            result[s, t, span, :LANES] = parts[p][:, :LANES] * keep[0, s, t : t + 1, :]


def widen(pairs):
    for source, target in pairs:
        target[...] = source[...].astype(F32)


def early_kernel(sizes, *refs):
    na, nz, runs, base, half_ring, planes = sizes
    if len(refs) == 18:
        refs = refs[1:]
    (weights, keep, mid, outer, before_low, after_low, low_low, high_low, coef, out,
     before, after, low, high, rows, result, out_sems) = refs
    half = nz // 2
    place = lax.rem(lax.axis_index("ang"), half_ring)
    wrap_before = jnp.where(place == 0, 1, 0)
    wrap_after = jnp.where(place == half_ring - 1, 1, 0)
    factors = edge_weights(planes)
    states = ((mid, base), (outer, 0))
    widen(((low_low, low), (high_low, high)))
    for begin, count in runs:
        end = begin + count
        if begin == 0:
            widen(((before_low, before),))

            def reader(ab, k, s, shift):
                if shift == -1:
                    source = jnp.where(wrap_before == 1, 1 - ab, ab)
                    return before[source, s, pl.ds(k * half, half), :]
                return states[k][0][ab, s, pl.ds((shift - states[k][1]) * half, half), :]

            explicit_angle(0, reader, low, high, factors, coef, rows, nz)
        if end == na:
            widen(((after_low, after),))

            def reader(ab, k, s, shift):
                if shift == 1:
                    source = jnp.where(wrap_after == 1, 1 - ab, ab)
                    return after[source, s, pl.ds(k * half, half), :]
                return states[k][0][ab, s, pl.ds((na - 1 + shift - states[k][1]) * half, half), :]

            explicit_angle(na - 1, reader, low, high, factors, coef, rows, nz)
        start, stop = max(begin, 1), min(end, na - 1)
        if stop > start:
            explicit_run(start, stop - start, states, low, high, factors, coef, rows, nz)
    leaves = []
    for s in range(3):
        for k, (begin, count) in enumerate(runs):
            finish_run(begin, count, s, rows, weights, keep, result, nz)
            span = pl.ds(begin, count)
            leave = pltpu.make_async_copy(result.at[s, span], out.at[s, span], out_sems.at[k, s])
            leave.start()
            leaves.append(leave)
    for leave in leaves:
        leave.wait()


def late_kernel(
    sizes, given, state, weights, keep, mine, theirs, outer, low_low, high_low, coef,
    out, mid, low, high, rows, result, out_sems,
):
    na, nz, lo, hi, base, planes = sizes
    half = nz // 2
    factors = edge_weights(planes)
    count = hi - lo
    widen(((low_low, low), (high_low, high)))
    for s in range(3):
        value = both_sides(mine[s], theirs[s], weights[s])
        store_run(mid, s, lo, 2, count, 0, value, keep, half)
        for ab in range(2):
            for k in range(2):
                to = pl.ds((2 + count) * k * half, 2 * half)
                mid[ab, s, to, :] = state[
                    ab, s, pl.ds((lo - 2 - base + (2 + count) * k) * half, 2 * half), :
                ]
    explicit_run(lo - 1, count + 2, ((mid, lo - 2), (outer, 0)), low, high, factors, coef, rows, nz)
    leaves = []
    for s in range(3):
        finish_run(lo - 1, count + 2, s, rows, weights, keep, result, nz)
        span = pl.ds(lo - 1, count + 2)
        leave = pltpu.make_async_copy(result.at[s, span], out.at[s, span], out_sems.at[s])
        leave.start()
        leaves.append(leave)
    for leave in leaves:
        leave.wait()


def ring(count, step):
    half = count // 2
    return [(i, i // half * half + (i % half + step) % half) for i in range(count)]


def plane_halos(edges, planes):
    if planes == 2:
        got = lax.ppermute(edges[0], "ax", [(0, 1), (1, 0)])
        return got, got
    up = [(i, i + 1) for i in range(planes - 1)]
    down = [(i + 1, i) for i in range(planes - 1)]
    return lax.ppermute(edges[1], "ax", up), lax.ppermute(edges[0], "ax", down)


def after(value, done):
    return lax.optimization_barrier((value, done))


def per_device(
    concentration, courant, axial_diffusion, angular_rate, rate_constants, species_map,
    wall_flags, radial_inverse,
):
    ns, na, nz, nr = concentration.shape
    half = nz // 2
    count = lax.axis_size("ang")
    planes = lax.axis_size("ax")
    n_edges = 1 if planes == 2 else 2
    quarter = na // 4
    ends = 2
    side = na // 2
    first_lo, first_cut, first_hi = ends, ends + na // 4, side
    last_lo, last_hi = na - 3 * ends, na - ends
    opposite = [(i, (i + count // 2) % count) for i in range(count)]

    def dma(*dims):
        return pltpu.SemaphoreType.DMA(dims)

    def message(angles):
        return shape(ns, angles * half, nr, dtype=BF16)

    conc = concentration.reshape(ns, na * nz, nr)
    field = pltpu.VMEM((ns, na * nz, nr), F32)
    *edges, first, last, coef = call(
        functools.partial(head_kernel, (na, nz, planes)),
        [shape(ns, na, nr)] * n_edges + [shape(ns, nz, nr)] * 2 + [shape(RATE + 3, half, nr)],
        [HBM] * 6,
        [VM] * (n_edges + 3),
        [
            field, pltpu.VMEM((1, nr), F32), pltpu.VMEM(angular_rate.shape, F32),
            pltpu.SMEM(axial_diffusion.shape, F32), pltpu.SMEM(rate_constants.shape, F32),
            pltpu.SMEM(species_map.shape, jnp.int32), dma(6),
        ],
        (conc, courant[None], axial_diffusion, angular_rate, rate_constants, species_map),
        58,
    )
    low, high = plane_halos(edges, planes)
    angle_before = lax.ppermute(last, "ang", [(i, (i + 1) % count) for i in range(count)])
    angle_after = lax.ppermute(first, "ang", [(i, (i - 1) % count) for i in range(count)])

    mid_a, mid_b, mid_x, mid_l = call(
        functools.partial(
            inner_kernel,
            (na, nz),
            (
                (first_lo, first_cut - first_lo),
                (first_cut, first_hi - first_cut),
                (first_hi, last_lo - first_hi),
                (last_lo, last_hi - last_lo),
            ),
        ),
        [
            shape(ns * (first_cut - first_lo) * half + na, nr, dtype=BF16),
            message(first_hi - first_cut), message(last_lo - first_hi), message(last_hi - last_lo),
        ],
        [ANY, VM, SM],
        [VM] * 4,
        [field, pltpu.VMEM((na, LANES), F32), pltpu.SemaphoreType.DMA],
        (conc, coef, wall_flags),
        8,
    )
    (mid_a, mid_b), (angle_before, angle_after) = after((mid_a, mid_b), (angle_before, angle_after))
    opp_a = lax.ppermute(mid_a, "ang", opposite)
    opp_b = lax.ppermute(mid_b, "ang", opposite)
    out1, out2 = call(
        functools.partial(frame_kernel, (na, nz, ends, planes)),
        [message(na // 2), message(na // 2 + 2 * ends)],
        [ANY] * 3 + [VM] * 2 + [ANY],
        [VM] * 2,
        [pltpu.VMEM((ns, (na + 2) * nz, nr), F32), pltpu.VMEM((RATE + 3, half, nr), F32), dma(4)],
        (conc, angle_before, angle_after, low, high, coef),
        8,
    )
    out2, opp_a = after(out2, opp_a)
    opp_2 = lax.ppermute(out2, "ang", opposite)
    out1, opp_b = after(out1, opp_b)
    opp_1 = lax.ppermute(out1, "ang", opposite)

    weights, keep = call(
        weights_kernel,
        [shape(ns, nr, 2 * nr, dtype=BF16), shape(2, ns, na, LANES)],
        [ANY, VM, VM],
        [VM] * 2,
        [pltpu.VMEM((ns, nr, nr), BF16), pltpu.VMEM((ns, nr, nr), BF16), dma(2, ns)],
        (radial_inverse, mid_a, opp_a),
        12,
    )

    def state(angles):
        return shape(2, ns, angles * half, nr)

    count_a, count_b = first_cut - first_lo, first_hi - first_cut
    (mid_first,) = call(
        functools.partial(
            radial_kernel,
            (((0, first_lo, 0, count_a),), ((0, first_cut, count_a, count_b),)),
            (),
            half,
        ),
        [state(count_a + count_b)],
        [VM] * 6,
        [VM],
        [],
        (weights, keep, mid_a, mid_b, opp_a, opp_b),
        8,
    )
    opp_1, mid_first = after(opp_1, mid_first)
    mid_x, opp_1 = after(mid_x, opp_1)
    opp_x = lax.ppermute(mid_x, "ang", opposite)
    (outer_first,) = call(
        functools.partial(radial_kernel, (((0, 0, 0, side),),), (), half),
        [state(side)],
        [VM] * 4,
        [VM],
        [],
        (weights, keep, out1, opp_1),
        8,
    )
    mid_l, opp_2 = after(mid_l, opp_2)
    opp_l = lax.ppermute(mid_l, "ang", opposite)
    plan = (((2, side, side, side), (0, 0, 0, ends), (1, na - ends, 0, ends)),)
    mid_left, ends_right, outer_state, *rest = call(
        functools.partial(
            radial_edges_kernel,
            (na, nz, planes),
            plan,
            ((0, 0, 0, first_lo, count_a + count_b), (1, 0, 2, 0, side)),
            half,
        ),
        [state(side), state(ends), state(na)]
        + [shape(2, ns, na, nr, dtype=BF16)] * n_edges
        + [shape(2, ns, nz, nr, dtype=BF16)] * 2,
        [VM] * 6,
        [VM] * (5 + n_edges),
        [pltpu.VMEM((n_edges, na, nr), F32)],
        (weights, keep, out2, opp_2, mid_first, outer_first),
        8,
    )
    *edges, first, last = rest
    low, high = plane_halos(edges, planes)
    angle_before = lax.ppermute(last, "ang", ring(count, 1))
    angle_after = lax.ppermute(first, "ang", ring(count, -1))
    stage = [pltpu.VMEM((ns, na * nz, 2 * nr), BF16), pltpu.VMEM((ns, na, nz, nr), F32)]
    edge_scratch = [pltpu.VMEM((2, ns, na, nr), F32)] * 2
    def early(runs, base, mid, given):
        return call(
            functools.partial(early_kernel, (na, nz, runs, base, count // 2, planes)),
            shape(ns, na, nz, nr),
            [ANY] * len(given) + [VM] * 9,
            ANY,
            [pltpu.VMEM((2, ns, nz, nr), F32)] * 2 + edge_scratch + stage + [dma(len(runs), ns)],
            (*given, weights, keep, mid, outer_state, angle_before, angle_after, low, high, coef),
            12,
            {0: 0} if given else None,
        )

    partial = early(((0, first_hi - 1),), 0, mid_left, ())
    opp_x, partial = after(opp_x, partial)
    base = first_hi - 2
    (mid_right,) = call(
        functools.partial(
            radial_kernel,
            (((0, first_hi, 2, last_lo - first_hi),),),
            ((0, base, 0, 0, 2), (1, 0, 0, na - ends - base, ends)),
            half,
        ),
        [state(na - base)],
        [VM] * 6,
        [VM],
        [],
        (weights, keep, mid_x, opp_x, mid_left, ends_right),
        8,
    )

    partial = early(
        ((first_hi - 1, last_lo - first_hi), (na - 1, 1)), base, mid_right, (partial,)
    )
    wide = last_hi - last_lo + 4
    return call(
        functools.partial(late_kernel, (na, nz, last_lo, last_hi, base, planes)),
        shape(ns, na, nz, nr),
        [ANY] + [VM] * 9,
        ANY,
        [pltpu.VMEM((2, ns, wide * half, nr), F32)] + edge_scratch + stage + [dma(ns)],
        (partial, mid_right, weights, keep, mid_l, opp_l, outer_state, low, high, coef),
        12,
        {0: 0},
    )


def solution(mesh):
    in_specs = (P(None, "ang", "ax", None), P(), P(), P(), P(), P(), P(None, "ang"), P())
    out_specs = P(None, "ang", "ax", None)
    return jax.shard_map(
        per_device, mesh=mesh, in_specs=in_specs, out_specs=out_specs, check_vma=False
    )
```

```python
import functools

import jax
import jax.numpy as jnp
from jax import lax
from jax.experimental import pallas as pl
from jax.experimental.pallas import tpu as pltpu
from jax.sharding import PartitionSpec as P

F32 = jnp.float32
BF16 = jnp.bfloat16
MIB = 1024 * 1024
LANES = 128

ANY = pl.BlockSpec(memory_space=pl.ANY)
HBM = pl.BlockSpec(memory_space=pltpu.HBM)
VM = pl.BlockSpec(memory_space=pltpu.VMEM)
SM = pl.BlockSpec(memory_space=pltpu.SMEM)

OWN, BEFORE, ANGULAR, AXIAL, RATE = 0, 3, 6, 9, 12


def call(body, out_shape, in_specs, out_specs, scratch, args, mib, aliases=None):
    return pl.pallas_call(
        body,
        out_shape=out_shape,
        in_specs=in_specs,
        out_specs=out_specs,
        scratch_shapes=scratch,
        input_output_aliases=aliases or {},
        cost_estimate=pl.CostEstimate(flops=1, bytes_accessed=1, transcendentals=0),
        compiler_params=pltpu.CompilerParams(vmem_limit_bytes=mib * MIB),
    )(*args)


def shape(*dims, dtype=F32):
    return jax.ShapeDtypeStruct(dims, dtype)


def transport(now, before, after, around, coef):
    made = (
        coef[RATE] * (now[1] * now[2]),
        coef[RATE + 1] * (now[0] * now[2]),
        coef[RATE + 2] * (now[0] * now[1]),
    )
    spent = made[0] + made[1] + made[2]
    out = []
    for s in range(3):
        value = now[s] * coef[OWN + s] + before[s] * coef[BEFORE + s]
        value = value + after[s] * coef[AXIAL + s] + around[s] * coef[ANGULAR + s]
        out.append(value + ((made[s] + made[s]) - spent))
    return out


def turned(first, second, rows):
    first, second = pltpu.roll(first, rows // 2, 0), pltpu.roll(second, rows // 2, 0)
    upper = lax.broadcasted_iota(jnp.int32, first.shape, 0) < rows // 2
    return jnp.where(upper, first, second), jnp.where(upper, second, first)


def first_step(read, low, high, coef, half):
    tiles = [[read(s, 0, k) for s in range(3)] for k in range(2)]
    around = [[read(s, -1, k) + read(s, 1, k) for s in range(3)] for k in range(2)]
    row = lax.broadcasted_iota(jnp.int32, tiles[0][0].shape, 0)
    top, bottom = row == 0, row == half - 1
    fall = [[pltpu.roll(v, 1, 0) for v in tile] for tile in tiles]
    rise = [[pltpu.roll(v, half - 1, 0) for v in tile] for tile in tiles]
    out = []
    for k in range(2):
        other = 1 - k
        before = [
            jnp.where(top, low(s) if low is not None and k == 0 else fall[other][s], fall[k][s])
            for s in range(3)
        ]
        after = [
            jnp.where(bottom, high(s) if high is not None and k == 1 else rise[other][s], rise[k][s])
            for s in range(3)
        ]
        out.append(transport(tiles[k], before, after, around[k], coef))
    pairs = [turned(out[0][s], out[1][s], half) for s in range(3)]
    return [p[0] for p in pairs], [p[1] for p in pairs]


def second_step(read, low, high, coef, half):
    tiles = [[read(k, s, 0) for s in range(3)] for k in range(2)]
    around = [[read(k, s, -1) + read(k, s, 1) for s in range(3)] for k in range(2)]
    row = lax.broadcasted_iota(jnp.int32, tiles[0][0].shape, 0)
    top, bottom = row == 0, row == half - 1
    first, last = row == half // 2, row == half // 2 - 1
    fall = [[pltpu.roll(v, 1, 0) for v in tile] for tile in tiles]
    rise = [[pltpu.roll(v, half - 1, 0) for v in tile] for tile in tiles]
    out = []
    for k in range(2):
        before = [jnp.where(top, fall[1 - k][s], fall[k][s]) for s in range(3)]
        after = [jnp.where(bottom, rise[1 - k][s], rise[k][s]) for s in range(3)]
        if k == 1:
            before = [jnp.where(first, low(s), before[s]) for s in range(3)]
            after = [jnp.where(last, high(s), after[s]) for s in range(3)]
        out.append(transport(tiles[k], before, after, around[k], coef))
    return out


def pack(tiles):
    return jnp.concatenate(tiles, 0).astype(BF16)


def at_rows(start, count, step):
    return pl.ds(pl.multiple_of(start, step), count)


def field_reader(field, t, nz):
    half = nz // 2
    return lambda s, shift, k: field[s, at_rows((t + shift) * nz + k * half, half, half), :]


def mid_run(field, out_of, begin, count, at, coef, nz):
    half = nz // 2

    def pair(step, carry):
        t = begin + step * 2
        tiles = [first_step(field_reader(field, t + k, nz), None, None, coef, half)[0] for k in range(2)]
        for s in range(3):
            out_of(s)[at_rows(at * half + step * nz, nz, nz), :] = pack([tiles[0][s], tiles[1][s]])
        return carry

    lax.fori_loop(0, count // 2, pair, 0)


def head_kernel(sizes, conc, cour, diff, ang, rate, smap, flags, *rest):
    na, nz, lo, hi, planes = sizes
    edges = rest[: 1 if planes == 2 else 2]
    mid, coef, field, flag_v, cour_v, ang_v, diff_s, rate_s, map_s, flags_s, sems = rest[
        len(edges) :
    ]
    half = nz // 2
    inner = pl.ds((lo - 1) * nz, (hi - lo + 2) * nz)
    left = pl.ds(0, (lo - 1) * nz)
    right = pl.ds((hi + 1) * nz, (na - hi - 1) * nz)
    small = [
        pltpu.make_async_copy(src, dst, sems.at[k + 3])
        for k, (src, dst) in enumerate(
            ((cour, cour_v), (ang, ang_v), (diff, diff_s), (rate, rate_s), (smap, map_s), (flags, flags_s))
        )
    ]
    copies = [
        pltpu.make_async_copy(conc.at[:, rows], field.at[:, rows], sems.at[k])
        for k, rows in enumerate((inner, left, right))
    ]
    for copy in small + copies:
        copy.start()
    for copy in small:
        copy.wait()
    tile = coef.shape[1:]
    for s in range(3):
        courant, angular = cour_v[...], ang_v[s : s + 1, :]
        axial = diff_s[s]
        total = jnp.float32(0.0)
        for k in range(map_s.shape[0]):
            total = total + jnp.where(map_s[k, 2] == s, rate_s[k], 0.0)
        coef[OWN + s] = jnp.broadcast_to((1.0 - 2.0 * axial) - courant - 2.0 * angular, tile)
        coef[BEFORE + s] = jnp.broadcast_to(courant + axial, tile)
        coef[ANGULAR + s] = jnp.broadcast_to(angular, tile)
        coef[AXIAL + s] = jnp.full(tile, axial, F32)
        coef[RATE + s] = jnp.full(tile, total, F32)
    lane = lax.broadcasted_iota(jnp.int32, (1, LANES), 1)
    for t in range(na):
        row = jnp.zeros((1, LANES), jnp.int32)
        for s in range(3):
            row = jnp.where(lane == s, flags_s[s, t], row)
        flag_v[t : t + 1, :] = row.astype(F32)
    rows = (hi - lo) * half
    span = pl.ds(3 * rows, na)
    mid[span, :] = jnp.zeros((na, mid.shape[1]), BF16)
    mid[span, :LANES] = flag_v[...].astype(BF16)
    copies[0].wait()
    mid_run(field, lambda s: mid.at[pl.ds(s * rows, rows)], lo, hi - lo, 0, coef, nz)
    copies[1].wait()
    copies[2].wait()
    for s in range(3):
        if planes == 2:
            row = jnp.where(lax.axis_index("ax") == 0, nz - 1, 0)
            for t in range(na):
                edges[0][s, t : t + 1, :] = field[s, pl.ds(t * nz + row, 1), :]
        else:
            for t in range(na):
                edges[0][s, t : t + 1, :] = field[s, t * nz : t * nz + 1, :]
                edges[1][s, t : t + 1, :] = field[s, (t + 1) * nz - 1 : (t + 1) * nz, :]


def inner_kernel(sizes, runs, conc, coef, *rest):
    na, nz = sizes
    outs, field, sem = rest[:-2], rest[-2], rest[-1]
    copy = pltpu.make_async_copy(conc, field, sem)
    copy.start()
    copy.wait()
    for out, parts in runs:
        at = 0
        for begin, count in parts:
            mid_run(field, outs[out].at.__getitem__, begin, count, at, coef, nz)
            at += count


def edge_weights(planes):
    if planes != 2:
        return 1.0, 1.0
    place = lax.axis_index("ax")
    return jnp.where(place == 1, 1.0, 0.0), jnp.where(place == 0, 1.0, 0.0)


def frame_kernel(
    sizes, conc, before, after, low, high, coef_in, out1, out2, field, coef, sems
):
    na, nz, ends, planes = sizes
    half = nz // 2
    copies = [
        pltpu.make_async_copy(conc, field.at[:, pl.ds(nz, na * nz)], sems.at[0]),
        pltpu.make_async_copy(before, field.at[:, pl.ds(0, nz)], sems.at[1]),
        pltpu.make_async_copy(after, field.at[:, pl.ds((na + 1) * nz, nz)], sems.at[2]),
        pltpu.make_async_copy(coef_in, coef, sems.at[3]),
    ]
    for copy in copies:
        copy.start()
    low_weight, high_weight = edge_weights(planes)
    for copy in copies:
        copy.wait()

    def angle(t):
        return first_step(
            field_reader(field, t + 1, nz),
            lambda s: low[s, pl.ds(t, 1), :] * low_weight,
            lambda s: high[s, pl.ds(t, 1), :] * high_weight,
            coef,
            half,
        )

    def pair(t, out, row, ends_row):
        tiles = [angle(t), angle(t + 1)]
        for s in range(3):
            out[s, pl.ds(row, nz), :] = pack([tiles[0][1][s], tiles[1][1][s]])
            if ends_row is not None:
                out2[s, pl.ds(ends_row, nz), :] = pack([tiles[0][0][s], tiles[1][0][s]])

    quarter = na // 4
    tail = na // 2 * half
    pair(0, out1, 0, tail)
    pair(na - 2, out2, (na // 2 - 2) * half, tail + nz)

    def first_part(step, carry):
        pair(step * 2, out1, pl.multiple_of(step * nz, nz), None)
        return carry

    def second_part(step, carry):
        pair(na // 2 + step * 2, out2, pl.multiple_of(step * nz, nz), None)
        return carry

    lax.fori_loop(1, quarter, first_part, 0)
    lax.fori_loop(0, quarter - 1, second_part, 0)


def weights_kernel(matrix, mine, theirs, out, keep, left, lower, sems):
    half = out.shape[1]
    copies = []
    for s in range(out.shape[0]):
        for k, ref in enumerate((left, lower)):
            src = matrix.at[s, pl.ds(k * half, half), pl.ds(0, half)]
            copies.append(pltpu.make_async_copy(src, ref.at[s], sems.at[k, s]))
    for copy in copies:
        copy.start()
    na = keep.shape[2]
    lane = lax.broadcasted_iota(jnp.int32, (na, LANES), 1)
    for ab, ref in enumerate((mine, theirs)):
        flags = ref[pl.ds(ref.shape[0] - na, na), :LANES].astype(F32)
        for s in range(out.shape[0]):
            moved = pltpu.roll(flags, LANES - s, 1) if s else flags
            keep[ab, s] = jnp.where(lane == 0, 1.0 - moved, 1.0)
    row = lax.broadcasted_iota(jnp.int32, (half, half), 0)
    col = lax.broadcasted_iota(jnp.int32, (half, half), 1)
    row = jnp.maximum(row, 1)
    pick = jnp.where(col == row, 1.0, 0.0).astype(BF16)
    flip = jnp.where(col == half - 1 - row, 1.0, 0.0).astype(BF16)
    for copy in copies:
        copy.wait()
    for s in range(out.shape[0]):
        out[s, :, :half] = jnp.dot(pick, left[s], preferred_element_type=F32).astype(BF16)
        out[s, :, half:] = jnp.dot(flip, lower[s], preferred_element_type=F32).astype(BF16)


def rows_product(rows, weights):
    return lax.dot_general(rows, weights, (((1,), (1,)), ((), ())), preferred_element_type=F32)


def both_sides(mine, theirs, weights):
    rows = jnp.concatenate(
        [jnp.concatenate([mine, theirs], 1), jnp.concatenate([theirs, mine], 1)], 0
    )
    return rows_product(rows, weights)


def store_run(state, s, begin, place, count, at, value, keep, half):
    total = value.shape[0] // 2
    for ab in range(2):
        part = value[ab * total + at * half : ab * total + (at + count) * half]
        state[ab, s, pl.ds(place * half, count * half), LANES:] = part[:, LANES:]
        for k in range(count):
            state[ab, s, pl.ds((place + k) * half, half), :LANES] = (
                part[k * half : (k + 1) * half, :LANES] * keep[ab, s, begin + k : begin + k + 1, :]
            )


def species_rows(ref, s, runs, half):
    if len(ref.shape) == 3:
        return ref[s]
    rows = sum(run[3] for run in runs) * half
    return ref[pl.ds(s * rows, rows), :]


def radial_kernel(plan, copies, half, weights, keep, *refs):
    n = len(plan)
    mines, theirs, refs = refs[:n], refs[n : 2 * n], refs[2 * n :]
    n_in = 1 + max((part for part, *_ in copies), default=-1)
    parts, states = refs[:n_in], refs[n_in:]
    for s in range(3):
        for k, runs in enumerate(plan):
            value = both_sides(
                species_rows(mines[k], s, runs, half),
                species_rows(theirs[k], s, runs, half),
                weights[s],
            )
            at = 0
            for which, begin, place, count in runs:
                store_run(states[which], s, begin, place, count, at, value, keep, half)
                at += count
    for part, source, which, place, count in copies:
        to, rows = pl.ds(place * half, count * half), pl.ds(source * half, count * half)
        for ab in range(2):
            for s in range(3):
                states[which][ab, s, to, :] = parts[part][ab, s, rows, :]


def edges_of_state(na, nz, planes, mid, mid_end, outer, edges, first, last, stage):
    half = nz // 2
    if planes == 2:
        row = jnp.where(lax.axis_index("ax") == 0, half // 2 - 1, half // 2)
    end = pl.ds((na - 1) * half, half)
    ends_end = pl.ds(mid_end.shape[2] - half, half)
    for ab in range(2):
        for s in range(3):
            for t in range(na):
                to = pl.ds(t, 1)
                at = t * half + half // 2
                if planes == 2:
                    stage[0, to, :] = outer[ab, s, pl.ds(t * half + row, 1), :]
                else:
                    stage[0, to, :] = outer[ab, s, at : at + 1, :]
                    stage[1, to, :] = outer[ab, s, at - 1 : at, :]
            for k, edge in enumerate(edges):
                edge[ab, s] = stage[k].astype(BF16)
            begin = pl.ds(0, half)
            first[ab, s] = pack([mid[ab, s, begin, :], outer[ab, s, begin, :]])
            last[ab, s] = pack([mid_end[ab, s, ends_end, :], outer[ab, s, end, :]])


def radial_edges_kernel(sizes, plan, copies, half, weights, keep, *refs):
    na, nz, planes = sizes
    n_edges = 1 if planes == 2 else 2
    *edges, first, last, stage = refs[-3 - n_edges :]
    refs = refs[: -3 - n_edges]
    radial_kernel(plan, copies, half, weights, keep, *refs)
    edges_of_state(na, nz, planes, refs[-3], refs[-2], refs[-1], edges, first, last, stage)


def explicit_angle(t, reader, low, high, edge_factors, coef, rows, nz):
    half = nz // 2
    for ab in range(2):
        out = second_step(
            functools.partial(reader, ab),
            lambda s: low[ab, s, pl.ds(t, 1), :] * edge_factors[0],
            lambda s: high[ab, s, pl.ds(t, 1), :] * edge_factors[1],
            coef,
            half,
        )
        width = out[0][0].shape[1]
        for s in range(3):
            rows[s, at_rows(t * nz, nz, nz), ab * width : (ab + 1) * width] = pack(
                [out[0][s], out[1][s]]
            )


def explicit_run(begin, count, states, low, high, edge_factors, coef, rows, nz):
    half = nz // 2

    def one(step, carry):
        t = begin + step

        def reader(ab, k, s, shift):
            state, base = states[k]
            return state[ab, s, at_rows((t - base + shift) * half, half, half), :]

        explicit_angle(t, reader, low, high, edge_factors, coef, rows, nz)
        return carry

    lax.fori_loop(0, count, one, 0)


def finish_run(begin, count, s, rows, weights, keep, result, nz):
    half = nz // 2
    value = rows_product(rows[s, pl.ds(begin * nz, count * nz), :], weights[s])
    for k in range(count):
        t = begin + k
        parts = turned(value[k * nz + half : (k + 1) * nz], value[k * nz : k * nz + half], half)
        for p in range(2):
            span = pl.ds(p * half, half)
            result[s, t, span, LANES:] = parts[p][:, LANES:]
            result[s, t, span, :LANES] = parts[p][:, :LANES] * keep[0, s, t : t + 1, :]


def widen(pairs):
    for source, target in pairs:
        target[...] = source[...].astype(F32)


def early_kernel(sizes, *refs):
    na, nz, runs, base, half_ring, planes = sizes
    if len(refs) == 18:
        refs = refs[1:]
    (weights, keep, mid, outer, before_low, after_low, low_low, high_low, coef, out,
     before, after, low, high, rows, result, out_sems) = refs
    half = nz // 2
    place = lax.rem(lax.axis_index("ang"), half_ring)
    wrap_before = jnp.where(place == 0, 1, 0)
    wrap_after = jnp.where(place == half_ring - 1, 1, 0)
    factors = edge_weights(planes)
    states = ((mid, base), (outer, 0))
    widen(((low_low, low), (high_low, high)))
    for begin, count in runs:
        end = begin + count
        if begin == 0:
            widen(((before_low, before),))

            def reader(ab, k, s, shift):
                if shift == -1:
                    source = jnp.where(wrap_before == 1, 1 - ab, ab)
                    return before[source, s, pl.ds(k * half, half), :]
                return states[k][0][ab, s, pl.ds((shift - states[k][1]) * half, half), :]

            explicit_angle(0, reader, low, high, factors, coef, rows, nz)
        if end == na:
            widen(((after_low, after),))

            def reader(ab, k, s, shift):
                if shift == 1:
                    source = jnp.where(wrap_after == 1, 1 - ab, ab)
                    return after[source, s, pl.ds(k * half, half), :]
                return states[k][0][ab, s, pl.ds((na - 1 + shift - states[k][1]) * half, half), :]

            explicit_angle(na - 1, reader, low, high, factors, coef, rows, nz)
        start, stop = max(begin, 1), min(end, na - 1)
        if stop > start:
            explicit_run(start, stop - start, states, low, high, factors, coef, rows, nz)
    leaves = []
    for s in range(3):
        for k, (begin, count) in enumerate(runs):
            finish_run(begin, count, s, rows, weights, keep, result, nz)
            span = pl.ds(begin, count)
            leave = pltpu.make_async_copy(result.at[s, span], out.at[s, span], out_sems.at[k, s])
            leave.start()
            leaves.append(leave)
    for leave in leaves:
        leave.wait()


def late_kernel(
    sizes, given, state, weights, keep, mine, theirs, outer, low_low, high_low, coef,
    out, mid, low, high, rows, result, out_sems,
):
    na, nz, lo, hi, base, planes = sizes
    half = nz // 2
    factors = edge_weights(planes)
    count = hi - lo
    widen(((low_low, low), (high_low, high)))
    for s in range(3):
        value = both_sides(mine[s], theirs[s], weights[s])
        store_run(mid, s, lo, 2, count, 0, value, keep, half)
        for ab in range(2):
            for k in range(2):
                to = pl.ds((2 + count) * k * half, 2 * half)
                mid[ab, s, to, :] = state[
                    ab, s, pl.ds((lo - 2 - base + (2 + count) * k) * half, 2 * half), :
                ]
    explicit_run(lo - 1, count + 2, ((mid, lo - 2), (outer, 0)), low, high, factors, coef, rows, nz)
    leaves = []
    for s in range(3):
        finish_run(lo - 1, count + 2, s, rows, weights, keep, result, nz)
        span = pl.ds(lo - 1, count + 2)
        leave = pltpu.make_async_copy(result.at[s, span], out.at[s, span], out_sems.at[s])
        leave.start()
        leaves.append(leave)
    for leave in leaves:
        leave.wait()


def ring(count, step):
    half = count // 2
    return [(i, i // half * half + (i % half + step) % half) for i in range(count)]


def plane_halos(edges, planes):
    if planes == 2:
        got = lax.ppermute(edges[0], "ax", [(0, 1), (1, 0)])
        return got, got
    up = [(i, i + 1) for i in range(planes - 1)]
    down = [(i + 1, i) for i in range(planes - 1)]
    return lax.ppermute(edges[1], "ax", up), lax.ppermute(edges[0], "ax", down)


def after(value, done):
    return lax.optimization_barrier((value, done))


def per_device(
    concentration, courant, axial_diffusion, angular_rate, rate_constants, species_map,
    wall_flags, radial_inverse,
):
    ns, na, nz, nr = concentration.shape
    half = nz // 2
    count = lax.axis_size("ang")
    planes = lax.axis_size("ax")
    n_edges = 1 if planes == 2 else 2
    quarter = na // 4
    ends = 2
    side = na // 2
    a_lo, a_cut, a_hi = ends, na // 4, 3 * na // 8
    x_hi, y_hi, l_hi = 22 * na // 32, 26 * na // 32, na - ends
    opposite = [(i, (i + count // 2) % count) for i in range(count)]

    def dma(*dims):
        return pltpu.SemaphoreType.DMA(dims)

    def message(angles):
        return shape(ns, angles * half, nr, dtype=BF16)

    angle_before = lax.ppermute(
        concentration[:, na - 1], "ang", [(i, (i + 1) % count) for i in range(count)]
    )
    angle_after = lax.ppermute(
        concentration[:, 0], "ang", [(i, (i - 1) % count) for i in range(count)]
    )
    conc = concentration.reshape(ns, na * nz, nr)
    field = pltpu.VMEM((ns, na * nz, nr), F32)
    *edges, mid_a, coef = call(
        functools.partial(head_kernel, (na, nz, a_lo, a_cut, planes)),
        [shape(ns, na, nr)] * n_edges
        + [
            shape(ns * (a_cut - a_lo) * half + na, nr, dtype=BF16),
            shape(RATE + 3, half, nr),
        ],
        [HBM] * 7,
        [VM] * (n_edges + 2),
        [
            field, pltpu.VMEM((na, LANES), F32), pltpu.VMEM((1, nr), F32),
            pltpu.VMEM(angular_rate.shape, F32), pltpu.SMEM(axial_diffusion.shape, F32),
            pltpu.SMEM(rate_constants.shape, F32), pltpu.SMEM(species_map.shape, jnp.int32),
            pltpu.SMEM(wall_flags.shape, jnp.int32), dma(9),
        ],
        (conc, courant[None], axial_diffusion, angular_rate, rate_constants, species_map, wall_flags),
        58,
    )
    mid_a, (angle_before, angle_after) = after(mid_a, (angle_before, angle_after))
    opp_a = lax.ppermute(mid_a, "ang", opposite)
    low, high = plane_halos(edges, planes)
    bounds = (a_cut, a_hi, x_hi, y_hi, l_hi)
    mid_b, mid_x, mid_y, mid_l = call(
        functools.partial(
            inner_kernel,
            (na, nz),
            tuple((k, ((bounds[k], bounds[k + 1] - bounds[k]),)) for k in range(4)),
        ),
        [message(bounds[k + 1] - bounds[k]) for k in range(4)],
        [ANY, VM],
        [VM] * 4,
        [field, pltpu.SemaphoreType.DMA],
        (conc, coef),
        8,
    )
    opp_b = lax.ppermute(mid_b, "ang", opposite)
    out1, out2 = call(
        functools.partial(frame_kernel, (na, nz, ends, planes)),
        [message(na // 2), message(na // 2 + 2 * ends)],
        [ANY] * 3 + [VM] * 2 + [ANY],
        [VM] * 2,
        [pltpu.VMEM((ns, (na + 2) * nz, nr), F32), pltpu.VMEM((RATE + 3, half, nr), F32), dma(4)],
        (conc, angle_before, angle_after, low, high, coef),
        8,
    )
    out2, opp_a = after(out2, opp_a)
    opp_2 = lax.ppermute(out2, "ang", opposite)
    out1, opp_b = after(out1, opp_b)
    opp_1 = lax.ppermute(out1, "ang", opposite)

    weights, keep = call(
        weights_kernel,
        [shape(ns, nr, 2 * nr, dtype=BF16), shape(2, ns, na, LANES)],
        [ANY, VM, VM],
        [VM] * 2,
        [pltpu.VMEM((ns, nr, nr), BF16), pltpu.VMEM((ns, nr, nr), BF16), dma(2, ns)],
        (radial_inverse, mid_a, opp_a),
        12,
    )

    def state(angles):
        return shape(2, ns, angles * half, nr)

    count_a, count_b = a_cut - a_lo, a_hi - a_cut
    (mid_first,) = call(
        functools.partial(
            radial_kernel,
            (((0, a_lo, 0, count_a),), ((0, a_cut, count_a, count_b),)),
            (),
            half,
        ),
        [state(count_a + count_b)],
        [VM] * 6,
        [VM],
        [],
        (weights, keep, mid_a, mid_b, opp_a, opp_b),
        8,
    )
    opp_1, mid_first = after(opp_1, mid_first)
    mid_x, opp_1 = after(mid_x, opp_1)
    opp_x = lax.ppermute(mid_x, "ang", opposite)
    (outer_first,) = call(
        functools.partial(radial_kernel, (((0, 0, 0, side),),), (), half),
        [state(side)],
        [VM] * 4,
        [VM],
        [],
        (weights, keep, out1, opp_1),
        8,
    )
    mid_y, opp_2 = after(mid_y, opp_2)
    opp_y = lax.ppermute(mid_y, "ang", opposite)
    plan = (((2, side, side, side), (0, 0, 0, ends), (1, na - ends, 0, ends)),)
    mid_left, ends_right, outer_state, *rest = call(
        functools.partial(
            radial_edges_kernel,
            (na, nz, planes),
            plan,
            ((0, 0, 0, ends, count_a + count_b), (1, 0, 2, 0, side)),
            half,
        ),
        [state(a_hi), state(ends), state(na)]
        + [shape(2, ns, na, nr, dtype=BF16)] * n_edges
        + [shape(2, ns, nz, nr, dtype=BF16)] * 2,
        [VM] * 6,
        [VM] * (5 + n_edges),
        [pltpu.VMEM((n_edges, na, nr), F32)],
        (weights, keep, out2, opp_2, mid_first, outer_first),
        8,
    )
    *edges, first, last = rest
    low, high = plane_halos(edges, planes)
    angle_before = lax.ppermute(last, "ang", ring(count, 1))
    angle_after = lax.ppermute(first, "ang", ring(count, -1))
    stage = [pltpu.VMEM((ns, na * nz, 2 * nr), BF16), pltpu.VMEM((ns, na, nz, nr), F32)]
    edge_scratch = [pltpu.VMEM((2, ns, na, nr), F32)] * 2
    def early(runs, base, mid, given):
        return call(
            functools.partial(early_kernel, (na, nz, runs, base, count // 2, planes)),
            shape(ns, na, nz, nr),
            [ANY] * len(given) + [VM] * 9,
            ANY,
            [pltpu.VMEM((2, ns, nz, nr), F32)] * 2 + edge_scratch + stage + [dma(len(runs), ns)],
            (*given, weights, keep, mid, outer_state, angle_before, angle_after, low, high, coef),
            12,
            {0: 0} if given else None,
        )

    def next_state(mine, theirs, begin, end, copies, parts, base, stop):
        return call(
            functools.partial(
                radial_kernel, (((0, begin, begin - base, end - begin),),), copies, half
            ),
            [state(stop - base)],
            [VM] * (4 + len(parts)),
            [VM],
            [],
            (weights, keep, mine, theirs, *parts),
            8,
        )[0]

    partial = early(((0, a_hi - 1),), 0, mid_left, ())
    opp_x, partial = after(opp_x, partial)
    mid_l, opp_x = after(mid_l, opp_x)
    opp_l = lax.ppermute(mid_l, "ang", opposite)
    base_x = a_hi - 2
    mid_x_state = next_state(
        mid_x, opp_x, a_hi, x_hi, ((0, base_x, 0, 0, 2),), (mid_left,), base_x, x_hi
    )
    partial = early(((a_hi - 1, x_hi - a_hi),), base_x, mid_x_state, (partial,))
    opp_y, partial = after(opp_y, partial)
    base = x_hi - 2
    mid_right = next_state(
        mid_y, opp_y, x_hi, y_hi,
        ((0, base - base_x, 0, 0, 2), (1, 0, 0, na - ends - base, ends)),
        (mid_x_state, ends_right), base, na,
    )
    partial = early(((x_hi - 1, y_hi - x_hi), (na - 1, 1)), base, mid_right, (partial,))
    wide = l_hi - y_hi + 4
    return call(
        functools.partial(late_kernel, (na, nz, y_hi, l_hi, base, planes)),
        shape(ns, na, nz, nr),
        [ANY] + [VM] * 9,
        ANY,
        [pltpu.VMEM((2, ns, wide * half, nr), F32)] + edge_scratch + stage + [dma(ns)],
        (partial, mid_right, weights, keep, mid_l, opp_l, outer_state, low, high, coef),
        12,
        {0: 0},
    )


def solution(mesh):
    in_specs = (P(None, "ang", "ax", None), P(), P(), P(), P(), P(), P(None, "ang"), P())
    out_specs = P(None, "ang", "ax", None)
    return jax.shard_map(
        per_device, mesh=mesh, in_specs=in_specs, out_specs=out_specs, check_vma=False
    )
```

```python
import functools

import jax
import jax.numpy as jnp
from jax import lax
from jax.experimental import pallas as pl
from jax.experimental.pallas import tpu as pltpu
from jax.sharding import PartitionSpec as P

F32 = jnp.float32
BF16 = jnp.bfloat16
MIB = 1024 * 1024
LANES = 128

ANY = pl.BlockSpec(memory_space=pl.ANY)
HBM = pl.BlockSpec(memory_space=pltpu.HBM)
VM = pl.BlockSpec(memory_space=pltpu.VMEM)
SM = pl.BlockSpec(memory_space=pltpu.SMEM)

OWN, BEFORE, ANGULAR, AXIAL, RATE = 0, 3, 6, 9, 12


def call(body, out_shape, in_specs, out_specs, scratch, args, mib, aliases=None):
    return pl.pallas_call(
        body,
        out_shape=out_shape,
        in_specs=in_specs,
        out_specs=out_specs,
        scratch_shapes=scratch,
        input_output_aliases=aliases or {},
        cost_estimate=pl.CostEstimate(flops=1, bytes_accessed=1, transcendentals=0),
        compiler_params=pltpu.CompilerParams(vmem_limit_bytes=mib * MIB),
    )(*args)


def shape(*dims, dtype=F32):
    return jax.ShapeDtypeStruct(dims, dtype)


def transport(now, before, after, around, coef):
    made = (
        coef[RATE] * (now[1] * now[2]),
        coef[RATE + 1] * (now[0] * now[2]),
        coef[RATE + 2] * (now[0] * now[1]),
    )
    spent = made[0] + made[1] + made[2]
    out = []
    for s in range(3):
        value = now[s] * coef[OWN + s] + before[s] * coef[BEFORE + s]
        value = value + after[s] * coef[AXIAL + s] + around[s] * coef[ANGULAR + s]
        out.append(value + ((made[s] + made[s]) - spent))
    return out


def turned(first, second, rows):
    first, second = pltpu.roll(first, rows // 2, 0), pltpu.roll(second, rows // 2, 0)
    upper = lax.broadcasted_iota(jnp.int32, first.shape, 0) < rows // 2
    return jnp.where(upper, first, second), jnp.where(upper, second, first)


def first_step(read, low, high, coef, half):
    tiles = [[read(s, 0, k) for s in range(3)] for k in range(2)]
    around = [[read(s, -1, k) + read(s, 1, k) for s in range(3)] for k in range(2)]
    row = lax.broadcasted_iota(jnp.int32, tiles[0][0].shape, 0)
    top, bottom = row == 0, row == half - 1
    fall = [[pltpu.roll(v, 1, 0) for v in tile] for tile in tiles]
    rise = [[pltpu.roll(v, half - 1, 0) for v in tile] for tile in tiles]
    out = []
    for k in range(2):
        other = 1 - k
        before = [
            jnp.where(top, low(s) if low is not None and k == 0 else fall[other][s], fall[k][s])
            for s in range(3)
        ]
        after = [
            jnp.where(bottom, high(s) if high is not None and k == 1 else rise[other][s], rise[k][s])
            for s in range(3)
        ]
        out.append(transport(tiles[k], before, after, around[k], coef))
    pairs = [turned(out[0][s], out[1][s], half) for s in range(3)]
    return [p[0] for p in pairs], [p[1] for p in pairs]


def second_step(read, low, high, coef, half):
    tiles = [[read(k, s, 0) for s in range(3)] for k in range(2)]
    around = [[read(k, s, -1) + read(k, s, 1) for s in range(3)] for k in range(2)]
    row = lax.broadcasted_iota(jnp.int32, tiles[0][0].shape, 0)
    top, bottom = row == 0, row == half - 1
    first, last = row == half // 2, row == half // 2 - 1
    fall = [[pltpu.roll(v, 1, 0) for v in tile] for tile in tiles]
    rise = [[pltpu.roll(v, half - 1, 0) for v in tile] for tile in tiles]
    out = []
    for k in range(2):
        before = [jnp.where(top, fall[1 - k][s], fall[k][s]) for s in range(3)]
        after = [jnp.where(bottom, rise[1 - k][s], rise[k][s]) for s in range(3)]
        if k == 1:
            before = [jnp.where(first, low(s), before[s]) for s in range(3)]
            after = [jnp.where(last, high(s), after[s]) for s in range(3)]
        out.append(transport(tiles[k], before, after, around[k], coef))
    return out


def pack(tiles):
    return jnp.concatenate(tiles, 0).astype(BF16)


def at_rows(start, count, step):
    return pl.ds(pl.multiple_of(start, step), count)


def field_reader(field, t, nz):
    half = nz // 2
    return lambda s, shift, k: field[s, at_rows((t + shift) * nz + k * half, half, half), :]


def mid_run(field, out_of, begin, count, at, coef, nz):
    half = nz // 2

    def pair(step, carry):
        t = begin + step * 2
        tiles = [first_step(field_reader(field, t + k, nz), None, None, coef, half)[0] for k in range(2)]
        for s in range(3):
            out_of(s)[at_rows(at * half + step * nz, nz, nz), :] = pack([tiles[0][s], tiles[1][s]])
        return carry

    lax.fori_loop(0, count // 2, pair, 0)


def head_kernel(sizes, conc, cour, diff, ang, rate, smap, flags, *rest):
    na, nz, lo, hi, planes = sizes
    edges = rest[: 1 if planes == 2 else 2]
    mid, coef, field, flag_v, cour_v, ang_v, diff_s, rate_s, map_s, flags_s, sems = rest[
        len(edges) :
    ]
    half = nz // 2
    inner = pl.ds((lo - 1) * nz, (hi - lo + 2) * nz)
    left = pl.ds(0, (lo - 1) * nz)
    right = pl.ds((hi + 1) * nz, (na - hi - 1) * nz)
    small = [
        pltpu.make_async_copy(src, dst, sems.at[k + 3])
        for k, (src, dst) in enumerate(
            ((cour, cour_v), (ang, ang_v), (diff, diff_s), (rate, rate_s), (smap, map_s), (flags, flags_s))
        )
    ]
    copies = [
        pltpu.make_async_copy(conc.at[:, rows], field.at[:, rows], sems.at[k])
        for k, rows in enumerate((inner, left, right))
    ]
    for copy in small + copies:
        copy.start()
    for copy in small:
        copy.wait()
    tile = coef.shape[1:]
    for s in range(3):
        courant, angular = cour_v[...], ang_v[s : s + 1, :]
        axial = diff_s[s]
        total = jnp.float32(0.0)
        for k in range(map_s.shape[0]):
            total = total + jnp.where(map_s[k, 2] == s, rate_s[k], 0.0)
        coef[OWN + s] = jnp.broadcast_to((1.0 - 2.0 * axial) - courant - 2.0 * angular, tile)
        coef[BEFORE + s] = jnp.broadcast_to(courant + axial, tile)
        coef[ANGULAR + s] = jnp.broadcast_to(angular, tile)
        coef[AXIAL + s] = jnp.full(tile, axial, F32)
        coef[RATE + s] = jnp.full(tile, total, F32)
    lane = lax.broadcasted_iota(jnp.int32, (1, LANES), 1)
    for t in range(na):
        row = jnp.zeros((1, LANES), jnp.int32)
        for s in range(3):
            row = jnp.where(lane == s, flags_s[s, t], row)
        flag_v[t : t + 1, :] = row.astype(F32)
    rows = (hi - lo) * half
    span = pl.ds(3 * rows, na)
    mid[span, :] = jnp.zeros((na, mid.shape[1]), BF16)
    mid[span, :LANES] = flag_v[...].astype(BF16)
    copies[0].wait()
    mid_run(field, lambda s: mid.at[pl.ds(s * rows, rows)], lo, hi - lo, 0, coef, nz)
    copies[1].wait()
    copies[2].wait()
    for s in range(3):
        if planes == 2:
            row = jnp.where(lax.axis_index("ax") == 0, nz - 1, 0)
            for t in range(na):
                edges[0][s, t : t + 1, :] = field[s, pl.ds(t * nz + row, 1), :]
        else:
            for t in range(na):
                edges[0][s, t : t + 1, :] = field[s, t * nz : t * nz + 1, :]
                edges[1][s, t : t + 1, :] = field[s, (t + 1) * nz - 1 : (t + 1) * nz, :]


def inner_kernel(sizes, runs, conc, coef, *rest):
    na, nz = sizes
    outs, field, sem = rest[:-2], rest[-2], rest[-1]
    copy = pltpu.make_async_copy(conc, field, sem)
    copy.start()
    copy.wait()
    for out, parts in runs:
        at = 0
        for begin, count in parts:
            mid_run(field, outs[out].at.__getitem__, begin, count, at, coef, nz)
            at += count


def edge_weights(planes):
    if planes != 2:
        return 1.0, 1.0
    place = lax.axis_index("ax")
    return jnp.where(place == 1, 1.0, 0.0), jnp.where(place == 0, 1.0, 0.0)


def frame_kernel(
    sizes, conc, before, after, low, high, coef_in, out1, out2, field, coef, sems
):
    na, nz, ends, planes = sizes
    half = nz // 2
    copies = [
        pltpu.make_async_copy(conc, field.at[:, pl.ds(nz, na * nz)], sems.at[0]),
        pltpu.make_async_copy(before, field.at[:, pl.ds(0, nz)], sems.at[1]),
        pltpu.make_async_copy(after, field.at[:, pl.ds((na + 1) * nz, nz)], sems.at[2]),
        pltpu.make_async_copy(coef_in, coef, sems.at[3]),
    ]
    for copy in copies:
        copy.start()
    low_weight, high_weight = edge_weights(planes)
    for copy in copies:
        copy.wait()

    def angle(t):
        return first_step(
            field_reader(field, t + 1, nz),
            lambda s: low[s, pl.ds(t, 1), :] * low_weight,
            lambda s: high[s, pl.ds(t, 1), :] * high_weight,
            coef,
            half,
        )

    def pair(t, out, row, ends_row):
        tiles = [angle(t), angle(t + 1)]
        for s in range(3):
            out[s, pl.ds(row, nz), :] = pack([tiles[0][1][s], tiles[1][1][s]])
            if ends_row is not None:
                out2[s, pl.ds(ends_row, nz), :] = pack([tiles[0][0][s], tiles[1][0][s]])

    quarter = na // 4
    tail = na // 2 * half
    pair(0, out1, 0, tail)
    pair(na - 2, out2, (na // 2 - 2) * half, tail + nz)

    def first_part(step, carry):
        pair(step * 2, out1, pl.multiple_of(step * nz, nz), None)
        return carry

    def second_part(step, carry):
        pair(na // 2 + step * 2, out2, pl.multiple_of(step * nz, nz), None)
        return carry

    lax.fori_loop(1, quarter, first_part, 0)
    lax.fori_loop(0, quarter - 1, second_part, 0)


def weights_kernel(matrix, mine, theirs, out, keep, left, lower, sems):
    half = out.shape[1]
    copies = []
    for s in range(out.shape[0]):
        for k, ref in enumerate((left, lower)):
            src = matrix.at[s, pl.ds(k * half, half), pl.ds(0, half)]
            copies.append(pltpu.make_async_copy(src, ref.at[s], sems.at[k, s]))
    for copy in copies:
        copy.start()
    na = keep.shape[2]
    lane = lax.broadcasted_iota(jnp.int32, (na, LANES), 1)
    for ab, ref in enumerate((mine, theirs)):
        flags = ref[pl.ds(ref.shape[0] - na, na), :LANES].astype(F32)
        for s in range(out.shape[0]):
            moved = pltpu.roll(flags, LANES - s, 1) if s else flags
            keep[ab, s] = jnp.where(lane == 0, 1.0 - moved, 1.0)
    row = lax.broadcasted_iota(jnp.int32, (half, half), 0)
    col = lax.broadcasted_iota(jnp.int32, (half, half), 1)
    row = jnp.maximum(row, 1)
    pick = jnp.where(col == row, 1.0, 0.0).astype(BF16)
    flip = jnp.where(col == half - 1 - row, 1.0, 0.0).astype(BF16)
    for copy in copies:
        copy.wait()
    for s in range(out.shape[0]):
        out[s, :, :half] = jnp.dot(pick, left[s], preferred_element_type=F32).astype(BF16)
        out[s, :, half:] = jnp.dot(flip, lower[s], preferred_element_type=F32).astype(BF16)


def rows_product(rows, weights):
    return lax.dot_general(rows, weights, (((1,), (1,)), ((), ())), preferred_element_type=F32)


def both_sides(mine, theirs, weights):
    rows = jnp.concatenate(
        [jnp.concatenate([mine, theirs], 1), jnp.concatenate([theirs, mine], 1)], 0
    )
    return rows_product(rows, weights)


def store_run(state, s, begin, place, count, at, value, keep, half):
    total = value.shape[0] // 2
    for ab in range(2):
        part = value[ab * total + at * half : ab * total + (at + count) * half]
        state[ab, s, pl.ds(place * half, count * half), LANES:] = part[:, LANES:]
        for k in range(count):
            state[ab, s, pl.ds((place + k) * half, half), :LANES] = (
                part[k * half : (k + 1) * half, :LANES] * keep[ab, s, begin + k : begin + k + 1, :]
            )


def species_rows(ref, s, runs, half):
    if len(ref.shape) == 3:
        return ref[s]
    rows = sum(run[3] for run in runs) * half
    return ref[pl.ds(s * rows, rows), :]


def radial_kernel(plan, copies, half, weights, keep, *refs):
    n = len(plan)
    mines, theirs, refs = refs[:n], refs[n : 2 * n], refs[2 * n :]
    n_in = 1 + max((part for part, *_ in copies), default=-1)
    parts, states = refs[:n_in], refs[n_in:]
    for s in range(3):
        for k, runs in enumerate(plan):
            value = both_sides(
                species_rows(mines[k], s, runs, half),
                species_rows(theirs[k], s, runs, half),
                weights[s],
            )
            at = 0
            for which, begin, place, count in runs:
                store_run(states[which], s, begin, place, count, at, value, keep, half)
                at += count
    for part, source, which, place, count in copies:
        to, rows = pl.ds(place * half, count * half), pl.ds(source * half, count * half)
        for ab in range(2):
            for s in range(3):
                states[which][ab, s, to, :] = parts[part][ab, s, rows, :]


def edges_of_state(na, nz, planes, mid, mid_end, outer, edges, first, last, stage):
    half = nz // 2
    if planes == 2:
        row = jnp.where(lax.axis_index("ax") == 0, half // 2 - 1, half // 2)
    end = pl.ds((na - 1) * half, half)
    ends_end = pl.ds(mid_end.shape[2] - half, half)
    for ab in range(2):
        for s in range(3):
            for t in range(na):
                to = pl.ds(t, 1)
                at = t * half + half // 2
                if planes == 2:
                    stage[0, to, :] = outer[ab, s, pl.ds(t * half + row, 1), :]
                else:
                    stage[0, to, :] = outer[ab, s, at : at + 1, :]
                    stage[1, to, :] = outer[ab, s, at - 1 : at, :]
            for k, edge in enumerate(edges):
                edge[ab, s] = stage[k].astype(BF16)
            begin = pl.ds(0, half)
            first[ab, s] = pack([mid[ab, s, begin, :], outer[ab, s, begin, :]])
            last[ab, s] = pack([mid_end[ab, s, ends_end, :], outer[ab, s, end, :]])


def radial_edges_kernel(sizes, plan, copies, half, weights, keep, *refs):
    na, nz, planes = sizes
    n_edges = 1 if planes == 2 else 2
    *edges, first, last, stage = refs[-3 - n_edges :]
    refs = refs[: -3 - n_edges]
    radial_kernel(plan, copies, half, weights, keep, *refs)
    edges_of_state(na, nz, planes, refs[-3], refs[-2], refs[-1], edges, first, last, stage)


def explicit_angle(t, reader, low, high, edge_factors, coef, rows, nz):
    half = nz // 2
    for ab in range(2):
        out = second_step(
            functools.partial(reader, ab),
            lambda s: low[ab, s, pl.ds(t, 1), :] * edge_factors[0],
            lambda s: high[ab, s, pl.ds(t, 1), :] * edge_factors[1],
            coef,
            half,
        )
        width = out[0][0].shape[1]
        for s in range(3):
            rows[s, at_rows(t * nz, nz, nz), ab * width : (ab + 1) * width] = pack(
                [out[0][s], out[1][s]]
            )


def explicit_run(begin, count, states, low, high, edge_factors, coef, rows, nz):
    half = nz // 2

    def one(step, carry):
        t = begin + step

        def reader(ab, k, s, shift):
            state, base = states[k]
            return state[ab, s, at_rows((t - base + shift) * half, half, half), :]

        explicit_angle(t, reader, low, high, edge_factors, coef, rows, nz)
        return carry

    lax.fori_loop(0, count, one, 0)


def finish_run(begin, count, s, rows, weights, keep, result, nz):
    half = nz // 2
    value = rows_product(rows[s, pl.ds(begin * nz, count * nz), :], weights[s])
    for k in range(count):
        t = begin + k
        parts = turned(value[k * nz + half : (k + 1) * nz], value[k * nz : k * nz + half], half)
        for p in range(2):
            span = pl.ds(p * half, half)
            result[s, t, span, LANES:] = parts[p][:, LANES:]
            result[s, t, span, :LANES] = parts[p][:, :LANES] * keep[0, s, t : t + 1, :]


def widen(pairs):
    for source, target in pairs:
        target[...] = source[...].astype(F32)


def early_kernel(sizes, *refs):
    na, nz, runs, base, half_ring, planes = sizes
    if len(refs) == 18:
        refs = refs[1:]
    (weights, keep, mid, outer, before_low, after_low, low_low, high_low, coef, out,
     before, after, low, high, rows, result, out_sems) = refs
    half = nz // 2
    place = lax.rem(lax.axis_index("ang"), half_ring)
    wrap_before = jnp.where(place == 0, 1, 0)
    wrap_after = jnp.where(place == half_ring - 1, 1, 0)
    factors = edge_weights(planes)
    states = ((mid, base), (outer, 0))
    widen(((low_low, low), (high_low, high)))
    for begin, count in runs:
        end = begin + count
        if begin == 0:
            widen(((before_low, before),))

            def reader(ab, k, s, shift):
                if shift == -1:
                    source = jnp.where(wrap_before == 1, 1 - ab, ab)
                    return before[source, s, pl.ds(k * half, half), :]
                return states[k][0][ab, s, pl.ds((shift - states[k][1]) * half, half), :]

            explicit_angle(0, reader, low, high, factors, coef, rows, nz)
        if end == na:
            widen(((after_low, after),))

            def reader(ab, k, s, shift):
                if shift == 1:
                    source = jnp.where(wrap_after == 1, 1 - ab, ab)
                    return after[source, s, pl.ds(k * half, half), :]
                return states[k][0][ab, s, pl.ds((na - 1 + shift - states[k][1]) * half, half), :]

            explicit_angle(na - 1, reader, low, high, factors, coef, rows, nz)
        start, stop = max(begin, 1), min(end, na - 1)
        if stop > start:
            explicit_run(start, stop - start, states, low, high, factors, coef, rows, nz)
    leaves = []
    for s in range(3):
        for k, (begin, count) in enumerate(runs):
            finish_run(begin, count, s, rows, weights, keep, result, nz)
            span = pl.ds(begin, count)
            leave = pltpu.make_async_copy(result.at[s, span], out.at[s, span], out_sems.at[k, s])
            leave.start()
            leaves.append(leave)
    for leave in leaves:
        leave.wait()


def late_kernel(
    sizes, given, state, weights, keep, mine, theirs, outer, low_low, high_low, coef,
    out, mid, low, high, rows, result, out_sems,
):
    na, nz, lo, hi, base, planes = sizes
    half = nz // 2
    factors = edge_weights(planes)
    count = hi - lo
    widen(((low_low, low), (high_low, high)))
    for s in range(3):
        value = both_sides(mine[s], theirs[s], weights[s])
        store_run(mid, s, lo, 2, count, 0, value, keep, half)
        for ab in range(2):
            for k in range(2):
                to = pl.ds((2 + count) * k * half, 2 * half)
                mid[ab, s, to, :] = state[
                    ab, s, pl.ds((lo - 2 - base + (2 + count) * k) * half, 2 * half), :
                ]
    explicit_run(lo - 1, count + 2, ((mid, lo - 2), (outer, 0)), low, high, factors, coef, rows, nz)
    leaves = []
    for s in range(3):
        finish_run(lo - 1, count + 2, s, rows, weights, keep, result, nz)
        span = pl.ds(lo - 1, count + 2)
        leave = pltpu.make_async_copy(result.at[s, span], out.at[s, span], out_sems.at[s])
        leave.start()
        leaves.append(leave)
    for leave in leaves:
        leave.wait()


def ring(count, step):
    half = count // 2
    return [(i, i // half * half + (i % half + step) % half) for i in range(count)]


def plane_halos(edges, planes):
    if planes == 2:
        got = lax.ppermute(edges[0], "ax", [(0, 1), (1, 0)])
        return got, got
    up = [(i, i + 1) for i in range(planes - 1)]
    down = [(i + 1, i) for i in range(planes - 1)]
    return lax.ppermute(edges[1], "ax", up), lax.ppermute(edges[0], "ax", down)


def after(value, done):
    return lax.optimization_barrier((value, done))


def per_device(
    concentration, courant, axial_diffusion, angular_rate, rate_constants, species_map,
    wall_flags, radial_inverse,
):
    ns, na, nz, nr = concentration.shape
    half = nz // 2
    count = lax.axis_size("ang")
    planes = lax.axis_size("ax")
    n_edges = 1 if planes == 2 else 2
    quarter = na // 4
    ends = 2
    side = na // 2
    a_lo, a_hi = ends, na // 4
    x_hi, y_hi, l_hi = 18 * na // 32, 26 * na // 32, na - ends
    opposite = [(i, (i + count // 2) % count) for i in range(count)]

    def dma(*dims):
        return pltpu.SemaphoreType.DMA(dims)

    def message(angles):
        return shape(ns, angles * half, nr, dtype=BF16)

    angle_before = lax.ppermute(
        concentration[:, na - 1], "ang", [(i, (i + 1) % count) for i in range(count)]
    )
    angle_after = lax.ppermute(
        concentration[:, 0], "ang", [(i, (i - 1) % count) for i in range(count)]
    )
    conc = concentration.reshape(ns, na * nz, nr)
    field = pltpu.VMEM((ns, na * nz, nr), F32)
    *edges, mid_a, coef = call(
        functools.partial(head_kernel, (na, nz, a_lo, a_hi, planes)),
        [shape(ns, na, nr)] * n_edges
        + [
            shape(ns * (a_hi - a_lo) * half + na, nr, dtype=BF16),
            shape(RATE + 3, half, nr),
        ],
        [HBM] * 7,
        [VM] * (n_edges + 2),
        [
            field, pltpu.VMEM((na, LANES), F32), pltpu.VMEM((1, nr), F32),
            pltpu.VMEM(angular_rate.shape, F32), pltpu.SMEM(axial_diffusion.shape, F32),
            pltpu.SMEM(rate_constants.shape, F32), pltpu.SMEM(species_map.shape, jnp.int32),
            pltpu.SMEM(wall_flags.shape, jnp.int32), dma(9),
        ],
        (conc, courant[None], axial_diffusion, angular_rate, rate_constants, species_map, wall_flags),
        58,
    )
    mid_a, (angle_before, angle_after) = after(mid_a, (angle_before, angle_after))
    opp_a = lax.ppermute(mid_a, "ang", opposite)
    low, high = plane_halos(edges, planes)
    bounds = (a_hi, x_hi, y_hi, l_hi)
    mid_x, mid_y, mid_l = call(
        functools.partial(
            inner_kernel,
            (na, nz),
            tuple((k, ((bounds[k], bounds[k + 1] - bounds[k]),)) for k in range(3)),
        ),
        [message(bounds[k + 1] - bounds[k]) for k in range(3)],
        [ANY, VM],
        [VM] * 3,
        [field, pltpu.SemaphoreType.DMA],
        (conc, coef),
        8,
    )
    out1, out2 = call(
        functools.partial(frame_kernel, (na, nz, ends, planes)),
        [message(na // 2), message(na // 2 + 2 * ends)],
        [ANY] * 3 + [VM] * 2 + [ANY],
        [VM] * 2,
        [pltpu.VMEM((ns, (na + 2) * nz, nr), F32), pltpu.VMEM((RATE + 3, half, nr), F32), dma(4)],
        (conc, angle_before, angle_after, low, high, coef),
        8,
    )
    (out1, out2), opp_a = after((out1, out2), opp_a)
    opp_2 = lax.ppermute(out2, "ang", opposite)
    opp_1 = lax.ppermute(out1, "ang", opposite)

    weights, keep = call(
        weights_kernel,
        [shape(ns, nr, 2 * nr, dtype=BF16), shape(2, ns, na, LANES)],
        [ANY, VM, VM],
        [VM] * 2,
        [pltpu.VMEM((ns, nr, nr), BF16), pltpu.VMEM((ns, nr, nr), BF16), dma(2, ns)],
        (radial_inverse, mid_a, opp_a),
        12,
    )

    def state(angles):
        return shape(2, ns, angles * half, nr)

    count_a = a_hi - a_lo
    (mid_first,) = call(
        functools.partial(radial_kernel, (((0, a_lo, 0, count_a),),), (), half),
        [state(count_a)],
        [VM] * 4,
        [VM],
        [],
        (weights, keep, mid_a, opp_a),
        8,
    )
    opp_1, mid_first = after(opp_1, mid_first)
    mid_x, opp_1 = after(mid_x, opp_1)
    opp_x = lax.ppermute(mid_x, "ang", opposite)
    (outer_first,) = call(
        functools.partial(radial_kernel, (((0, 0, 0, side),),), (), half),
        [state(side)],
        [VM] * 4,
        [VM],
        [],
        (weights, keep, out1, opp_1),
        8,
    )
    mid_y, opp_2 = after(mid_y, opp_2)
    opp_y = lax.ppermute(mid_y, "ang", opposite)
    plan = (((2, side, side, side), (0, 0, 0, ends), (1, na - ends, 0, ends)),)
    mid_left, ends_right, outer_state, *rest = call(
        functools.partial(
            radial_edges_kernel,
            (na, nz, planes),
            plan,
            ((0, 0, 0, ends, count_a), (1, 0, 2, 0, side)),
            half,
        ),
        [state(a_hi), state(ends), state(na)]
        + [shape(2, ns, na, nr, dtype=BF16)] * n_edges
        + [shape(2, ns, nz, nr, dtype=BF16)] * 2,
        [VM] * 6,
        [VM] * (5 + n_edges),
        [pltpu.VMEM((n_edges, na, nr), F32)],
        (weights, keep, out2, opp_2, mid_first, outer_first),
        8,
    )
    *edges, first, last = rest
    low, high = plane_halos(edges, planes)
    angle_before = lax.ppermute(last, "ang", ring(count, 1))
    angle_after = lax.ppermute(first, "ang", ring(count, -1))
    stage = [pltpu.VMEM((ns, na * nz, 2 * nr), BF16), pltpu.VMEM((ns, na, nz, nr), F32)]
    edge_scratch = [pltpu.VMEM((2, ns, na, nr), F32)] * 2
    def early(runs, base, mid, given):
        return call(
            functools.partial(early_kernel, (na, nz, runs, base, count // 2, planes)),
            shape(ns, na, nz, nr),
            [ANY] * len(given) + [VM] * 9,
            ANY,
            [pltpu.VMEM((2, ns, nz, nr), F32)] * 2 + edge_scratch + stage + [dma(len(runs), ns)],
            (*given, weights, keep, mid, outer_state, angle_before, angle_after, low, high, coef),
            12,
            {0: 0} if given else None,
        )

    def next_state(mine, theirs, begin, end, copies, parts, base, stop):
        return call(
            functools.partial(
                radial_kernel, (((0, begin, begin - base, end - begin),),), copies, half
            ),
            [state(stop - base)],
            [VM] * (4 + len(parts)),
            [VM],
            [],
            (weights, keep, mine, theirs, *parts),
            8,
        )[0]

    mid_l, opp_x = after(mid_l, opp_x)
    opp_l = lax.ppermute(mid_l, "ang", opposite)
    mid_x_state = next_state(
        mid_x, opp_x, a_hi, x_hi, ((0, 0, 0, 0, a_hi),), (mid_left,), 0, x_hi
    )
    partial = early(((0, x_hi - 1),), 0, mid_x_state, ())
    opp_y, partial = after(opp_y, partial)
    base = x_hi - 2
    mid_right = next_state(
        mid_y, opp_y, x_hi, y_hi,
        ((0, base, 0, 0, 2), (1, 0, 0, na - ends - base, ends)),
        (mid_x_state, ends_right), base, na,
    )
    partial = early(((x_hi - 1, y_hi - x_hi), (na - 1, 1)), base, mid_right, (partial,))
    wide = l_hi - y_hi + 4
    return call(
        functools.partial(late_kernel, (na, nz, y_hi, l_hi, base, planes)),
        shape(ns, na, nz, nr),
        [ANY] + [VM] * 9,
        ANY,
        [pltpu.VMEM((2, ns, wide * half, nr), F32)] + edge_scratch + stage + [dma(ns)],
        (partial, mid_right, weights, keep, mid_l, opp_l, outer_state, low, high, coef),
        12,
        {0: 0},
    )


def solution(mesh):
    in_specs = (P(None, "ang", "ax", None), P(), P(), P(), P(), P(), P(None, "ang"), P())
    out_specs = P(None, "ang", "ax", None)
    return jax.shard_map(
        per_device, mesh=mesh, in_specs=in_specs, out_specs=out_specs, check_vma=False
    )
```

```python
import functools

import jax
import jax.numpy as jnp
from jax import lax
from jax.experimental import pallas as pl
from jax.experimental.pallas import tpu as pltpu
from jax.sharding import PartitionSpec as P

F32 = jnp.float32
BF16 = jnp.bfloat16
MIB = 1024 * 1024
LANES = 128

ANY = pl.BlockSpec(memory_space=pl.ANY)
HBM = pl.BlockSpec(memory_space=pltpu.HBM)
VM = pl.BlockSpec(memory_space=pltpu.VMEM)
SM = pl.BlockSpec(memory_space=pltpu.SMEM)

OWN, BEFORE, ANGULAR, AXIAL, RATE = 0, 3, 6, 9, 12


def call(body, out_shape, in_specs, out_specs, scratch, args, mib, aliases=None):
    return pl.pallas_call(
        body,
        out_shape=out_shape,
        in_specs=in_specs,
        out_specs=out_specs,
        scratch_shapes=scratch,
        input_output_aliases=aliases or {},
        cost_estimate=pl.CostEstimate(flops=1, bytes_accessed=1, transcendentals=0),
        compiler_params=pltpu.CompilerParams(vmem_limit_bytes=mib * MIB),
    )(*args)


def shape(*dims, dtype=F32):
    return jax.ShapeDtypeStruct(dims, dtype)


def transport(now, before, after, around, coef):
    made = (
        coef[RATE] * (now[1] * now[2]),
        coef[RATE + 1] * (now[0] * now[2]),
        coef[RATE + 2] * (now[0] * now[1]),
    )
    spent = made[0] + made[1] + made[2]
    out = []
    for s in range(3):
        value = now[s] * coef[OWN + s] + before[s] * coef[BEFORE + s]
        value = value + after[s] * coef[AXIAL + s] + around[s] * coef[ANGULAR + s]
        out.append(value + ((made[s] + made[s]) - spent))
    return out


def turned(first, second, rows):
    first, second = pltpu.roll(first, rows // 2, 0), pltpu.roll(second, rows // 2, 0)
    upper = lax.broadcasted_iota(jnp.int32, first.shape, 0) < rows // 2
    return jnp.where(upper, first, second), jnp.where(upper, second, first)


def first_step(read, low, high, coef, half):
    tiles = [[read(s, 0, k) for s in range(3)] for k in range(2)]
    around = [[read(s, -1, k) + read(s, 1, k) for s in range(3)] for k in range(2)]
    row = lax.broadcasted_iota(jnp.int32, tiles[0][0].shape, 0)
    top, bottom = row == 0, row == half - 1
    fall = [[pltpu.roll(v, 1, 0) for v in tile] for tile in tiles]
    rise = [[pltpu.roll(v, half - 1, 0) for v in tile] for tile in tiles]
    out = []
    for k in range(2):
        other = 1 - k
        before = [
            jnp.where(top, low(s) if low is not None and k == 0 else fall[other][s], fall[k][s])
            for s in range(3)
        ]
        after = [
            jnp.where(bottom, high(s) if high is not None and k == 1 else rise[other][s], rise[k][s])
            for s in range(3)
        ]
        out.append(transport(tiles[k], before, after, around[k], coef))
    pairs = [turned(out[0][s], out[1][s], half) for s in range(3)]
    return [p[0] for p in pairs], [p[1] for p in pairs]


def second_step(read, low, high, coef, half):
    tiles = [[read(k, s, 0) for s in range(3)] for k in range(2)]
    around = [[read(k, s, -1) + read(k, s, 1) for s in range(3)] for k in range(2)]
    row = lax.broadcasted_iota(jnp.int32, tiles[0][0].shape, 0)
    top, bottom = row == 0, row == half - 1
    first, last = row == half // 2, row == half // 2 - 1
    fall = [[pltpu.roll(v, 1, 0) for v in tile] for tile in tiles]
    rise = [[pltpu.roll(v, half - 1, 0) for v in tile] for tile in tiles]
    out = []
    for k in range(2):
        before = [jnp.where(top, fall[1 - k][s], fall[k][s]) for s in range(3)]
        after = [jnp.where(bottom, rise[1 - k][s], rise[k][s]) for s in range(3)]
        if k == 1:
            before = [jnp.where(first, low(s), before[s]) for s in range(3)]
            after = [jnp.where(last, high(s), after[s]) for s in range(3)]
        out.append(transport(tiles[k], before, after, around[k], coef))
    return out


def pack(tiles):
    return jnp.concatenate(tiles, 0).astype(BF16)


def at_rows(start, count, step):
    return pl.ds(pl.multiple_of(start, step), count)


def field_reader(field, t, nz):
    half = nz // 2
    return lambda s, shift, k: field[s, at_rows((t + shift) * nz + k * half, half, half), :]


def mid_run(field, out_of, begin, count, at, coef, nz):
    half = nz // 2

    def pair(step, carry):
        t = begin + step * 2
        tiles = [first_step(field_reader(field, t + k, nz), None, None, coef, half)[0] for k in range(2)]
        for s in range(3):
            out_of(s)[at_rows(at * half + step * nz, nz, nz), :] = pack([tiles[0][s], tiles[1][s]])
        return carry

    lax.fori_loop(0, count // 2, pair, 0)


def head_kernel(sizes, conc, cour, diff, ang, rate, smap, flags, *rest):
    na, nz, lo, hi, planes = sizes
    edges = rest[: 1 if planes == 2 else 2]
    mid, coef, field, flag_v, cour_v, ang_v, diff_s, rate_s, map_s, flags_s, sems = rest[
        len(edges) :
    ]
    half = nz // 2
    inner = pl.ds((lo - 1) * nz, (hi - lo + 2) * nz)
    left = pl.ds(0, (lo - 1) * nz)
    right = pl.ds((hi + 1) * nz, (na - hi - 1) * nz)
    small = [
        pltpu.make_async_copy(src, dst, sems.at[k + 3])
        for k, (src, dst) in enumerate(
            ((cour, cour_v), (ang, ang_v), (diff, diff_s), (rate, rate_s), (smap, map_s), (flags, flags_s))
        )
    ]
    copies = [
        pltpu.make_async_copy(conc.at[:, rows], field.at[:, rows], sems.at[k])
        for k, rows in enumerate((inner, left, right))
    ]
    for copy in small + copies:
        copy.start()
    for copy in small:
        copy.wait()
    tile = coef.shape[1:]
    for s in range(3):
        courant, angular = cour_v[...], ang_v[s : s + 1, :]
        axial = diff_s[s]
        total = jnp.float32(0.0)
        for k in range(map_s.shape[0]):
            total = total + jnp.where(map_s[k, 2] == s, rate_s[k], 0.0)
        coef[OWN + s] = jnp.broadcast_to((1.0 - 2.0 * axial) - courant - 2.0 * angular, tile)
        coef[BEFORE + s] = jnp.broadcast_to(courant + axial, tile)
        coef[ANGULAR + s] = jnp.broadcast_to(angular, tile)
        coef[AXIAL + s] = jnp.full(tile, axial, F32)
        coef[RATE + s] = jnp.full(tile, total, F32)
    lane = lax.broadcasted_iota(jnp.int32, (1, LANES), 1)
    for t in range(na):
        row = jnp.zeros((1, LANES), jnp.int32)
        for s in range(3):
            row = jnp.where(lane == s, flags_s[s, t], row)
        flag_v[t : t + 1, :] = row.astype(F32)
    rows = (hi - lo) * half
    span = pl.ds(3 * rows, na)
    mid[span, :] = jnp.zeros((na, mid.shape[1]), BF16)
    mid[span, :LANES] = flag_v[...].astype(BF16)
    copies[0].wait()
    mid_run(field, lambda s: mid.at[pl.ds(s * rows, rows)], lo, hi - lo, 0, coef, nz)
    copies[1].wait()
    copies[2].wait()
    for s in range(3):
        if planes == 2:
            row = jnp.where(lax.axis_index("ax") == 0, nz - 1, 0)
            for t in range(na):
                edges[0][s, t : t + 1, :] = field[s, pl.ds(t * nz + row, 1), :]
        else:
            for t in range(na):
                edges[0][s, t : t + 1, :] = field[s, t * nz : t * nz + 1, :]
                edges[1][s, t : t + 1, :] = field[s, (t + 1) * nz - 1 : (t + 1) * nz, :]


def inner_kernel(sizes, runs, conc, coef, *rest):
    na, nz = sizes
    outs, field, sem = rest[:-2], rest[-2], rest[-1]
    copy = pltpu.make_async_copy(conc, field, sem)
    copy.start()
    copy.wait()
    for out, parts in runs:
        at = 0
        for begin, count in parts:
            mid_run(field, outs[out].at.__getitem__, begin, count, at, coef, nz)
            at += count


def edge_weights(planes):
    if planes != 2:
        return 1.0, 1.0
    place = lax.axis_index("ax")
    return jnp.where(place == 1, 1.0, 0.0), jnp.where(place == 0, 1.0, 0.0)


def frame_kernel(
    sizes, conc, before, after, low, high, coef_in, out1, out2, field, coef, sems
):
    na, nz, ends, planes = sizes
    half = nz // 2
    copies = [
        pltpu.make_async_copy(conc, field.at[:, pl.ds(nz, na * nz)], sems.at[0]),
        pltpu.make_async_copy(before, field.at[:, pl.ds(0, nz)], sems.at[1]),
        pltpu.make_async_copy(after, field.at[:, pl.ds((na + 1) * nz, nz)], sems.at[2]),
        pltpu.make_async_copy(coef_in, coef, sems.at[3]),
    ]
    for copy in copies:
        copy.start()
    low_weight, high_weight = edge_weights(planes)
    for copy in copies:
        copy.wait()

    def angle(t):
        return first_step(
            field_reader(field, t + 1, nz),
            lambda s: low[s, pl.ds(t, 1), :] * low_weight,
            lambda s: high[s, pl.ds(t, 1), :] * high_weight,
            coef,
            half,
        )

    def pair(t, out, row, ends_row):
        tiles = [angle(t), angle(t + 1)]
        for s in range(3):
            out[s, pl.ds(row, nz), :] = pack([tiles[0][1][s], tiles[1][1][s]])
            if ends_row is not None:
                out2[s, pl.ds(ends_row, nz), :] = pack([tiles[0][0][s], tiles[1][0][s]])

    quarter = na // 4
    tail = na // 2 * half
    pair(0, out1, 0, tail)
    pair(na - 2, out2, (na // 2 - 2) * half, tail + nz)

    def first_part(step, carry):
        pair(step * 2, out1, pl.multiple_of(step * nz, nz), None)
        return carry

    def second_part(step, carry):
        pair(na // 2 + step * 2, out2, pl.multiple_of(step * nz, nz), None)
        return carry

    lax.fori_loop(1, quarter, first_part, 0)
    lax.fori_loop(0, quarter - 1, second_part, 0)


def weights_kernel(matrix, mine, theirs, out, keep, left, lower, sems):
    half = out.shape[1]
    copies = []
    for s in range(out.shape[0]):
        for k, ref in enumerate((left, lower)):
            src = matrix.at[s, pl.ds(k * half, half), pl.ds(0, half)]
            copies.append(pltpu.make_async_copy(src, ref.at[s], sems.at[k, s]))
    for copy in copies:
        copy.start()
    na = keep.shape[2]
    lane = lax.broadcasted_iota(jnp.int32, (na, LANES), 1)
    for ab, ref in enumerate((mine, theirs)):
        flags = ref[pl.ds(ref.shape[0] - na, na), :LANES].astype(F32)
        for s in range(out.shape[0]):
            moved = pltpu.roll(flags, LANES - s, 1) if s else flags
            keep[ab, s] = jnp.where(lane == 0, 1.0 - moved, 1.0)
    row = lax.broadcasted_iota(jnp.int32, (half, half), 0)
    col = lax.broadcasted_iota(jnp.int32, (half, half), 1)
    row = jnp.maximum(row, 1)
    pick = jnp.where(col == row, 1.0, 0.0).astype(BF16)
    flip = jnp.where(col == half - 1 - row, 1.0, 0.0).astype(BF16)
    for copy in copies:
        copy.wait()
    for s in range(out.shape[0]):
        out[s, :, :half] = jnp.dot(pick, left[s], preferred_element_type=F32).astype(BF16)
        out[s, :, half:] = jnp.dot(flip, lower[s], preferred_element_type=F32).astype(BF16)


def rows_product(rows, weights):
    return lax.dot_general(rows, weights, (((1,), (1,)), ((), ())), preferred_element_type=F32)


def both_sides(mine, theirs, weights):
    rows = jnp.concatenate(
        [jnp.concatenate([mine, theirs], 1), jnp.concatenate([theirs, mine], 1)], 0
    )
    return rows_product(rows, weights)


def store_run(state, s, begin, place, count, at, value, keep, half):
    total = value.shape[0] // 2
    for ab in range(2):
        part = value[ab * total + at * half : ab * total + (at + count) * half]
        state[ab, s, pl.ds(place * half, count * half), LANES:] = part[:, LANES:]
        for k in range(count):
            state[ab, s, pl.ds((place + k) * half, half), :LANES] = (
                part[k * half : (k + 1) * half, :LANES] * keep[ab, s, begin + k : begin + k + 1, :]
            )


def species_rows(ref, s, runs, half):
    if len(ref.shape) == 3:
        return ref[s]
    rows = sum(run[3] for run in runs) * half
    return ref[pl.ds(s * rows, rows), :]


def radial_kernel(plan, copies, half, weights, keep, *refs):
    n = len(plan)
    mines, theirs, refs = refs[:n], refs[n : 2 * n], refs[2 * n :]
    n_in = 1 + max((part for part, *_ in copies), default=-1)
    parts, states = refs[:n_in], refs[n_in:]
    for s in range(3):
        for k, runs in enumerate(plan):
            value = both_sides(
                species_rows(mines[k], s, runs, half),
                species_rows(theirs[k], s, runs, half),
                weights[s],
            )
            at = 0
            for which, begin, place, count in runs:
                store_run(states[which], s, begin, place, count, at, value, keep, half)
                at += count
    for part, source, which, place, count in copies:
        to, rows = pl.ds(place * half, count * half), pl.ds(source * half, count * half)
        for ab in range(2):
            for s in range(3):
                states[which][ab, s, to, :] = parts[part][ab, s, rows, :]


def edges_of_state(na, nz, planes, mid, mid_end, outer, edges, first, last, stage):
    half = nz // 2
    if planes == 2:
        row = jnp.where(lax.axis_index("ax") == 0, half // 2 - 1, half // 2)
    end = pl.ds((na - 1) * half, half)
    ends_end = pl.ds(mid_end.shape[2] - half, half)
    for ab in range(2):
        for s in range(3):
            for t in range(na):
                to = pl.ds(t, 1)
                at = t * half + half // 2
                if planes == 2:
                    stage[0, to, :] = outer[ab, s, pl.ds(t * half + row, 1), :]
                else:
                    stage[0, to, :] = outer[ab, s, at : at + 1, :]
                    stage[1, to, :] = outer[ab, s, at - 1 : at, :]
            for k, edge in enumerate(edges):
                edge[ab, s] = stage[k].astype(BF16)
            begin = pl.ds(0, half)
            first[ab, s] = pack([mid[ab, s, begin, :], outer[ab, s, begin, :]])
            last[ab, s] = pack([mid_end[ab, s, ends_end, :], outer[ab, s, end, :]])


def radial_edges_kernel(sizes, plan, copies, half, weights, keep, *refs):
    na, nz, planes = sizes
    n_edges = 1 if planes == 2 else 2
    *edges, first, last, stage = refs[-3 - n_edges :]
    refs = refs[: -3 - n_edges]
    radial_kernel(plan, copies, half, weights, keep, *refs)
    edges_of_state(na, nz, planes, refs[-2], refs[-2], refs[-1], edges, first, last, stage)


def explicit_angle(t, reader, low, high, edge_factors, coef, rows, nz):
    half = nz // 2
    for ab in range(2):
        out = second_step(
            functools.partial(reader, ab),
            lambda s: low[ab, s, pl.ds(t, 1), :] * edge_factors[0],
            lambda s: high[ab, s, pl.ds(t, 1), :] * edge_factors[1],
            coef,
            half,
        )
        width = out[0][0].shape[1]
        for s in range(3):
            rows[s, at_rows(t * nz, nz, nz), ab * width : (ab + 1) * width] = pack(
                [out[0][s], out[1][s]]
            )


def explicit_run(begin, count, states, low, high, edge_factors, coef, rows, nz):
    half = nz // 2

    def one(step, carry):
        t = begin + step

        def reader(ab, k, s, shift):
            state, base = states[k]
            return state[ab, s, at_rows((t - base + shift) * half, half, half), :]

        explicit_angle(t, reader, low, high, edge_factors, coef, rows, nz)
        return carry

    lax.fori_loop(0, count, one, 0)


def finish_run(begin, count, s, rows, weights, keep, result, nz):
    half = nz // 2
    value = rows_product(rows[s, pl.ds(begin * nz, count * nz), :], weights[s])
    for k in range(count):
        t = begin + k
        parts = turned(value[k * nz + half : (k + 1) * nz], value[k * nz : k * nz + half], half)
        for p in range(2):
            span = pl.ds(p * half, half)
            result[s, t, span, LANES:] = parts[p][:, LANES:]
            result[s, t, span, :LANES] = parts[p][:, :LANES] * keep[0, s, t : t + 1, :]


def widen(pairs):
    for source, target in pairs:
        target[...] = source[...].astype(F32)


def early_kernel(sizes, *refs):
    na, nz, runs, half_ring, planes = sizes
    (weights, keep, mid, outer, before_low, after_low, low_low, high_low, coef, out,
     before, after, low, high, rows, result, out_sems) = refs
    half = nz // 2
    place = lax.rem(lax.axis_index("ang"), half_ring)
    wrap_before = jnp.where(place == 0, 1, 0)
    wrap_after = jnp.where(place == half_ring - 1, 1, 0)
    factors = edge_weights(planes)
    widen(((low_low, low), (high_low, high)))
    for begin, count, base in runs:
        end = begin + count
        states = ((mid, base), (outer, 0))
        if begin == 0:
            widen(((before_low, before),))

            def reader(ab, k, s, shift):
                if shift == -1:
                    source = jnp.where(wrap_before == 1, 1 - ab, ab)
                    return before[source, s, pl.ds(k * half, half), :]
                return states[k][0][ab, s, pl.ds((shift - states[k][1]) * half, half), :]

            explicit_angle(0, reader, low, high, factors, coef, rows, nz)
        if end == na:
            widen(((after_low, after),))

            def reader(ab, k, s, shift):
                if shift == 1:
                    source = jnp.where(wrap_after == 1, 1 - ab, ab)
                    return after[source, s, pl.ds(k * half, half), :]
                return states[k][0][ab, s, pl.ds((na - 1 + shift - states[k][1]) * half, half), :]

            explicit_angle(na - 1, reader, low, high, factors, coef, rows, nz)
        start, stop = max(begin, 1), min(end, na - 1)
        if stop > start:
            explicit_run(start, stop - start, states, low, high, factors, coef, rows, nz)
    leaves = []
    for s in range(3):
        for k, (begin, count, _) in enumerate(runs):
            finish_run(begin, count, s, rows, weights, keep, result, nz)
            span = pl.ds(begin, count)
            leave = pltpu.make_async_copy(result.at[s, span], out.at[s, span], out_sems.at[k, s])
            leave.start()
            leaves.append(leave)
    for leave in leaves:
        leave.wait()


def late_kernel(
    sizes, given, state, weights, keep, mine, theirs, outer, low_low, high_low, coef,
    out, mid, low, high, rows, result, out_sems,
):
    na, nz, lo, hi, planes = sizes
    half = nz // 2
    factors = edge_weights(planes)
    count = hi - lo
    widen(((low_low, low), (high_low, high)))
    for s in range(3):
        value = both_sides(mine[s], theirs[s], weights[s])
        store_run(mid, s, lo, 2, count, 0, value, keep, half)
        for ab in range(2):
            for k in range(2):
                to = pl.ds((2 + count) * k * half, 2 * half)
                mid[ab, s, to, :] = state[ab, s, pl.ds((lo - 2 + 2 * k) * half, 2 * half), :]
    explicit_run(lo - 1, count + 2, ((mid, lo - 2), (outer, 0)), low, high, factors, coef, rows, nz)
    leaves = []
    for s in range(3):
        finish_run(lo - 1, count + 2, s, rows, weights, keep, result, nz)
        span = pl.ds(lo - 1, count + 2)
        leave = pltpu.make_async_copy(result.at[s, span], out.at[s, span], out_sems.at[s])
        leave.start()
        leaves.append(leave)
    for leave in leaves:
        leave.wait()


def ring(count, step):
    half = count // 2
    return [(i, i // half * half + (i % half + step) % half) for i in range(count)]


def plane_halos(edges, planes):
    if planes == 2:
        got = lax.ppermute(edges[0], "ax", [(0, 1), (1, 0)])
        return got, got
    up = [(i, i + 1) for i in range(planes - 1)]
    down = [(i + 1, i) for i in range(planes - 1)]
    return lax.ppermute(edges[1], "ax", up), lax.ppermute(edges[0], "ax", down)


def after(value, done):
    return lax.optimization_barrier((value, done))


def per_device(
    concentration, courant, axial_diffusion, angular_rate, rate_constants, species_map,
    wall_flags, radial_inverse,
):
    ns, na, nz, nr = concentration.shape
    half = nz // 2
    count = lax.axis_size("ang")
    planes = lax.axis_size("ax")
    n_edges = 1 if planes == 2 else 2
    quarter = na // 4
    ends = 2
    side = na // 2
    a_lo, a_cut, a_hi, x_hi = ends, ends + na // 4, side, na - ends
    opposite = [(i, (i + count // 2) % count) for i in range(count)]

    def dma(*dims):
        return pltpu.SemaphoreType.DMA(dims)

    def message(angles):
        return shape(ns, angles * half, nr, dtype=BF16)

    angle_before = lax.ppermute(
        concentration[:, na - 1], "ang", [(i, (i + 1) % count) for i in range(count)]
    )
    angle_after = lax.ppermute(
        concentration[:, 0], "ang", [(i, (i - 1) % count) for i in range(count)]
    )
    conc = concentration.reshape(ns, na * nz, nr)
    field = pltpu.VMEM((ns, na * nz, nr), F32)
    *edges, mid_a, coef = call(
        functools.partial(head_kernel, (na, nz, a_lo, a_cut, planes)),
        [shape(ns, na, nr)] * n_edges
        + [
            shape(ns * (a_cut - a_lo) * half + na, nr, dtype=BF16),
            shape(RATE + 3, half, nr),
        ],
        [HBM] * 7,
        [VM] * (n_edges + 2),
        [
            field, pltpu.VMEM((na, LANES), F32), pltpu.VMEM((1, nr), F32),
            pltpu.VMEM(angular_rate.shape, F32), pltpu.SMEM(axial_diffusion.shape, F32),
            pltpu.SMEM(rate_constants.shape, F32), pltpu.SMEM(species_map.shape, jnp.int32),
            pltpu.SMEM(wall_flags.shape, jnp.int32), dma(9),
        ],
        (conc, courant[None], axial_diffusion, angular_rate, rate_constants, species_map, wall_flags),
        58,
    )
    mid_a, (angle_before, angle_after) = after(mid_a, (angle_before, angle_after))
    opp_a = lax.ppermute(mid_a, "ang", opposite)
    low, high = plane_halos(edges, planes)
    bounds = (a_cut, a_hi, x_hi)
    mid_b, mid_x = call(
        functools.partial(
            inner_kernel,
            (na, nz),
            tuple((k, ((bounds[k], bounds[k + 1] - bounds[k]),)) for k in range(2)),
        ),
        [message(bounds[k + 1] - bounds[k]) for k in range(2)],
        [ANY, VM],
        [VM] * 2,
        [field, pltpu.SemaphoreType.DMA],
        (conc, coef),
        8,
    )
    opp_b = lax.ppermute(mid_b, "ang", opposite)
    out1, out2 = call(
        functools.partial(frame_kernel, (na, nz, ends, planes)),
        [message(na // 2), message(na // 2 + 2 * ends)],
        [ANY] * 3 + [VM] * 2 + [ANY],
        [VM] * 2,
        [pltpu.VMEM((ns, (na + 2) * nz, nr), F32), pltpu.VMEM((RATE + 3, half, nr), F32), dma(4)],
        (conc, angle_before, angle_after, low, high, coef),
        8,
    )
    out2, opp_a = after(out2, opp_a)
    opp_2 = lax.ppermute(out2, "ang", opposite)
    out1, opp_b = after(out1, opp_b)
    opp_1 = lax.ppermute(out1, "ang", opposite)

    weights, keep = call(
        weights_kernel,
        [shape(ns, nr, 2 * nr, dtype=BF16), shape(2, ns, na, LANES)],
        [ANY, VM, VM],
        [VM] * 2,
        [pltpu.VMEM((ns, nr, nr), BF16), pltpu.VMEM((ns, nr, nr), BF16), dma(2, ns)],
        (radial_inverse, mid_a, opp_a),
        12,
    )

    def state(angles):
        return shape(2, ns, angles * half, nr)

    count_a, count_b = a_cut - a_lo, a_hi - a_cut
    (mid_first,) = call(
        functools.partial(
            radial_kernel,
            (((0, a_lo, 0, count_a),), ((0, a_cut, count_a, count_b),)),
            (),
            half,
        ),
        [state(count_a + count_b)],
        [VM] * 6,
        [VM],
        [],
        (weights, keep, mid_a, mid_b, opp_a, opp_b),
        8,
    )
    opp_1, mid_first = after(opp_1, mid_first)
    mid_x, opp_1 = after(mid_x, opp_1)
    opp_x = lax.ppermute(mid_x, "ang", opposite)
    (outer_first,) = call(
        functools.partial(radial_kernel, (((0, 0, 0, side),),), (), half),
        [state(side)],
        [VM] * 4,
        [VM],
        [],
        (weights, keep, out1, opp_1),
        8,
    )
    plan = (((1, side, side, side), (0, 0, 0, ends), (0, na - ends, a_hi, ends)),)
    mid_left, outer_state, *rest = call(
        functools.partial(
            radial_edges_kernel,
            (na, nz, planes),
            plan,
            ((0, 0, 0, ends, count_a + count_b), (1, 0, 1, 0, side)),
            half,
        ),
        [state(a_hi + ends), state(na)]
        + [shape(2, ns, na, nr, dtype=BF16)] * n_edges
        + [shape(2, ns, nz, nr, dtype=BF16)] * 2,
        [VM] * 6,
        [VM] * (4 + n_edges),
        [pltpu.VMEM((n_edges, na, nr), F32)],
        (weights, keep, out2, opp_2, mid_first, outer_first),
        8,
    )
    *edges, first, last = rest
    low, high = plane_halos(edges, planes)
    angle_before = lax.ppermute(last, "ang", ring(count, 1))
    angle_after = lax.ppermute(first, "ang", ring(count, -1))
    stage = [pltpu.VMEM((ns, na * nz, 2 * nr), BF16), pltpu.VMEM((ns, na, nz, nr), F32)]
    edge_scratch = [pltpu.VMEM((2, ns, na, nr), F32)] * 2
    runs = ((0, a_hi - 1, 0), (na - 1, 1, na - ends - a_hi))
    partial = call(
        functools.partial(early_kernel, (na, nz, runs, count // 2, planes)),
        shape(ns, na, nz, nr),
        [VM] * 9,
        ANY,
        [pltpu.VMEM((2, ns, nz, nr), F32)] * 2 + edge_scratch + stage + [dma(len(runs), ns)],
        (weights, keep, mid_left, outer_state, angle_before, angle_after, low, high, coef),
        12,
    )
    wide = x_hi - a_hi + 4
    return call(
        functools.partial(late_kernel, (na, nz, a_hi, x_hi, planes)),
        shape(ns, na, nz, nr),
        [ANY] + [VM] * 9,
        ANY,
        [pltpu.VMEM((2, ns, wide * half, nr), F32)] + edge_scratch + stage + [dma(ns)],
        (partial, mid_left, weights, keep, mid_x, opp_x, outer_state, low, high, coef),
        12,
        {0: 0},
    )


def solution(mesh):
    in_specs = (P(None, "ang", "ax", None), P(), P(), P(), P(), P(), P(None, "ang"), P())
    out_specs = P(None, "ang", "ax", None)
    return jax.shard_map(
        per_device, mesh=mesh, in_specs=in_specs, out_specs=out_specs, check_vma=False
    )
```

```python
import functools

import jax
import jax.numpy as jnp
from jax import lax
from jax.experimental import pallas as pl
from jax.experimental.pallas import tpu as pltpu
from jax.sharding import PartitionSpec as P

F32 = jnp.float32
BF16 = jnp.bfloat16
MIB = 1024 * 1024
LANES = 128

ANY = pl.BlockSpec(memory_space=pl.ANY)
HBM = pl.BlockSpec(memory_space=pltpu.HBM)
VM = pl.BlockSpec(memory_space=pltpu.VMEM)
SM = pl.BlockSpec(memory_space=pltpu.SMEM)

OWN, BEFORE, ANGULAR, AXIAL, RATE = 0, 3, 6, 9, 12


def call(body, out_shape, in_specs, out_specs, scratch, args, mib, aliases=None):
    return pl.pallas_call(
        body,
        out_shape=out_shape,
        in_specs=in_specs,
        out_specs=out_specs,
        scratch_shapes=scratch,
        input_output_aliases=aliases or {},
        cost_estimate=pl.CostEstimate(flops=1, bytes_accessed=1, transcendentals=0),
        compiler_params=pltpu.CompilerParams(vmem_limit_bytes=mib * MIB),
    )(*args)


def shape(*dims, dtype=F32):
    return jax.ShapeDtypeStruct(dims, dtype)


def transport(now, before, after, around, coef):
    made = (
        coef[RATE] * (now[1] * now[2]),
        coef[RATE + 1] * (now[0] * now[2]),
        coef[RATE + 2] * (now[0] * now[1]),
    )
    spent = made[0] + made[1] + made[2]
    out = []
    for s in range(3):
        value = now[s] * coef[OWN + s] + before[s] * coef[BEFORE + s]
        value = value + after[s] * coef[AXIAL + s] + around[s] * coef[ANGULAR + s]
        out.append(value + ((made[s] + made[s]) - spent))
    return out


def turned(first, second, rows):
    first, second = pltpu.roll(first, rows // 2, 0), pltpu.roll(second, rows // 2, 0)
    upper = lax.broadcasted_iota(jnp.int32, first.shape, 0) < rows // 2
    return jnp.where(upper, first, second), jnp.where(upper, second, first)


def first_step(read, low, high, coef, half):
    tiles = [[read(s, 0, k) for s in range(3)] for k in range(2)]
    around = [[read(s, -1, k) + read(s, 1, k) for s in range(3)] for k in range(2)]
    row = lax.broadcasted_iota(jnp.int32, tiles[0][0].shape, 0)
    top, bottom = row == 0, row == half - 1
    fall = [[pltpu.roll(v, 1, 0) for v in tile] for tile in tiles]
    rise = [[pltpu.roll(v, half - 1, 0) for v in tile] for tile in tiles]
    out = []
    for k in range(2):
        other = 1 - k
        before = [
            jnp.where(top, low(s) if low is not None and k == 0 else fall[other][s], fall[k][s])
            for s in range(3)
        ]
        after = [
            jnp.where(bottom, high(s) if high is not None and k == 1 else rise[other][s], rise[k][s])
            for s in range(3)
        ]
        out.append(transport(tiles[k], before, after, around[k], coef))
    pairs = [turned(out[0][s], out[1][s], half) for s in range(3)]
    return [p[0] for p in pairs], [p[1] for p in pairs]


def second_step(read, low, high, coef, half):
    tiles = [[read(k, s, 0) for s in range(3)] for k in range(2)]
    around = [[read(k, s, -1) + read(k, s, 1) for s in range(3)] for k in range(2)]
    row = lax.broadcasted_iota(jnp.int32, tiles[0][0].shape, 0)
    top, bottom = row == 0, row == half - 1
    first, last = row == half // 2, row == half // 2 - 1
    fall = [[pltpu.roll(v, 1, 0) for v in tile] for tile in tiles]
    rise = [[pltpu.roll(v, half - 1, 0) for v in tile] for tile in tiles]
    out = []
    for k in range(2):
        before = [jnp.where(top, fall[1 - k][s], fall[k][s]) for s in range(3)]
        after = [jnp.where(bottom, rise[1 - k][s], rise[k][s]) for s in range(3)]
        if k == 1:
            before = [jnp.where(first, low(s), before[s]) for s in range(3)]
            after = [jnp.where(last, high(s), after[s]) for s in range(3)]
        out.append(transport(tiles[k], before, after, around[k], coef))
    return out


def pack(tiles):
    return jnp.concatenate(tiles, 0).astype(BF16)


def at_rows(start, count, step):
    return pl.ds(pl.multiple_of(start, step), count)


def field_reader(field, t, nz):
    half = nz // 2
    return lambda s, shift, k: field[s, at_rows((t + shift) * nz + k * half, half, half), :]


def mid_run(field, out_of, begin, count, at, coef, nz):
    half = nz // 2

    def pair(step, carry):
        t = begin + step * 2
        tiles = [first_step(field_reader(field, t + k, nz), None, None, coef, half)[0] for k in range(2)]
        for s in range(3):
            out_of(s)[at_rows(at * half + step * nz, nz, nz), :] = pack([tiles[0][s], tiles[1][s]])
        return carry

    lax.fori_loop(0, count // 2, pair, 0)


def head_kernel(sizes, conc, cour, diff, ang, rate, smap, flags, *rest):
    na, nz, lo, hi, planes = sizes
    edges = rest[: 1 if planes == 2 else 2]
    mid, coef, field, flag_v, cour_v, ang_v, diff_s, rate_s, map_s, flags_s, sems = rest[
        len(edges) :
    ]
    half = nz // 2
    inner = pl.ds((lo - 1) * nz, (hi - lo + 2) * nz)
    left = pl.ds(0, (lo - 1) * nz)
    right = pl.ds((hi + 1) * nz, (na - hi - 1) * nz)
    small = [
        pltpu.make_async_copy(src, dst, sems.at[k + 3])
        for k, (src, dst) in enumerate(
            ((cour, cour_v), (ang, ang_v), (diff, diff_s), (rate, rate_s), (smap, map_s), (flags, flags_s))
        )
    ]
    copies = [
        pltpu.make_async_copy(conc.at[:, rows], field.at[:, rows], sems.at[k])
        for k, rows in enumerate((inner, left, right))
    ]
    for copy in small + copies:
        copy.start()
    for copy in small:
        copy.wait()
    tile = coef.shape[1:]
    for s in range(3):
        courant, angular = cour_v[...], ang_v[s : s + 1, :]
        axial = diff_s[s]
        total = jnp.float32(0.0)
        for k in range(map_s.shape[0]):
            total = total + jnp.where(map_s[k, 2] == s, rate_s[k], 0.0)
        coef[OWN + s] = jnp.broadcast_to((1.0 - 2.0 * axial) - courant - 2.0 * angular, tile)
        coef[BEFORE + s] = jnp.broadcast_to(courant + axial, tile)
        coef[ANGULAR + s] = jnp.broadcast_to(angular, tile)
        coef[AXIAL + s] = jnp.full(tile, axial, F32)
        coef[RATE + s] = jnp.full(tile, total, F32)
    lane = lax.broadcasted_iota(jnp.int32, (1, LANES), 1)
    for t in range(na):
        row = jnp.zeros((1, LANES), jnp.int32)
        for s in range(3):
            row = jnp.where(lane == s, flags_s[s, t], row)
        flag_v[t : t + 1, :] = row.astype(F32)
    rows = (hi - lo) * half
    span = pl.ds(3 * rows, na)
    mid[span, :] = jnp.zeros((na, mid.shape[1]), BF16)
    mid[span, :LANES] = flag_v[...].astype(BF16)
    copies[0].wait()
    mid_run(field, lambda s: mid.at[pl.ds(s * rows, rows)], lo, hi - lo, 0, coef, nz)
    copies[1].wait()
    copies[2].wait()
    for s in range(3):
        if planes == 2:
            row = jnp.where(lax.axis_index("ax") == 0, nz - 1, 0)
            for t in range(na):
                edges[0][s, t : t + 1, :] = field[s, pl.ds(t * nz + row, 1), :]
        else:
            for t in range(na):
                edges[0][s, t : t + 1, :] = field[s, t * nz : t * nz + 1, :]
                edges[1][s, t : t + 1, :] = field[s, (t + 1) * nz - 1 : (t + 1) * nz, :]


def inner_kernel(sizes, runs, conc, coef, *rest):
    na, nz = sizes
    outs, field, sem = rest[:-2], rest[-2], rest[-1]
    copy = pltpu.make_async_copy(conc, field, sem)
    copy.start()
    copy.wait()
    for out, parts in runs:
        at = 0
        for begin, count in parts:
            mid_run(field, outs[out].at.__getitem__, begin, count, at, coef, nz)
            at += count


def edge_weights(planes):
    if planes != 2:
        return 1.0, 1.0
    place = lax.axis_index("ax")
    return jnp.where(place == 1, 1.0, 0.0), jnp.where(place == 0, 1.0, 0.0)


def frame_kernel(
    sizes, conc, before, after, low, high, coef_in, out1, out2, field, coef, sems
):
    na, nz, ends, planes = sizes
    half = nz // 2
    copies = [
        pltpu.make_async_copy(conc, field.at[:, pl.ds(nz, na * nz)], sems.at[0]),
        pltpu.make_async_copy(before, field.at[:, pl.ds(0, nz)], sems.at[1]),
        pltpu.make_async_copy(after, field.at[:, pl.ds((na + 1) * nz, nz)], sems.at[2]),
        pltpu.make_async_copy(coef_in, coef, sems.at[3]),
    ]
    for copy in copies:
        copy.start()
    low_weight, high_weight = edge_weights(planes)
    for copy in copies:
        copy.wait()

    def angle(t):
        return first_step(
            field_reader(field, t + 1, nz),
            lambda s: low[s, pl.ds(t, 1), :] * low_weight,
            lambda s: high[s, pl.ds(t, 1), :] * high_weight,
            coef,
            half,
        )

    def pair(t, out, row, ends_row):
        tiles = [angle(t), angle(t + 1)]
        for s in range(3):
            out[s, pl.ds(row, nz), :] = pack([tiles[0][1][s], tiles[1][1][s]])
            if ends_row is not None:
                out2[s, pl.ds(ends_row, nz), :] = pack([tiles[0][0][s], tiles[1][0][s]])

    quarter = na // 4
    tail = na // 2 * half
    pair(0, out1, 0, tail)
    pair(na - 2, out2, (na // 2 - 2) * half, tail + nz)

    def first_part(step, carry):
        pair(step * 2, out1, pl.multiple_of(step * nz, nz), None)
        return carry

    def second_part(step, carry):
        pair(na // 2 + step * 2, out2, pl.multiple_of(step * nz, nz), None)
        return carry

    lax.fori_loop(1, quarter, first_part, 0)
    lax.fori_loop(0, quarter - 1, second_part, 0)


def weights_kernel(matrix, mine, theirs, out, keep, left, lower, sems):
    half = out.shape[1]
    copies = []
    for s in range(out.shape[0]):
        for k, ref in enumerate((left, lower)):
            src = matrix.at[s, pl.ds(k * half, half), pl.ds(0, half)]
            copies.append(pltpu.make_async_copy(src, ref.at[s], sems.at[k, s]))
    for copy in copies:
        copy.start()
    na = keep.shape[2]
    lane = lax.broadcasted_iota(jnp.int32, (na, LANES), 1)
    for ab, ref in enumerate((mine, theirs)):
        flags = ref[pl.ds(ref.shape[0] - na, na), :LANES].astype(F32)
        for s in range(out.shape[0]):
            moved = pltpu.roll(flags, LANES - s, 1) if s else flags
            keep[ab, s] = jnp.where(lane == 0, 1.0 - moved, 1.0)
    row = lax.broadcasted_iota(jnp.int32, (half, half), 0)
    col = lax.broadcasted_iota(jnp.int32, (half, half), 1)
    row = jnp.maximum(row, 1)
    pick = jnp.where(col == row, 1.0, 0.0).astype(BF16)
    flip = jnp.where(col == half - 1 - row, 1.0, 0.0).astype(BF16)
    for copy in copies:
        copy.wait()
    for s in range(out.shape[0]):
        out[s, :, :half] = jnp.dot(pick, left[s], preferred_element_type=F32).astype(BF16)
        out[s, :, half:] = jnp.dot(flip, lower[s], preferred_element_type=F32).astype(BF16)


def rows_product(rows, weights):
    return lax.dot_general(rows, weights, (((1,), (1,)), ((), ())), preferred_element_type=F32)


def both_sides(mine, theirs, weights):
    rows = jnp.concatenate(
        [jnp.concatenate([mine, theirs], 1), jnp.concatenate([theirs, mine], 1)], 0
    )
    return rows_product(rows, weights)


def store_run(state, s, begin, place, count, at, value, keep, half):
    total = value.shape[0] // 2
    for ab in range(2):
        part = value[ab * total + at * half : ab * total + (at + count) * half]
        state[ab, s, pl.ds(place * half, count * half), LANES:] = part[:, LANES:]
        for k in range(count):
            state[ab, s, pl.ds((place + k) * half, half), :LANES] = (
                part[k * half : (k + 1) * half, :LANES] * keep[ab, s, begin + k : begin + k + 1, :]
            )


def species_rows(ref, s, runs, half):
    if len(ref.shape) == 3:
        return ref[s]
    rows = sum(run[3] for run in runs) * half
    return ref[pl.ds(s * rows, rows), :]


def radial_kernel(plan, copies, half, weights, keep, *refs):
    n = len(plan)
    mines, theirs, refs = refs[:n], refs[n : 2 * n], refs[2 * n :]
    n_in = 1 + max((part for part, *_ in copies), default=-1)
    parts, states = refs[:n_in], refs[n_in:]
    for s in range(3):
        for k, runs in enumerate(plan):
            value = both_sides(
                species_rows(mines[k], s, runs, half),
                species_rows(theirs[k], s, runs, half),
                weights[s],
            )
            at = 0
            for which, begin, place, count in runs:
                store_run(states[which], s, begin, place, count, at, value, keep, half)
                at += count
    for part, source, which, place, count in copies:
        to, rows = pl.ds(place * half, count * half), pl.ds(source * half, count * half)
        for ab in range(2):
            for s in range(3):
                states[which][ab, s, to, :] = parts[part][ab, s, rows, :]


def edges_of_state(na, nz, planes, mid, mid_end, outer, edges, first, last, stage):
    half = nz // 2
    if planes == 2:
        row = jnp.where(lax.axis_index("ax") == 0, half // 2 - 1, half // 2)
    end = pl.ds((na - 1) * half, half)
    ends_end = pl.ds(mid_end.shape[2] - half, half)
    for ab in range(2):
        for s in range(3):
            for t in range(na):
                to = pl.ds(t, 1)
                at = t * half + half // 2
                if planes == 2:
                    stage[0, to, :] = outer[ab, s, pl.ds(t * half + row, 1), :]
                else:
                    stage[0, to, :] = outer[ab, s, at : at + 1, :]
                    stage[1, to, :] = outer[ab, s, at - 1 : at, :]
            for k, edge in enumerate(edges):
                edge[ab, s] = stage[k].astype(BF16)
            begin = pl.ds(0, half)
            first[ab, s] = pack([mid[ab, s, begin, :], outer[ab, s, begin, :]])
            last[ab, s] = pack([mid_end[ab, s, ends_end, :], outer[ab, s, end, :]])


def radial_edges_kernel(sizes, plan, copies, half, weights, keep, *refs):
    na, nz, planes = sizes
    n_edges = 1 if planes == 2 else 2
    *edges, first, last, stage = refs[-3 - n_edges :]
    refs = refs[: -3 - n_edges]
    radial_kernel(plan, copies, half, weights, keep, *refs)
    edges_of_state(na, nz, planes, refs[-2], refs[-2], refs[-1], edges, first, last, stage)


def explicit_angle(t, reader, low, high, edge_factors, coef, rows, nz):
    half = nz // 2
    for ab in range(2):
        out = second_step(
            functools.partial(reader, ab),
            lambda s: low[ab, s, pl.ds(t, 1), :] * edge_factors[0],
            lambda s: high[ab, s, pl.ds(t, 1), :] * edge_factors[1],
            coef,
            half,
        )
        width = out[0][0].shape[1]
        for s in range(3):
            rows[s, at_rows(t * nz, nz, nz), ab * width : (ab + 1) * width] = pack(
                [out[0][s], out[1][s]]
            )


def explicit_run(begin, count, states, low, high, edge_factors, coef, rows, nz):
    half = nz // 2

    def one(step, carry):
        t = begin + step

        def reader(ab, k, s, shift):
            state, base = states[k]
            return state[ab, s, at_rows((t - base + shift) * half, half, half), :]

        explicit_angle(t, reader, low, high, edge_factors, coef, rows, nz)
        return carry

    lax.fori_loop(0, count, one, 0)


def finish_run(begin, count, s, rows, weights, keep, result, nz):
    half = nz // 2
    value = rows_product(rows[s, pl.ds(begin * nz, count * nz), :], weights[s])
    for k in range(count):
        t = begin + k
        parts = turned(value[k * nz + half : (k + 1) * nz], value[k * nz : k * nz + half], half)
        for p in range(2):
            span = pl.ds(p * half, half)
            result[s, t, span, LANES:] = parts[p][:, LANES:]
            result[s, t, span, :LANES] = parts[p][:, :LANES] * keep[0, s, t : t + 1, :]


def widen(pairs):
    for source, target in pairs:
        target[...] = source[...].astype(F32)


def early_kernel(sizes, *refs):
    na, nz, runs, half_ring, planes = sizes
    (weights, keep, mid, outer, before_low, after_low, low_low, high_low, coef, out,
     before, after, low, high, rows, result, out_sems) = refs
    half = nz // 2
    place = lax.rem(lax.axis_index("ang"), half_ring)
    wrap_before = jnp.where(place == 0, 1, 0)
    wrap_after = jnp.where(place == half_ring - 1, 1, 0)
    factors = edge_weights(planes)
    widen(((low_low, low), (high_low, high)))
    for begin, count, base in runs:
        end = begin + count
        states = ((mid, base), (outer, 0))
        if begin == 0:
            widen(((before_low, before),))

            def reader(ab, k, s, shift):
                if shift == -1:
                    source = jnp.where(wrap_before == 1, 1 - ab, ab)
                    return before[source, s, pl.ds(k * half, half), :]
                return states[k][0][ab, s, pl.ds((shift - states[k][1]) * half, half), :]

            explicit_angle(0, reader, low, high, factors, coef, rows, nz)
        if end == na:
            widen(((after_low, after),))

            def reader(ab, k, s, shift):
                if shift == 1:
                    source = jnp.where(wrap_after == 1, 1 - ab, ab)
                    return after[source, s, pl.ds(k * half, half), :]
                return states[k][0][ab, s, pl.ds((na - 1 + shift - states[k][1]) * half, half), :]

            explicit_angle(na - 1, reader, low, high, factors, coef, rows, nz)
        start, stop = max(begin, 1), min(end, na - 1)
        if stop > start:
            explicit_run(start, stop - start, states, low, high, factors, coef, rows, nz)
    leaves = []
    for s in range(3):
        for k, (begin, count, _) in enumerate(runs):
            finish_run(begin, count, s, rows, weights, keep, result, nz)
            span = pl.ds(begin, count)
            leave = pltpu.make_async_copy(result.at[s, span], out.at[s, span], out_sems.at[k, s])
            leave.start()
            leaves.append(leave)
    for leave in leaves:
        leave.wait()


def late_kernel(
    sizes, given, state, weights, keep, mine, theirs, outer, low_low, high_low, coef,
    out, mid, low, high, rows, result, out_sems,
):
    na, nz, lo, hi, planes = sizes
    half = nz // 2
    factors = edge_weights(planes)
    count = hi - lo
    widen(((low_low, low), (high_low, high)))
    for s in range(3):
        value = both_sides(mine[s], theirs[s], weights[s])
        store_run(mid, s, lo, 2, count, 0, value, keep, half)
        for ab in range(2):
            for k in range(2):
                to = pl.ds((2 + count) * k * half, 2 * half)
                mid[ab, s, to, :] = state[ab, s, pl.ds((lo - 2 + 2 * k) * half, 2 * half), :]
    explicit_run(lo - 1, count + 2, ((mid, lo - 2), (outer, 0)), low, high, factors, coef, rows, nz)
    leaves = []
    for s in range(3):
        finish_run(lo - 1, count + 2, s, rows, weights, keep, result, nz)
        span = pl.ds(lo - 1, count + 2)
        leave = pltpu.make_async_copy(result.at[s, span], out.at[s, span], out_sems.at[s])
        leave.start()
        leaves.append(leave)
    for leave in leaves:
        leave.wait()


def ring(count, step):
    half = count // 2
    return [(i, i // half * half + (i % half + step) % half) for i in range(count)]


def plane_halos(edges, planes):
    if planes == 2:
        got = lax.ppermute(edges[0], "ax", [(0, 1), (1, 0)])
        return got, got
    up = [(i, i + 1) for i in range(planes - 1)]
    down = [(i + 1, i) for i in range(planes - 1)]
    return lax.ppermute(edges[1], "ax", up), lax.ppermute(edges[0], "ax", down)


def after(value, done):
    return lax.optimization_barrier((value, done))


def per_device(
    concentration, courant, axial_diffusion, angular_rate, rate_constants, species_map,
    wall_flags, radial_inverse,
):
    ns, na, nz, nr = concentration.shape
    half = nz // 2
    count = lax.axis_size("ang")
    planes = lax.axis_size("ax")
    n_edges = 1 if planes == 2 else 2
    quarter = na // 4
    ends = 2
    side = na // 2
    a_lo, a_cut, a_hi, x_hi = ends, ends + na // 4, side + ends, na - ends
    opposite = [(i, (i + count // 2) % count) for i in range(count)]

    def dma(*dims):
        return pltpu.SemaphoreType.DMA(dims)

    def message(angles):
        return shape(ns, angles * half, nr, dtype=BF16)

    angle_before = lax.ppermute(
        concentration[:, na - 1], "ang", [(i, (i + 1) % count) for i in range(count)]
    )
    angle_after = lax.ppermute(
        concentration[:, 0], "ang", [(i, (i - 1) % count) for i in range(count)]
    )
    conc = concentration.reshape(ns, na * nz, nr)
    field = pltpu.VMEM((ns, na * nz, nr), F32)
    *edges, mid_a, coef = call(
        functools.partial(head_kernel, (na, nz, a_lo, a_cut, planes)),
        [shape(ns, na, nr)] * n_edges
        + [
            shape(ns * (a_cut - a_lo) * half + na, nr, dtype=BF16),
            shape(RATE + 3, half, nr),
        ],
        [HBM] * 7,
        [VM] * (n_edges + 2),
        [
            field, pltpu.VMEM((na, LANES), F32), pltpu.VMEM((1, nr), F32),
            pltpu.VMEM(angular_rate.shape, F32), pltpu.SMEM(axial_diffusion.shape, F32),
            pltpu.SMEM(rate_constants.shape, F32), pltpu.SMEM(species_map.shape, jnp.int32),
            pltpu.SMEM(wall_flags.shape, jnp.int32), dma(9),
        ],
        (conc, courant[None], axial_diffusion, angular_rate, rate_constants, species_map, wall_flags),
        58,
    )
    mid_a, (angle_before, angle_after) = after(mid_a, (angle_before, angle_after))
    opp_a = lax.ppermute(mid_a, "ang", opposite)
    low, high = plane_halos(edges, planes)
    bounds = (a_cut, a_hi, x_hi)
    mid_b, mid_x = call(
        functools.partial(
            inner_kernel,
            (na, nz),
            tuple((k, ((bounds[k], bounds[k + 1] - bounds[k]),)) for k in range(2)),
        ),
        [message(bounds[k + 1] - bounds[k]) for k in range(2)],
        [ANY, VM],
        [VM] * 2,
        [field, pltpu.SemaphoreType.DMA],
        (conc, coef),
        8,
    )
    opp_b = lax.ppermute(mid_b, "ang", opposite)
    out1, out2 = call(
        functools.partial(frame_kernel, (na, nz, ends, planes)),
        [message(na // 2), message(na // 2 + 2 * ends)],
        [ANY] * 3 + [VM] * 2 + [ANY],
        [VM] * 2,
        [pltpu.VMEM((ns, (na + 2) * nz, nr), F32), pltpu.VMEM((RATE + 3, half, nr), F32), dma(4)],
        (conc, angle_before, angle_after, low, high, coef),
        8,
    )
    out2, opp_a = after(out2, opp_a)
    opp_2 = lax.ppermute(out2, "ang", opposite)
    out1, opp_b = after(out1, opp_b)
    opp_1 = lax.ppermute(out1, "ang", opposite)

    weights, keep = call(
        weights_kernel,
        [shape(ns, nr, 2 * nr, dtype=BF16), shape(2, ns, na, LANES)],
        [ANY, VM, VM],
        [VM] * 2,
        [pltpu.VMEM((ns, nr, nr), BF16), pltpu.VMEM((ns, nr, nr), BF16), dma(2, ns)],
        (radial_inverse, mid_a, opp_a),
        12,
    )

    def state(angles):
        return shape(2, ns, angles * half, nr)

    count_a, count_b = a_cut - a_lo, a_hi - a_cut
    (mid_first,) = call(
        functools.partial(
            radial_kernel,
            (((0, a_lo, 0, count_a),), ((0, a_cut, count_a, count_b),)),
            (),
            half,
        ),
        [state(count_a + count_b)],
        [VM] * 6,
        [VM],
        [],
        (weights, keep, mid_a, mid_b, opp_a, opp_b),
        8,
    )
    opp_1, mid_first = after(opp_1, mid_first)
    mid_x, (opp_1, opp_2) = after(mid_x, (opp_1, opp_2))
    opp_x = lax.ppermute(mid_x, "ang", opposite)
    (outer_first,) = call(
        functools.partial(radial_kernel, (((0, 0, 0, side),),), (), half),
        [state(side)],
        [VM] * 4,
        [VM],
        [],
        (weights, keep, out1, opp_1),
        8,
    )
    plan = (((1, side, side, side), (0, 0, 0, ends), (0, na - ends, a_hi, ends)),)
    mid_left, outer_state, *rest = call(
        functools.partial(
            radial_edges_kernel,
            (na, nz, planes),
            plan,
            ((0, 0, 0, ends, count_a + count_b), (1, 0, 1, 0, side)),
            half,
        ),
        [state(a_hi + ends), state(na)]
        + [shape(2, ns, na, nr, dtype=BF16)] * n_edges
        + [shape(2, ns, nz, nr, dtype=BF16)] * 2,
        [VM] * 6,
        [VM] * (4 + n_edges),
        [pltpu.VMEM((n_edges, na, nr), F32)],
        (weights, keep, out2, opp_2, mid_first, outer_first),
        8,
    )
    *edges, first, last = rest
    low, high = plane_halos(edges, planes)
    angle_before = lax.ppermute(last, "ang", ring(count, 1))
    angle_after = lax.ppermute(first, "ang", ring(count, -1))
    stage = [pltpu.VMEM((ns, na * nz, 2 * nr), BF16), pltpu.VMEM((ns, na, nz, nr), F32)]
    edge_scratch = [pltpu.VMEM((2, ns, na, nr), F32)] * 2
    runs = ((0, a_hi - 1, 0), (na - 1, 1, na - ends - a_hi))
    partial = call(
        functools.partial(early_kernel, (na, nz, runs, count // 2, planes)),
        shape(ns, na, nz, nr),
        [VM] * 9,
        ANY,
        [pltpu.VMEM((2, ns, nz, nr), F32)] * 2 + edge_scratch + stage + [dma(len(runs), ns)],
        (weights, keep, mid_left, outer_state, angle_before, angle_after, low, high, coef),
        12,
    )
    wide = x_hi - a_hi + 4
    return call(
        functools.partial(late_kernel, (na, nz, a_hi, x_hi, planes)),
        shape(ns, na, nz, nr),
        [ANY] + [VM] * 9,
        ANY,
        [pltpu.VMEM((2, ns, wide * half, nr), F32)] + edge_scratch + stage + [dma(ns)],
        (partial, mid_left, weights, keep, mid_x, opp_x, outer_state, low, high, coef),
        12,
        {0: 0},
    )


def solution(mesh):
    in_specs = (P(None, "ang", "ax", None), P(), P(), P(), P(), P(), P(None, "ang"), P())
    out_specs = P(None, "ang", "ax", None)
    return jax.shard_map(
        per_device, mesh=mesh, in_specs=in_specs, out_specs=out_specs, check_vma=False
    )
```

```python
import functools

import jax
import jax.numpy as jnp
from jax import lax
from jax.experimental import pallas as pl
from jax.experimental.pallas import tpu as pltpu
from jax.sharding import PartitionSpec as P

F32 = jnp.float32
BF16 = jnp.bfloat16
MIB = 1024 * 1024
LANES = 128

ANY = pl.BlockSpec(memory_space=pl.ANY)
HBM = pl.BlockSpec(memory_space=pltpu.HBM)
VM = pl.BlockSpec(memory_space=pltpu.VMEM)
SM = pl.BlockSpec(memory_space=pltpu.SMEM)

OWN, BEFORE, ANGULAR, AXIAL, RATE = 0, 3, 6, 9, 12


def call(body, out_shape, in_specs, out_specs, scratch, args, mib, aliases=None):
    return pl.pallas_call(
        body,
        out_shape=out_shape,
        in_specs=in_specs,
        out_specs=out_specs,
        scratch_shapes=scratch,
        input_output_aliases=aliases or {},
        cost_estimate=pl.CostEstimate(flops=1, bytes_accessed=1, transcendentals=0),
        compiler_params=pltpu.CompilerParams(vmem_limit_bytes=mib * MIB),
    )(*args)


def shape(*dims, dtype=F32):
    return jax.ShapeDtypeStruct(dims, dtype)


def transport(now, before, after, around, coef):
    made = (
        coef[RATE] * (now[1] * now[2]),
        coef[RATE + 1] * (now[0] * now[2]),
        coef[RATE + 2] * (now[0] * now[1]),
    )
    spent = made[0] + made[1] + made[2]
    out = []
    for s in range(3):
        value = now[s] * coef[OWN + s] + before[s] * coef[BEFORE + s]
        value = value + after[s] * coef[AXIAL + s] + around[s] * coef[ANGULAR + s]
        out.append(value + ((made[s] + made[s]) - spent))
    return out


def turned(first, second, rows):
    first, second = pltpu.roll(first, rows // 2, 0), pltpu.roll(second, rows // 2, 0)
    upper = lax.broadcasted_iota(jnp.int32, first.shape, 0) < rows // 2
    return jnp.where(upper, first, second), jnp.where(upper, second, first)


def first_step(read, low, high, coef, half):
    tiles = [[read(s, 0, k) for s in range(3)] for k in range(2)]
    around = [[read(s, -1, k) + read(s, 1, k) for s in range(3)] for k in range(2)]
    row = lax.broadcasted_iota(jnp.int32, tiles[0][0].shape, 0)
    top, bottom = row == 0, row == half - 1
    fall = [[pltpu.roll(v, 1, 0) for v in tile] for tile in tiles]
    rise = [[pltpu.roll(v, half - 1, 0) for v in tile] for tile in tiles]
    out = []
    for k in range(2):
        other = 1 - k
        before = [
            jnp.where(top, low(s) if low is not None and k == 0 else fall[other][s], fall[k][s])
            for s in range(3)
        ]
        after = [
            jnp.where(bottom, high(s) if high is not None and k == 1 else rise[other][s], rise[k][s])
            for s in range(3)
        ]
        out.append(transport(tiles[k], before, after, around[k], coef))
    pairs = [turned(out[0][s], out[1][s], half) for s in range(3)]
    return [p[0] for p in pairs], [p[1] for p in pairs]


def second_step(read, low, high, coef, half):
    tiles = [[read(k, s, 0) for s in range(3)] for k in range(2)]
    around = [[read(k, s, -1) + read(k, s, 1) for s in range(3)] for k in range(2)]
    row = lax.broadcasted_iota(jnp.int32, tiles[0][0].shape, 0)
    top, bottom = row == 0, row == half - 1
    first, last = row == half // 2, row == half // 2 - 1
    fall = [[pltpu.roll(v, 1, 0) for v in tile] for tile in tiles]
    rise = [[pltpu.roll(v, half - 1, 0) for v in tile] for tile in tiles]
    out = []
    for k in range(2):
        before = [jnp.where(top, fall[1 - k][s], fall[k][s]) for s in range(3)]
        after = [jnp.where(bottom, rise[1 - k][s], rise[k][s]) for s in range(3)]
        if k == 1:
            before = [jnp.where(first, low(s), before[s]) for s in range(3)]
            after = [jnp.where(last, high(s), after[s]) for s in range(3)]
        out.append(transport(tiles[k], before, after, around[k], coef))
    return out


def pack(tiles):
    return jnp.concatenate(tiles, 0).astype(BF16)


def at_rows(start, count, step):
    return pl.ds(pl.multiple_of(start, step), count)


def field_reader(field, t, nz):
    half = nz // 2
    return lambda s, shift, k: field[s, at_rows((t + shift) * nz + k * half, half, half), :]


def mid_run(field, out_of, begin, count, at, coef, nz):
    half = nz // 2

    def pair(step, carry):
        t = begin + step * 2
        tiles = [first_step(field_reader(field, t + k, nz), None, None, coef, half)[0] for k in range(2)]
        for s in range(3):
            out_of(s)[at_rows(at * half + step * nz, nz, nz), :] = pack([tiles[0][s], tiles[1][s]])
        return carry

    lax.fori_loop(0, count // 2, pair, 0)


def head_kernel(sizes, conc, cour, diff, ang, rate, smap, flags, *rest):
    na, nz, lo, hi, planes = sizes
    edges = rest[: 1 if planes == 2 else 2]
    mid, coef, field, flag_v, cour_v, ang_v, diff_s, rate_s, map_s, flags_s, sems = rest[
        len(edges) :
    ]
    half = nz // 2
    inner = pl.ds((lo - 1) * nz, (hi - lo + 2) * nz)
    left = pl.ds(0, (lo - 1) * nz)
    right = pl.ds((hi + 1) * nz, (na - hi - 1) * nz)
    small = [
        pltpu.make_async_copy(src, dst, sems.at[k + 3])
        for k, (src, dst) in enumerate(
            ((cour, cour_v), (ang, ang_v), (diff, diff_s), (rate, rate_s), (smap, map_s), (flags, flags_s))
        )
    ]
    copies = [
        pltpu.make_async_copy(conc.at[:, rows], field.at[:, rows], sems.at[k])
        for k, rows in enumerate((inner, left, right))
    ]
    for copy in small + copies:
        copy.start()
    for copy in small:
        copy.wait()
    tile = coef.shape[1:]
    for s in range(3):
        courant, angular = cour_v[...], ang_v[s : s + 1, :]
        axial = diff_s[s]
        total = jnp.float32(0.0)
        for k in range(map_s.shape[0]):
            total = total + jnp.where(map_s[k, 2] == s, rate_s[k], 0.0)
        coef[OWN + s] = jnp.broadcast_to((1.0 - 2.0 * axial) - courant - 2.0 * angular, tile)
        coef[BEFORE + s] = jnp.broadcast_to(courant + axial, tile)
        coef[ANGULAR + s] = jnp.broadcast_to(angular, tile)
        coef[AXIAL + s] = jnp.full(tile, axial, F32)
        coef[RATE + s] = jnp.full(tile, total, F32)
    lane = lax.broadcasted_iota(jnp.int32, (1, LANES), 1)
    for t in range(na):
        row = jnp.zeros((1, LANES), jnp.int32)
        for s in range(3):
            row = jnp.where(lane == s, flags_s[s, t], row)
        flag_v[t : t + 1, :] = row.astype(F32)
    rows = (hi - lo) * half
    span = pl.ds(3 * rows, na)
    mid[span, :] = jnp.zeros((na, mid.shape[1]), BF16)
    mid[span, :LANES] = flag_v[...].astype(BF16)
    copies[0].wait()
    mid_run(field, lambda s: mid.at[pl.ds(s * rows, rows)], lo, hi - lo, 0, coef, nz)
    copies[1].wait()
    copies[2].wait()
    for s in range(3):
        if planes == 2:
            row = jnp.where(lax.axis_index("ax") == 0, nz - 1, 0)
            for t in range(na):
                edges[0][s, t : t + 1, :] = field[s, pl.ds(t * nz + row, 1), :]
        else:
            for t in range(na):
                edges[0][s, t : t + 1, :] = field[s, t * nz : t * nz + 1, :]
                edges[1][s, t : t + 1, :] = field[s, (t + 1) * nz - 1 : (t + 1) * nz, :]


def inner_kernel(sizes, runs, conc, coef, *rest):
    na, nz = sizes
    outs, field, sem = rest[:-2], rest[-2], rest[-1]
    copy = pltpu.make_async_copy(conc, field, sem)
    copy.start()
    copy.wait()
    for out, parts in runs:
        at = 0
        for begin, count in parts:
            mid_run(field, outs[out].at.__getitem__, begin, count, at, coef, nz)
            at += count


def edge_weights(planes):
    if planes != 2:
        return 1.0, 1.0
    place = lax.axis_index("ax")
    return jnp.where(place == 1, 1.0, 0.0), jnp.where(place == 0, 1.0, 0.0)


def frame_kernel(
    sizes, conc, before, after, low, high, coef_in, out1, out2, field, coef, sems
):
    na, nz, ends, planes = sizes
    half = nz // 2
    copies = [
        pltpu.make_async_copy(conc, field.at[:, pl.ds(nz, na * nz)], sems.at[0]),
        pltpu.make_async_copy(before, field.at[:, pl.ds(0, nz)], sems.at[1]),
        pltpu.make_async_copy(after, field.at[:, pl.ds((na + 1) * nz, nz)], sems.at[2]),
        pltpu.make_async_copy(coef_in, coef, sems.at[3]),
    ]
    for copy in copies:
        copy.start()
    low_weight, high_weight = edge_weights(planes)
    for copy in copies:
        copy.wait()

    def angle(t):
        return first_step(
            field_reader(field, t + 1, nz),
            lambda s: low[s, pl.ds(t, 1), :] * low_weight,
            lambda s: high[s, pl.ds(t, 1), :] * high_weight,
            coef,
            half,
        )

    def pair(t, out, row, ends_row):
        tiles = [angle(t), angle(t + 1)]
        for s in range(3):
            out[s, pl.ds(row, nz), :] = pack([tiles[0][1][s], tiles[1][1][s]])
            if ends_row is not None:
                out2[s, pl.ds(ends_row, nz), :] = pack([tiles[0][0][s], tiles[1][0][s]])

    quarter = na // 4
    tail = na // 2 * half
    pair(0, out1, 0, tail)
    pair(na - 2, out2, (na // 2 - 2) * half, tail + nz)

    def first_part(step, carry):
        pair(step * 2, out1, pl.multiple_of(step * nz, nz), None)
        return carry

    def second_part(step, carry):
        pair(na // 2 + step * 2, out2, pl.multiple_of(step * nz, nz), None)
        return carry

    lax.fori_loop(1, quarter, first_part, 0)
    lax.fori_loop(0, quarter - 1, second_part, 0)


def weights_kernel(matrix, mine, theirs, out, keep, left, lower, sems):
    half = out.shape[1]
    copies = []
    for s in range(out.shape[0]):
        for k, ref in enumerate((left, lower)):
            src = matrix.at[s, pl.ds(k * half, half), pl.ds(0, half)]
            copies.append(pltpu.make_async_copy(src, ref.at[s], sems.at[k, s]))
    for copy in copies:
        copy.start()
    na = keep.shape[2]
    lane = lax.broadcasted_iota(jnp.int32, (na, LANES), 1)
    for ab, ref in enumerate((mine, theirs)):
        flags = ref[pl.ds(ref.shape[0] - na, na), :LANES].astype(F32)
        for s in range(out.shape[0]):
            moved = pltpu.roll(flags, LANES - s, 1) if s else flags
            keep[ab, s] = jnp.where(lane == 0, 1.0 - moved, 1.0)
    row = lax.broadcasted_iota(jnp.int32, (half, half), 0)
    col = lax.broadcasted_iota(jnp.int32, (half, half), 1)
    row = jnp.maximum(row, 1)
    pick = jnp.where(col == row, 1.0, 0.0).astype(BF16)
    flip = jnp.where(col == half - 1 - row, 1.0, 0.0).astype(BF16)
    for copy in copies:
        copy.wait()
    for s in range(out.shape[0]):
        out[s, :, :half] = jnp.dot(pick, left[s], preferred_element_type=F32).astype(BF16)
        out[s, :, half:] = jnp.dot(flip, lower[s], preferred_element_type=F32).astype(BF16)


def rows_product(rows, weights):
    return lax.dot_general(rows, weights, (((1,), (1,)), ((), ())), preferred_element_type=F32)


def both_sides(mine, theirs, weights):
    rows = jnp.concatenate(
        [jnp.concatenate([mine, theirs], 1), jnp.concatenate([theirs, mine], 1)], 0
    )
    return rows_product(rows, weights)


def store_run(state, s, begin, place, count, at, value, keep, half):
    total = value.shape[0] // 2
    for ab in range(2):
        part = value[ab * total + at * half : ab * total + (at + count) * half]
        state[ab, s, pl.ds(place * half, count * half), LANES:] = part[:, LANES:]
        for k in range(count):
            state[ab, s, pl.ds((place + k) * half, half), :LANES] = (
                part[k * half : (k + 1) * half, :LANES] * keep[ab, s, begin + k : begin + k + 1, :]
            )


def species_rows(ref, s, runs, half):
    if len(ref.shape) == 3:
        return ref[s]
    rows = sum(run[3] for run in runs) * half
    return ref[pl.ds(s * rows, rows), :]


def radial_kernel(plan, copies, half, weights, keep, *refs):
    n = len(plan)
    mines, theirs, refs = refs[:n], refs[n : 2 * n], refs[2 * n :]
    n_in = 1 + max((part for part, *_ in copies), default=-1)
    parts, states = refs[:n_in], refs[n_in:]
    for s in range(3):
        for k, runs in enumerate(plan):
            value = both_sides(
                species_rows(mines[k], s, runs, half),
                species_rows(theirs[k], s, runs, half),
                weights[s],
            )
            at = 0
            for which, begin, place, count in runs:
                store_run(states[which], s, begin, place, count, at, value, keep, half)
                at += count
    for part, source, which, place, count in copies:
        to, rows = pl.ds(place * half, count * half), pl.ds(source * half, count * half)
        for ab in range(2):
            for s in range(3):
                states[which][ab, s, to, :] = parts[part][ab, s, rows, :]


def edges_of_state(na, nz, planes, mid, mid_end, outer, edges, first, last, stage):
    half = nz // 2
    if planes == 2:
        row = jnp.where(lax.axis_index("ax") == 0, half // 2 - 1, half // 2)
    end = pl.ds((na - 1) * half, half)
    ends_end = pl.ds(mid_end.shape[2] - half, half)
    for ab in range(2):
        for s in range(3):
            for t in range(na):
                to = pl.ds(t, 1)
                at = t * half + half // 2
                if planes == 2:
                    stage[0, to, :] = outer[ab, s, pl.ds(t * half + row, 1), :]
                else:
                    stage[0, to, :] = outer[ab, s, at : at + 1, :]
                    stage[1, to, :] = outer[ab, s, at - 1 : at, :]
            for k, edge in enumerate(edges):
                edge[ab, s] = stage[k].astype(BF16)
            begin = pl.ds(0, half)
            first[ab, s] = pack([mid[ab, s, begin, :], outer[ab, s, begin, :]])
            last[ab, s] = pack([mid_end[ab, s, ends_end, :], outer[ab, s, end, :]])


def radial_edges_kernel(sizes, plan, copies, half, weights, keep, *refs):
    na, nz, planes = sizes
    n_edges = 1 if planes == 2 else 2
    *edges, first, last, stage = refs[-3 - n_edges :]
    refs = refs[: -3 - n_edges]
    radial_kernel(plan, copies, half, weights, keep, *refs)
    edges_of_state(na, nz, planes, refs[-2], refs[-2], refs[-1], edges, first, last, stage)


def explicit_angle(t, reader, low, high, edge_factors, coef, rows, nz):
    half = nz // 2
    for ab in range(2):
        out = second_step(
            functools.partial(reader, ab),
            lambda s: low[ab, s, pl.ds(t, 1), :] * edge_factors[0],
            lambda s: high[ab, s, pl.ds(t, 1), :] * edge_factors[1],
            coef,
            half,
        )
        width = out[0][0].shape[1]
        for s in range(3):
            rows[s, at_rows(t * nz, nz, nz), ab * width : (ab + 1) * width] = pack(
                [out[0][s], out[1][s]]
            )


def explicit_run(begin, count, states, low, high, edge_factors, coef, rows, nz):
    half = nz // 2

    def one(step, carry):
        t = begin + step

        def reader(ab, k, s, shift):
            state, base = states[k]
            return state[ab, s, at_rows((t - base + shift) * half, half, half), :]

        explicit_angle(t, reader, low, high, edge_factors, coef, rows, nz)
        return carry

    lax.fori_loop(0, count, one, 0)


def finish_run(begin, count, s, rows, weights, keep, result, nz):
    half = nz // 2
    value = rows_product(rows[s, pl.ds(begin * nz, count * nz), :], weights[s])
    for k in range(count):
        t = begin + k
        parts = turned(value[k * nz + half : (k + 1) * nz], value[k * nz : k * nz + half], half)
        for p in range(2):
            span = pl.ds(p * half, half)
            result[s, t, span, LANES:] = parts[p][:, LANES:]
            result[s, t, span, :LANES] = parts[p][:, :LANES] * keep[0, s, t : t + 1, :]


def widen(pairs):
    for source, target in pairs:
        target[...] = source[...].astype(F32)


def early_kernel(sizes, *refs):
    na, nz, runs, half_ring, planes = sizes
    (weights, keep, mid, outer, before_low, after_low, low_low, high_low, coef, out,
     before, after, low, high, rows, result, out_sems) = refs
    half = nz // 2
    place = lax.rem(lax.axis_index("ang"), half_ring)
    wrap_before = jnp.where(place == 0, 1, 0)
    wrap_after = jnp.where(place == half_ring - 1, 1, 0)
    factors = edge_weights(planes)
    widen(((low_low, low), (high_low, high)))
    for begin, count, base in runs:
        end = begin + count
        states = ((mid, base), (outer, 0))
        if begin == 0:
            widen(((before_low, before),))

            def reader(ab, k, s, shift):
                if shift == -1:
                    source = jnp.where(wrap_before == 1, 1 - ab, ab)
                    return before[source, s, pl.ds(k * half, half), :]
                return states[k][0][ab, s, pl.ds((shift - states[k][1]) * half, half), :]

            explicit_angle(0, reader, low, high, factors, coef, rows, nz)
        if end == na:
            widen(((after_low, after),))

            def reader(ab, k, s, shift):
                if shift == 1:
                    source = jnp.where(wrap_after == 1, 1 - ab, ab)
                    return after[source, s, pl.ds(k * half, half), :]
                return states[k][0][ab, s, pl.ds((na - 1 + shift - states[k][1]) * half, half), :]

            explicit_angle(na - 1, reader, low, high, factors, coef, rows, nz)
        start, stop = max(begin, 1), min(end, na - 1)
        if stop > start:
            explicit_run(start, stop - start, states, low, high, factors, coef, rows, nz)
    leaves = []
    for s in range(3):
        for k, (begin, count, _) in enumerate(runs):
            finish_run(begin, count, s, rows, weights, keep, result, nz)
            span = pl.ds(begin, count)
            leave = pltpu.make_async_copy(result.at[s, span], out.at[s, span], out_sems.at[k, s])
            leave.start()
            leaves.append(leave)
    for leave in leaves:
        leave.wait()


def late_kernel(
    sizes, given, state, weights, keep, mine, theirs, outer, low_low, high_low, coef,
    out, mid, low, high, rows, result, out_sems,
):
    na, nz, lo, hi, planes = sizes
    half = nz // 2
    factors = edge_weights(planes)
    count = hi - lo
    widen(((low_low, low), (high_low, high)))
    for s in range(3):
        value = both_sides(mine[s], theirs[s], weights[s])
        store_run(mid, s, lo, 2, count, 0, value, keep, half)
        for ab in range(2):
            for k in range(2):
                to = pl.ds((2 + count) * k * half, 2 * half)
                mid[ab, s, to, :] = state[ab, s, pl.ds((lo - 2 + 2 * k) * half, 2 * half), :]
    explicit_run(lo - 1, count + 2, ((mid, lo - 2), (outer, 0)), low, high, factors, coef, rows, nz)
    leaves = []
    for s in range(3):
        finish_run(lo - 1, count + 2, s, rows, weights, keep, result, nz)
        span = pl.ds(lo - 1, count + 2)
        leave = pltpu.make_async_copy(result.at[s, span], out.at[s, span], out_sems.at[s])
        leave.start()
        leaves.append(leave)
    for leave in leaves:
        leave.wait()


def ring(count, step):
    half = count // 2
    return [(i, i // half * half + (i % half + step) % half) for i in range(count)]


def plane_halos(edges, planes):
    if planes == 2:
        got = lax.ppermute(edges[0], "ax", [(0, 1), (1, 0)])
        return got, got
    up = [(i, i + 1) for i in range(planes - 1)]
    down = [(i + 1, i) for i in range(planes - 1)]
    return lax.ppermute(edges[1], "ax", up), lax.ppermute(edges[0], "ax", down)


def after(value, done):
    return lax.optimization_barrier((value, done))


def per_device(
    concentration, courant, axial_diffusion, angular_rate, rate_constants, species_map,
    wall_flags, radial_inverse,
):
    ns, na, nz, nr = concentration.shape
    half = nz // 2
    count = lax.axis_size("ang")
    planes = lax.axis_size("ax")
    n_edges = 1 if planes == 2 else 2
    quarter = na // 4
    ends = 2
    side = na // 2
    a_lo, a_cut, a_hi, x_hi = ends, na // 4, 7 * na // 16, na - ends
    opposite = [(i, (i + count // 2) % count) for i in range(count)]

    def dma(*dims):
        return pltpu.SemaphoreType.DMA(dims)

    def message(angles):
        return shape(ns, angles * half, nr, dtype=BF16)

    angle_before = lax.ppermute(
        concentration[:, na - 1], "ang", [(i, (i + 1) % count) for i in range(count)]
    )
    angle_after = lax.ppermute(
        concentration[:, 0], "ang", [(i, (i - 1) % count) for i in range(count)]
    )
    conc = concentration.reshape(ns, na * nz, nr)
    field = pltpu.VMEM((ns, na * nz, nr), F32)
    *edges, mid_a, coef = call(
        functools.partial(head_kernel, (na, nz, a_lo, a_cut, planes)),
        [shape(ns, na, nr)] * n_edges
        + [
            shape(ns * (a_cut - a_lo) * half + na, nr, dtype=BF16),
            shape(RATE + 3, half, nr),
        ],
        [HBM] * 7,
        [VM] * (n_edges + 2),
        [
            field, pltpu.VMEM((na, LANES), F32), pltpu.VMEM((1, nr), F32),
            pltpu.VMEM(angular_rate.shape, F32), pltpu.SMEM(axial_diffusion.shape, F32),
            pltpu.SMEM(rate_constants.shape, F32), pltpu.SMEM(species_map.shape, jnp.int32),
            pltpu.SMEM(wall_flags.shape, jnp.int32), dma(9),
        ],
        (conc, courant[None], axial_diffusion, angular_rate, rate_constants, species_map, wall_flags),
        58,
    )
    mid_a, (angle_before, angle_after) = after(mid_a, (angle_before, angle_after))
    opp_a = lax.ppermute(mid_a, "ang", opposite)
    low, high = plane_halos(edges, planes)
    bounds = (a_cut, a_hi, x_hi)
    mid_b, mid_x = call(
        functools.partial(
            inner_kernel,
            (na, nz),
            tuple((k, ((bounds[k], bounds[k + 1] - bounds[k]),)) for k in range(2)),
        ),
        [message(bounds[k + 1] - bounds[k]) for k in range(2)],
        [ANY, VM],
        [VM] * 2,
        [field, pltpu.SemaphoreType.DMA],
        (conc, coef),
        8,
    )
    opp_b = lax.ppermute(mid_b, "ang", opposite)
    out1, out2 = call(
        functools.partial(frame_kernel, (na, nz, ends, planes)),
        [message(na // 2), message(na // 2 + 2 * ends)],
        [ANY] * 3 + [VM] * 2 + [ANY],
        [VM] * 2,
        [pltpu.VMEM((ns, (na + 2) * nz, nr), F32), pltpu.VMEM((RATE + 3, half, nr), F32), dma(4)],
        (conc, angle_before, angle_after, low, high, coef),
        8,
    )
    out2, opp_a = after(out2, opp_a)
    opp_2 = lax.ppermute(out2, "ang", opposite)
    out1, opp_b = after(out1, opp_b)
    opp_1 = lax.ppermute(out1, "ang", opposite)

    weights, keep = call(
        weights_kernel,
        [shape(ns, nr, 2 * nr, dtype=BF16), shape(2, ns, na, LANES)],
        [ANY, VM, VM],
        [VM] * 2,
        [pltpu.VMEM((ns, nr, nr), BF16), pltpu.VMEM((ns, nr, nr), BF16), dma(2, ns)],
        (radial_inverse, mid_a, opp_a),
        12,
    )

    def state(angles):
        return shape(2, ns, angles * half, nr)

    count_a, count_b = a_cut - a_lo, a_hi - a_cut
    (mid_first,) = call(
        functools.partial(
            radial_kernel,
            (((0, a_lo, 0, count_a),), ((0, a_cut, count_a, count_b),)),
            (),
            half,
        ),
        [state(count_a + count_b)],
        [VM] * 6,
        [VM],
        [],
        (weights, keep, mid_a, mid_b, opp_a, opp_b),
        8,
    )
    opp_1, mid_first = after(opp_1, mid_first)
    mid_x, (opp_1, opp_2) = after(mid_x, (opp_1, opp_2))
    opp_x = lax.ppermute(mid_x, "ang", opposite)
    (outer_first,) = call(
        functools.partial(radial_kernel, (((0, 0, 0, side),),), (), half),
        [state(side)],
        [VM] * 4,
        [VM],
        [],
        (weights, keep, out1, opp_1),
        8,
    )
    plan = (((1, side, side, side), (0, 0, 0, ends), (0, na - ends, a_hi, ends)),)
    mid_left, outer_state, *rest = call(
        functools.partial(
            radial_edges_kernel,
            (na, nz, planes),
            plan,
            ((0, 0, 0, ends, count_a + count_b), (1, 0, 1, 0, side)),
            half,
        ),
        [state(a_hi + ends), state(na)]
        + [shape(2, ns, na, nr, dtype=BF16)] * n_edges
        + [shape(2, ns, nz, nr, dtype=BF16)] * 2,
        [VM] * 6,
        [VM] * (4 + n_edges),
        [pltpu.VMEM((n_edges, na, nr), F32)],
        (weights, keep, out2, opp_2, mid_first, outer_first),
        8,
    )
    *edges, first, last = rest
    low, high = plane_halos(edges, planes)
    angle_before = lax.ppermute(last, "ang", ring(count, 1))
    angle_after = lax.ppermute(first, "ang", ring(count, -1))
    stage = [pltpu.VMEM((ns, na * nz, 2 * nr), BF16), pltpu.VMEM((ns, na, nz, nr), F32)]
    edge_scratch = [pltpu.VMEM((2, ns, na, nr), F32)] * 2
    runs = ((0, a_hi - 1, 0), (na - 1, 1, na - ends - a_hi))
    partial = call(
        functools.partial(early_kernel, (na, nz, runs, count // 2, planes)),
        shape(ns, na, nz, nr),
        [VM] * 9,
        ANY,
        [pltpu.VMEM((2, ns, nz, nr), F32)] * 2 + edge_scratch + stage + [dma(len(runs), ns)],
        (weights, keep, mid_left, outer_state, angle_before, angle_after, low, high, coef),
        12,
    )
    wide = x_hi - a_hi + 4
    return call(
        functools.partial(late_kernel, (na, nz, a_hi, x_hi, planes)),
        shape(ns, na, nz, nr),
        [ANY] + [VM] * 9,
        ANY,
        [pltpu.VMEM((2, ns, wide * half, nr), F32)] + edge_scratch + stage + [dma(ns)],
        (partial, mid_left, weights, keep, mid_x, opp_x, outer_state, low, high, coef),
        12,
        {0: 0},
    )


def solution(mesh):
    in_specs = (P(None, "ang", "ax", None), P(), P(), P(), P(), P(), P(None, "ang"), P())
    out_specs = P(None, "ang", "ax", None)
    return jax.shard_map(
        per_device, mesh=mesh, in_specs=in_specs, out_specs=out_specs, check_vma=False
    )
```

```python
import functools

import jax
import jax.numpy as jnp
from jax import lax
from jax.experimental import pallas as pl
from jax.experimental.pallas import tpu as pltpu
from jax.sharding import PartitionSpec as P

F32 = jnp.float32
BF16 = jnp.bfloat16
MIB = 1024 * 1024
LANES = 128

ANY = pl.BlockSpec(memory_space=pl.ANY)
HBM = pl.BlockSpec(memory_space=pltpu.HBM)
VM = pl.BlockSpec(memory_space=pltpu.VMEM)
SM = pl.BlockSpec(memory_space=pltpu.SMEM)

OWN, BEFORE, ANGULAR, AXIAL, RATE = 0, 3, 6, 9, 12


def call(body, out_shape, in_specs, out_specs, scratch, args, mib, aliases=None):
    return pl.pallas_call(
        body,
        out_shape=out_shape,
        in_specs=in_specs,
        out_specs=out_specs,
        scratch_shapes=scratch,
        input_output_aliases=aliases or {},
        cost_estimate=pl.CostEstimate(flops=1, bytes_accessed=1, transcendentals=0),
        compiler_params=pltpu.CompilerParams(vmem_limit_bytes=mib * MIB),
    )(*args)


def shape(*dims, dtype=F32):
    return jax.ShapeDtypeStruct(dims, dtype)


def transport(now, before, after, around, coef):
    made = (
        coef[RATE] * (now[1] * now[2]),
        coef[RATE + 1] * (now[0] * now[2]),
        coef[RATE + 2] * (now[0] * now[1]),
    )
    spent = made[0] + made[1] + made[2]
    out = []
    for s in range(3):
        value = now[s] * coef[OWN + s] + before[s] * coef[BEFORE + s]
        value = value + after[s] * coef[AXIAL + s] + around[s] * coef[ANGULAR + s]
        out.append(value + ((made[s] + made[s]) - spent))
    return out


def turned(first, second, rows):
    first, second = pltpu.roll(first, rows // 2, 0), pltpu.roll(second, rows // 2, 0)
    upper = lax.broadcasted_iota(jnp.int32, first.shape, 0) < rows // 2
    return jnp.where(upper, first, second), jnp.where(upper, second, first)


def first_step(read, low, high, coef, half):
    tiles = [[read(s, 0, k) for s in range(3)] for k in range(2)]
    around = [[read(s, -1, k) + read(s, 1, k) for s in range(3)] for k in range(2)]
    row = lax.broadcasted_iota(jnp.int32, tiles[0][0].shape, 0)
    top, bottom = row == 0, row == half - 1
    fall = [[pltpu.roll(v, 1, 0) for v in tile] for tile in tiles]
    rise = [[pltpu.roll(v, half - 1, 0) for v in tile] for tile in tiles]
    out = []
    for k in range(2):
        other = 1 - k
        before = [
            jnp.where(top, low(s) if low is not None and k == 0 else fall[other][s], fall[k][s])
            for s in range(3)
        ]
        after = [
            jnp.where(bottom, high(s) if high is not None and k == 1 else rise[other][s], rise[k][s])
            for s in range(3)
        ]
        out.append(transport(tiles[k], before, after, around[k], coef))
    pairs = [turned(out[0][s], out[1][s], half) for s in range(3)]
    return [p[0] for p in pairs], [p[1] for p in pairs]


def second_step(read, low, high, coef, half):
    tiles = [[read(k, s, 0) for s in range(3)] for k in range(2)]
    around = [[read(k, s, -1) + read(k, s, 1) for s in range(3)] for k in range(2)]
    row = lax.broadcasted_iota(jnp.int32, tiles[0][0].shape, 0)
    top, bottom = row == 0, row == half - 1
    first, last = row == half // 2, row == half // 2 - 1
    fall = [[pltpu.roll(v, 1, 0) for v in tile] for tile in tiles]
    rise = [[pltpu.roll(v, half - 1, 0) for v in tile] for tile in tiles]
    out = []
    for k in range(2):
        before = [jnp.where(top, fall[1 - k][s], fall[k][s]) for s in range(3)]
        after = [jnp.where(bottom, rise[1 - k][s], rise[k][s]) for s in range(3)]
        if k == 1:
            before = [jnp.where(first, low(s), before[s]) for s in range(3)]
            after = [jnp.where(last, high(s), after[s]) for s in range(3)]
        out.append(transport(tiles[k], before, after, around[k], coef))
    return out


def pack(tiles):
    return jnp.concatenate(tiles, 0).astype(BF16)


def at_rows(start, count, step):
    return pl.ds(pl.multiple_of(start, step), count)


def field_reader(field, t, nz):
    half = nz // 2
    return lambda s, shift, k: field[s, at_rows((t + shift) * nz + k * half, half, half), :]


def mid_run(field, out_of, begin, count, at, coef, nz):
    half = nz // 2

    def pair(step, carry):
        t = begin + step * 2
        tiles = [first_step(field_reader(field, t + k, nz), None, None, coef, half)[0] for k in range(2)]
        for s in range(3):
            out_of(s)[at_rows(at * half + step * nz, nz, nz), :] = pack([tiles[0][s], tiles[1][s]])
        return carry

    lax.fori_loop(0, count // 2, pair, 0)


def head_kernel(sizes, conc, cour, diff, ang, rate, smap, flags, *rest):
    na, nz, lo, hi, planes = sizes
    edges = rest[: 1 if planes == 2 else 2]
    mid, coef, field, flag_v, cour_v, ang_v, diff_s, rate_s, map_s, flags_s, sems = rest[
        len(edges) :
    ]
    half = nz // 2
    inner = pl.ds((lo - 1) * nz, (hi - lo + 2) * nz)
    left = pl.ds(0, (lo - 1) * nz)
    right = pl.ds((hi + 1) * nz, (na - hi - 1) * nz)
    small = [
        pltpu.make_async_copy(src, dst, sems.at[k + 3])
        for k, (src, dst) in enumerate(
            ((cour, cour_v), (ang, ang_v), (diff, diff_s), (rate, rate_s), (smap, map_s), (flags, flags_s))
        )
    ]
    copies = [
        pltpu.make_async_copy(conc.at[:, rows], field.at[:, rows], sems.at[k])
        for k, rows in enumerate((inner, left, right))
    ]
    for copy in small + copies:
        copy.start()
    for copy in small:
        copy.wait()
    tile = coef.shape[1:]
    for s in range(3):
        courant, angular = cour_v[...], ang_v[s : s + 1, :]
        axial = diff_s[s]
        total = jnp.float32(0.0)
        for k in range(map_s.shape[0]):
            total = total + jnp.where(map_s[k, 2] == s, rate_s[k], 0.0)
        coef[OWN + s] = jnp.broadcast_to((1.0 - 2.0 * axial) - courant - 2.0 * angular, tile)
        coef[BEFORE + s] = jnp.broadcast_to(courant + axial, tile)
        coef[ANGULAR + s] = jnp.broadcast_to(angular, tile)
        coef[AXIAL + s] = jnp.full(tile, axial, F32)
        coef[RATE + s] = jnp.full(tile, total, F32)
    lane = lax.broadcasted_iota(jnp.int32, (1, LANES), 1)
    for t in range(na):
        row = jnp.zeros((1, LANES), jnp.int32)
        for s in range(3):
            row = jnp.where(lane == s, flags_s[s, t], row)
        flag_v[t : t + 1, :] = row.astype(F32)
    rows = (hi - lo) * half
    span = pl.ds(3 * rows, na)
    mid[span, :] = jnp.zeros((na, mid.shape[1]), BF16)
    mid[span, :LANES] = flag_v[...].astype(BF16)
    copies[0].wait()
    mid_run(field, lambda s: mid.at[pl.ds(s * rows, rows)], lo, hi - lo, 0, coef, nz)
    copies[1].wait()
    copies[2].wait()
    for s in range(3):
        if planes == 2:
            row = jnp.where(lax.axis_index("ax") == 0, nz - 1, 0)
            for t in range(na):
                edges[0][s, t : t + 1, :] = field[s, pl.ds(t * nz + row, 1), :]
        else:
            for t in range(na):
                edges[0][s, t : t + 1, :] = field[s, t * nz : t * nz + 1, :]
                edges[1][s, t : t + 1, :] = field[s, (t + 1) * nz - 1 : (t + 1) * nz, :]


def inner_kernel(sizes, runs, conc, coef, *rest):
    na, nz = sizes
    outs, field, sem = rest[:-2], rest[-2], rest[-1]
    copy = pltpu.make_async_copy(conc, field, sem)
    copy.start()
    copy.wait()
    for out, parts in runs:
        at = 0
        for begin, count in parts:
            mid_run(field, outs[out].at.__getitem__, begin, count, at, coef, nz)
            at += count


def edge_weights(planes):
    if planes != 2:
        return 1.0, 1.0
    place = lax.axis_index("ax")
    return jnp.where(place == 1, 1.0, 0.0), jnp.where(place == 0, 1.0, 0.0)


def frame_kernel(
    sizes, conc, before, after, low, high, coef_in, out1, out2, field, coef, sems
):
    na, nz, ends, planes = sizes
    half = nz // 2
    copies = [
        pltpu.make_async_copy(conc, field.at[:, pl.ds(nz, na * nz)], sems.at[0]),
        pltpu.make_async_copy(before, field.at[:, pl.ds(0, nz)], sems.at[1]),
        pltpu.make_async_copy(after, field.at[:, pl.ds((na + 1) * nz, nz)], sems.at[2]),
        pltpu.make_async_copy(coef_in, coef, sems.at[3]),
    ]
    for copy in copies:
        copy.start()
    low_weight, high_weight = edge_weights(planes)
    for copy in copies:
        copy.wait()

    def angle(t):
        return first_step(
            field_reader(field, t + 1, nz),
            lambda s: low[s, pl.ds(t, 1), :] * low_weight,
            lambda s: high[s, pl.ds(t, 1), :] * high_weight,
            coef,
            half,
        )

    def pair(t, out, row, ends_row):
        tiles = [angle(t), angle(t + 1)]
        for s in range(3):
            out[s, pl.ds(row, nz), :] = pack([tiles[0][1][s], tiles[1][1][s]])
            if ends_row is not None:
                out2[s, pl.ds(ends_row, nz), :] = pack([tiles[0][0][s], tiles[1][0][s]])

    quarter = na // 4
    tail = na // 2 * half
    pair(0, out1, 0, tail)
    pair(na - 2, out2, (na // 2 - 2) * half, tail + nz)

    def first_part(step, carry):
        pair(step * 2, out1, pl.multiple_of(step * nz, nz), None)
        return carry

    def second_part(step, carry):
        pair(na // 2 + step * 2, out2, pl.multiple_of(step * nz, nz), None)
        return carry

    lax.fori_loop(1, quarter, first_part, 0)
    lax.fori_loop(0, quarter - 1, second_part, 0)


def weights_kernel(matrix, mine, theirs, out, keep, left, lower, sems):
    half = out.shape[1]
    copies = []
    for s in range(out.shape[0]):
        for k, ref in enumerate((left, lower)):
            src = matrix.at[s, pl.ds(k * half, half), pl.ds(0, half)]
            copies.append(pltpu.make_async_copy(src, ref.at[s], sems.at[k, s]))
    for copy in copies:
        copy.start()
    na = keep.shape[2]
    lane = lax.broadcasted_iota(jnp.int32, (na, LANES), 1)
    for ab, ref in enumerate((mine, theirs)):
        flags = ref[pl.ds(ref.shape[0] - na, na), :LANES].astype(F32)
        for s in range(out.shape[0]):
            moved = pltpu.roll(flags, LANES - s, 1) if s else flags
            keep[ab, s] = jnp.where(lane == 0, 1.0 - moved, 1.0)
    row = lax.broadcasted_iota(jnp.int32, (half, half), 0)
    col = lax.broadcasted_iota(jnp.int32, (half, half), 1)
    row = jnp.maximum(row, 1)
    pick = jnp.where(col == row, 1.0, 0.0).astype(BF16)
    flip = jnp.where(col == half - 1 - row, 1.0, 0.0).astype(BF16)
    for copy in copies:
        copy.wait()
    for s in range(out.shape[0]):
        out[s, :, :half] = jnp.dot(pick, left[s], preferred_element_type=F32).astype(BF16)
        out[s, :, half:] = jnp.dot(flip, lower[s], preferred_element_type=F32).astype(BF16)


def rows_product(rows, weights):
    return lax.dot_general(rows, weights, (((1,), (1,)), ((), ())), preferred_element_type=F32)


def both_sides(mine, theirs, weights):
    rows = jnp.concatenate(
        [jnp.concatenate([mine, theirs], 1), jnp.concatenate([theirs, mine], 1)], 0
    )
    return rows_product(rows, weights)


def store_run(state, s, begin, place, count, at, value, keep, half):
    total = value.shape[0] // 2
    for ab in range(2):
        part = value[ab * total + at * half : ab * total + (at + count) * half]
        state[ab, s, pl.ds(place * half, count * half), LANES:] = part[:, LANES:]
        for k in range(count):
            state[ab, s, pl.ds((place + k) * half, half), :LANES] = (
                part[k * half : (k + 1) * half, :LANES] * keep[ab, s, begin + k : begin + k + 1, :]
            )


def species_rows(ref, s, runs, half):
    if len(ref.shape) == 3:
        return ref[s]
    rows = sum(run[3] for run in runs) * half
    return ref[pl.ds(s * rows, rows), :]


def radial_kernel(plan, copies, half, weights, keep, *refs):
    n = len(plan)
    mines, theirs, refs = refs[:n], refs[n : 2 * n], refs[2 * n :]
    n_in = 1 + max((part for part, *_ in copies), default=-1)
    parts, states = refs[:n_in], refs[n_in:]
    for s in range(3):
        for k, runs in enumerate(plan):
            value = both_sides(
                species_rows(mines[k], s, runs, half),
                species_rows(theirs[k], s, runs, half),
                weights[s],
            )
            at = 0
            for which, begin, place, count in runs:
                store_run(states[which], s, begin, place, count, at, value, keep, half)
                at += count
    for part, source, which, place, count in copies:
        to, rows = pl.ds(place * half, count * half), pl.ds(source * half, count * half)
        for ab in range(2):
            for s in range(3):
                states[which][ab, s, to, :] = parts[part][ab, s, rows, :]


def edges_of_state(na, nz, planes, mid, mid_end, outer, edges, first, last, stage):
    half = nz // 2
    if planes == 2:
        row = jnp.where(lax.axis_index("ax") == 0, half // 2 - 1, half // 2)
    end = pl.ds((na - 1) * half, half)
    ends_end = pl.ds(mid_end.shape[2] - half, half)
    for ab in range(2):
        for s in range(3):
            for t in range(na):
                to = pl.ds(t, 1)
                at = t * half + half // 2
                if planes == 2:
                    stage[0, to, :] = outer[ab, s, pl.ds(t * half + row, 1), :]
                else:
                    stage[0, to, :] = outer[ab, s, at : at + 1, :]
                    stage[1, to, :] = outer[ab, s, at - 1 : at, :]
            for k, edge in enumerate(edges):
                edge[ab, s] = stage[k].astype(BF16)
            begin = pl.ds(0, half)
            first[ab, s] = pack([mid[ab, s, begin, :], outer[ab, s, begin, :]])
            last[ab, s] = pack([mid_end[ab, s, ends_end, :], outer[ab, s, end, :]])


def radial_edges_kernel(sizes, plan, copies, half, weights, keep, *refs):
    na, nz, planes = sizes
    n_edges = 1 if planes == 2 else 2
    *edges, first, last, stage = refs[-3 - n_edges :]
    refs = refs[: -3 - n_edges]
    radial_kernel(plan, copies, half, weights, keep, *refs)
    edges_of_state(na, nz, planes, refs[-2], refs[-2], refs[-1], edges, first, last, stage)


def explicit_angle(t, reader, low, high, edge_factors, coef, rows, nz):
    half = nz // 2
    for ab in range(2):
        out = second_step(
            functools.partial(reader, ab),
            lambda s: low[ab, s, pl.ds(t, 1), :] * edge_factors[0],
            lambda s: high[ab, s, pl.ds(t, 1), :] * edge_factors[1],
            coef,
            half,
        )
        width = out[0][0].shape[1]
        for s in range(3):
            rows[s, at_rows(t * nz, nz, nz), ab * width : (ab + 1) * width] = pack(
                [out[0][s], out[1][s]]
            )


def explicit_run(begin, count, states, low, high, edge_factors, coef, rows, nz):
    half = nz // 2

    def one(step, carry):
        t = begin + step

        def reader(ab, k, s, shift):
            state, base = states[k]
            return state[ab, s, at_rows((t - base + shift) * half, half, half), :]

        explicit_angle(t, reader, low, high, edge_factors, coef, rows, nz)
        return carry

    lax.fori_loop(0, count, one, 0)


def finish_run(begin, count, s, rows, weights, keep, result, nz):
    half = nz // 2
    value = rows_product(rows[s, pl.ds(begin * nz, count * nz), :], weights[s])
    for k in range(count):
        t = begin + k
        parts = turned(value[k * nz + half : (k + 1) * nz], value[k * nz : k * nz + half], half)
        for p in range(2):
            span = pl.ds(p * half, half)
            result[s, t, span, LANES:] = parts[p][:, LANES:]
            result[s, t, span, :LANES] = parts[p][:, :LANES] * keep[0, s, t : t + 1, :]


def widen(pairs):
    for source, target in pairs:
        target[...] = source[...].astype(F32)


def early_kernel(sizes, *refs):
    na, nz, runs, half_ring, planes = sizes
    (weights, keep, mid, outer, before_low, after_low, low_low, high_low, coef, out,
     before, after, low, high, rows, result, out_sems) = refs
    half = nz // 2
    place = lax.rem(lax.axis_index("ang"), half_ring)
    wrap_before = jnp.where(place == 0, 1, 0)
    wrap_after = jnp.where(place == half_ring - 1, 1, 0)
    factors = edge_weights(planes)
    widen(((low_low, low), (high_low, high)))
    for begin, count, base in runs:
        end = begin + count
        states = ((mid, base), (outer, 0))
        if begin == 0:
            widen(((before_low, before),))

            def reader(ab, k, s, shift):
                if shift == -1:
                    source = jnp.where(wrap_before == 1, 1 - ab, ab)
                    return before[source, s, pl.ds(k * half, half), :]
                return states[k][0][ab, s, pl.ds((shift - states[k][1]) * half, half), :]

            explicit_angle(0, reader, low, high, factors, coef, rows, nz)
        if end == na:
            widen(((after_low, after),))

            def reader(ab, k, s, shift):
                if shift == 1:
                    source = jnp.where(wrap_after == 1, 1 - ab, ab)
                    return after[source, s, pl.ds(k * half, half), :]
                return states[k][0][ab, s, pl.ds((na - 1 + shift - states[k][1]) * half, half), :]

            explicit_angle(na - 1, reader, low, high, factors, coef, rows, nz)
        start, stop = max(begin, 1), min(end, na - 1)
        if stop > start:
            explicit_run(start, stop - start, states, low, high, factors, coef, rows, nz)
    leaves = []
    for s in range(3):
        for k, (begin, count, _) in enumerate(runs):
            finish_run(begin, count, s, rows, weights, keep, result, nz)
            span = pl.ds(begin, count)
            leave = pltpu.make_async_copy(result.at[s, span], out.at[s, span], out_sems.at[k, s])
            leave.start()
            leaves.append(leave)
    for leave in leaves:
        leave.wait()


def late_kernel(
    sizes, given, state, weights, keep, mine, theirs, outer, low_low, high_low, coef,
    out, mid, low, high, rows, result, out_sems,
):
    na, nz, lo, hi, planes = sizes
    half = nz // 2
    factors = edge_weights(planes)
    count = hi - lo
    widen(((low_low, low), (high_low, high)))
    for s in range(3):
        value = both_sides(mine[s], theirs[s], weights[s])
        store_run(mid, s, lo, 2, count, 0, value, keep, half)
        for ab in range(2):
            for k in range(2):
                to = pl.ds((2 + count) * k * half, 2 * half)
                mid[ab, s, to, :] = state[ab, s, pl.ds((lo - 2 + 2 * k) * half, 2 * half), :]
    explicit_run(lo - 1, count + 2, ((mid, lo - 2), (outer, 0)), low, high, factors, coef, rows, nz)
    leaves = []
    for s in range(3):
        finish_run(lo - 1, count + 2, s, rows, weights, keep, result, nz)
        span = pl.ds(lo - 1, count + 2)
        leave = pltpu.make_async_copy(result.at[s, span], out.at[s, span], out_sems.at[s])
        leave.start()
        leaves.append(leave)
    for leave in leaves:
        leave.wait()


def ring(count, step):
    half = count // 2
    return [(i, i // half * half + (i % half + step) % half) for i in range(count)]


def plane_halos(edges, planes):
    if planes == 2:
        got = lax.ppermute(edges[0], "ax", [(0, 1), (1, 0)])
        return got, got
    up = [(i, i + 1) for i in range(planes - 1)]
    down = [(i + 1, i) for i in range(planes - 1)]
    return lax.ppermute(edges[1], "ax", up), lax.ppermute(edges[0], "ax", down)


def after(value, done):
    return lax.optimization_barrier((value, done))


def per_device(
    concentration, courant, axial_diffusion, angular_rate, rate_constants, species_map,
    wall_flags, radial_inverse,
):
    ns, na, nz, nr = concentration.shape
    half = nz // 2
    count = lax.axis_size("ang")
    planes = lax.axis_size("ax")
    n_edges = 1 if planes == 2 else 2
    quarter = na // 4
    ends = 2
    side = na // 2
    a_lo, a_hi, x_hi = ends, side, na - ends
    opposite = [(i, (i + count // 2) % count) for i in range(count)]

    def dma(*dims):
        return pltpu.SemaphoreType.DMA(dims)

    def message(angles):
        return shape(ns, angles * half, nr, dtype=BF16)

    angle_before = lax.ppermute(
        concentration[:, na - 1], "ang", [(i, (i + 1) % count) for i in range(count)]
    )
    angle_after = lax.ppermute(
        concentration[:, 0], "ang", [(i, (i - 1) % count) for i in range(count)]
    )
    conc = concentration.reshape(ns, na * nz, nr)
    field = pltpu.VMEM((ns, na * nz, nr), F32)
    *edges, mid_a, coef = call(
        functools.partial(head_kernel, (na, nz, a_lo, a_hi, planes)),
        [shape(ns, na, nr)] * n_edges
        + [
            shape(ns * (a_hi - a_lo) * half + na, nr, dtype=BF16),
            shape(RATE + 3, half, nr),
        ],
        [HBM] * 7,
        [VM] * (n_edges + 2),
        [
            field, pltpu.VMEM((na, LANES), F32), pltpu.VMEM((1, nr), F32),
            pltpu.VMEM(angular_rate.shape, F32), pltpu.SMEM(axial_diffusion.shape, F32),
            pltpu.SMEM(rate_constants.shape, F32), pltpu.SMEM(species_map.shape, jnp.int32),
            pltpu.SMEM(wall_flags.shape, jnp.int32), dma(9),
        ],
        (conc, courant[None], axial_diffusion, angular_rate, rate_constants, species_map, wall_flags),
        58,
    )
    mid_a, (angle_before, angle_after) = after(mid_a, (angle_before, angle_after))
    opp_a = lax.ppermute(mid_a, "ang", opposite)
    low, high = plane_halos(edges, planes)
    (mid_x,) = call(
        functools.partial(
            inner_kernel,
            (na, nz),
            ((0, ((a_hi, x_hi - a_hi),)),),
        ),
        [message(x_hi - a_hi)],
        [ANY, VM],
        [VM],
        [field, pltpu.SemaphoreType.DMA],
        (conc, coef),
        8,
    )
    out1, out2 = call(
        functools.partial(frame_kernel, (na, nz, ends, planes)),
        [message(na // 2), message(na // 2 + 2 * ends)],
        [ANY] * 3 + [VM] * 2 + [ANY],
        [VM] * 2,
        [pltpu.VMEM((ns, (na + 2) * nz, nr), F32), pltpu.VMEM((RATE + 3, half, nr), F32), dma(4)],
        (conc, angle_before, angle_after, low, high, coef),
        8,
    )
    (out1, out2), opp_a = after((out1, out2), opp_a)
    opp_2 = lax.ppermute(out2, "ang", opposite)
    opp_1 = lax.ppermute(out1, "ang", opposite)

    weights, keep = call(
        weights_kernel,
        [shape(ns, nr, 2 * nr, dtype=BF16), shape(2, ns, na, LANES)],
        [ANY, VM, VM],
        [VM] * 2,
        [pltpu.VMEM((ns, nr, nr), BF16), pltpu.VMEM((ns, nr, nr), BF16), dma(2, ns)],
        (radial_inverse, mid_a, opp_a),
        12,
    )

    def state(angles):
        return shape(2, ns, angles * half, nr)

    count_a = a_hi - a_lo
    (mid_first,) = call(
        functools.partial(radial_kernel, (((0, a_lo, 0, count_a),),), (), half),
        [state(count_a)],
        [VM] * 4,
        [VM],
        [],
        (weights, keep, mid_a, opp_a),
        8,
    )
    opp_1, mid_first = after(opp_1, mid_first)
    mid_x, (opp_1, opp_2) = after(mid_x, (opp_1, opp_2))
    opp_x = lax.ppermute(mid_x, "ang", opposite)
    (outer_first,) = call(
        functools.partial(radial_kernel, (((0, 0, 0, side),),), (), half),
        [state(side)],
        [VM] * 4,
        [VM],
        [],
        (weights, keep, out1, opp_1),
        8,
    )
    plan = (((1, side, side, side), (0, 0, 0, ends), (0, na - ends, a_hi, ends)),)
    mid_left, outer_state, *rest = call(
        functools.partial(
            radial_edges_kernel,
            (na, nz, planes),
            plan,
            ((0, 0, 0, ends, count_a), (1, 0, 1, 0, side)),
            half,
        ),
        [state(a_hi + ends), state(na)]
        + [shape(2, ns, na, nr, dtype=BF16)] * n_edges
        + [shape(2, ns, nz, nr, dtype=BF16)] * 2,
        [VM] * 6,
        [VM] * (4 + n_edges),
        [pltpu.VMEM((n_edges, na, nr), F32)],
        (weights, keep, out2, opp_2, mid_first, outer_first),
        8,
    )
    *edges, first, last = rest
    low, high = plane_halos(edges, planes)
    angle_before = lax.ppermute(last, "ang", ring(count, 1))
    angle_after = lax.ppermute(first, "ang", ring(count, -1))
    stage = [pltpu.VMEM((ns, na * nz, 2 * nr), BF16), pltpu.VMEM((ns, na, nz, nr), F32)]
    edge_scratch = [pltpu.VMEM((2, ns, na, nr), F32)] * 2
    runs = ((0, a_hi - 1, 0), (na - 1, 1, na - ends - a_hi))
    partial = call(
        functools.partial(early_kernel, (na, nz, runs, count // 2, planes)),
        shape(ns, na, nz, nr),
        [VM] * 9,
        ANY,
        [pltpu.VMEM((2, ns, nz, nr), F32)] * 2 + edge_scratch + stage + [dma(len(runs), ns)],
        (weights, keep, mid_left, outer_state, angle_before, angle_after, low, high, coef),
        12,
    )
    wide = x_hi - a_hi + 4
    return call(
        functools.partial(late_kernel, (na, nz, a_hi, x_hi, planes)),
        shape(ns, na, nz, nr),
        [ANY] + [VM] * 9,
        ANY,
        [pltpu.VMEM((2, ns, wide * half, nr), F32)] + edge_scratch + stage + [dma(ns)],
        (partial, mid_left, weights, keep, mid_x, opp_x, outer_state, low, high, coef),
        12,
        {0: 0},
    )


def solution(mesh):
    in_specs = (P(None, "ang", "ax", None), P(), P(), P(), P(), P(), P(None, "ang"), P())
    out_specs = P(None, "ang", "ax", None)
    return jax.shard_map(
        per_device, mesh=mesh, in_specs=in_specs, out_specs=out_specs, check_vma=False
    )
```
